32 devices in a mesh: dp: 16 (over z, y, x), space: 2 (over core).
Axes of the slice: x: 2, y: 2, z: 4, core: 2. Of those that a mesh axis runs over, the one named last changes fastest.
Arguments:
- features: bfloat16 [16, 16, 96, 512], P('dp', 'space'), may hold values from -6 to 6
- top_down: bfloat16 [16, 8, 48, 256], P('dp', 'space'), may hold values from -6 to 6
- lateral_weight: bfloat16 [512, 256], replicated, may hold values from -0.25 to 0.25
- out_kernel: bfloat16 [3, 3, 256, 256], replicated, may hold values from -0.125 to 0.125
- cotangent: bfloat16 [16, 16, 96, 256], P('dp', 'space'), may hold values from -1.5 to 1.5
Outputs:
- p3_out: bfloat16 [16, 16, 96, 256], P('dp', 'space')
- grad_top: bfloat16 [16, 8, 48, 256], P('dp', 'space')
- grad_kernel: bfloat16 [3, 3, 256, 256], replicated
- grad_lateral: bfloat16 [512, 256], replicated
The draws below stay inside these ranges and needn't reach their ends.
All inputs are finite; a program needn't handle non-finite values.
Results may differ from the reference program's by a relative error of at most 0.0053.
Values may be sent and summed in bfloat16 or wider, within the bound.
No kernel may reach another device: no remote copies, remote signals or barrier semaphores. Data moves between devices by JAX's collectives and lax.ppermute only.
A program may use at most 64 MiB of HBM per device.

```python
import jax
import jax.numpy as jnp
from jax import lax

CH = 256
CIN = 512
COLS = 96
IMAGES = 16
ROWS = 16


def steps_of(key, extent, split, low, high):
    level, own = 1.0, jax.random.fold_in(key, 6)
    for dim, blocks in split:
        steps = jnp.exp(jax.random.uniform(jax.random.fold_in(own, dim), (blocks,), jnp.float32, low / len(split), high / len(split)))
        level = level * jnp.repeat(steps, extent[dim] // blocks).reshape([-1 if axis == dim else 1 for axis in range(len(extent))])
    return level


def bell_draw(rng, dims, spread, bound, split=(), kind=jnp.bfloat16):
    level = steps_of(rng, dims, split, -0.22, 0.18) if split else 1.0
    drawn = jax.random.normal(rng, dims, jnp.float32) * spread * level
    return jnp.minimum(jnp.maximum(drawn, -bound), bound).astype(kind)


def setup_inputs(seed: int = 0) -> dict:
    seeds = jax.random.split(jax.random.key(seed), 6)
    return {
        "features": bell_draw(seeds[0], (IMAGES, ROWS, COLS, CIN), 1.0, 6.0, ((0, 16), (1, 2))),
        "top_down": bell_draw(seeds[1], (IMAGES, ROWS // 2, COLS // 2, CH), 1.0, 6.0, ((0, 16), (1, 2))),
        "lateral_weight": bell_draw(seeds[2], (CIN, CH), CIN ** -0.5, 0.25),
        "out_kernel": bell_draw(seeds[3], (3, 3, CH, CH), (9 * CH) ** -0.5, 0.125),
        "cotangent": bell_draw(seeds[4], (IMAGES, ROWS, COLS, CH), 0.25, 1.5, ((0, 16), (1, 2))),
    }


def row_band(source, tap_row, row_count, col_count):
    pieces = [source[tap_row:tap_row + row_count, tap_col:tap_col + col_count, :] for tap_col in range(3)]
    joined = jnp.concatenate(pieces, axis=-1)
    return joined.reshape(row_count * col_count, joined.shape[-1])


def reference(features, top_down, lateral_weight, out_kernel, cotangent):
    channels = lateral_weight.shape[1]
    forward_stack = out_kernel.reshape(3, 3 * CH, CH)
    backward_stack = jnp.transpose(out_kernel[:, ::-1], (0, 1, 3, 2)).reshape(3, 3 * CH, CH)

    def per_image(carry, inputs):
        kernel_acc, lateral_acc = carry
        image_feat, image_top, image_cot = inputs
        flat_feat = image_feat.reshape(ROWS * COLS, CIN)
        lateral = jnp.dot(flat_feat, lateral_weight, preferred_element_type=jnp.float32).reshape(ROWS, COLS, channels)
        upsampled = jnp.repeat(jnp.repeat(image_top, 2, axis=0), 2, axis=1).astype(jnp.float32)
        merged = (lateral + upsampled).astype(jnp.bfloat16)
        padded = jnp.pad(merged, ((1, 1), (1, 1), (0, 0)))
        flat_cot = image_cot.reshape(ROWS * COLS, channels)
        output = jnp.zeros((ROWS * COLS, channels), jnp.float32)
        kernel_terms = []
        for tap_row in range(3):
            strip = row_band(padded, tap_row, ROWS, COLS)
            output = output + jnp.dot(strip, forward_stack[tap_row], preferred_element_type=jnp.float32)
            kernel_terms.append(lax.dot_general(strip, flat_cot, (((0,), (0,)), ((), ())), preferred_element_type=jnp.float32).reshape(3, channels, channels))
        kernel_acc = kernel_acc + jnp.stack(kernel_terms)
        cot_padded = jnp.pad(image_cot, ((1, 1), (1, 1), (0, 0)))
        grad_acc = jnp.zeros((ROWS * COLS, channels), jnp.float32)
        for tap_row in range(3):
            strip = row_band(cot_padded, 2 - tap_row, ROWS, COLS)
            grad_acc = grad_acc + jnp.dot(strip, backward_stack[tap_row], preferred_element_type=jnp.float32)
        grad_merged = grad_acc.astype(jnp.bfloat16)
        grad_top = grad_merged.astype(jnp.float32).reshape(ROWS // 2, 2, COLS // 2, 2, channels).sum(axis=(1, 3)).astype(jnp.bfloat16)
        lateral_acc = lateral_acc + lax.dot_general(flat_feat, grad_merged, (((0,), (0,)), ((), ())), preferred_element_type=jnp.float32)
        result = output.astype(jnp.bfloat16).reshape(ROWS, COLS, channels)
        return (kernel_acc, lateral_acc), (result, grad_top)

    start = (jnp.zeros((3, 3, CH, CH), jnp.float32), jnp.zeros((CIN, CH), jnp.float32))
    (kernel_acc, lateral_acc), (p3_out, grad_top) = lax.scan(per_image, start, (features, top_down, cotangent))
    grad_kernel = (kernel_acc / IMAGES).astype(jnp.bfloat16)
    grad_lateral = (lateral_acc / IMAGES).astype(jnp.bfloat16)
    return p3_out, grad_top, grad_kernel, grad_lateral
```

```python
import functools

import jax
import jax.numpy as jnp
from jax import lax
from jax.experimental import pallas as pl
from jax.experimental.pallas import tpu as pltpu
from jax.sharding import PartitionSpec as P

F32 = jnp.float32
BF16 = jnp.bfloat16


def neighbour_rows(array):
    peers = lax.axis_size("space")
    rows = array.shape[0]
    if peers == 1:
        return array[0], array[0]
    if peers == 2:
        here = lax.axis_index("space")
        edge = lax.dynamic_index_in_dim(array, (1 - here) * (rows - 1), 0, keepdims=False)
        got = lax.ppermute(edge, "space", [(0, 1), (1, 0)])
        return got, got
    up = [(i, i + 1) for i in range(peers - 1)]
    down = [(j, i) for i, j in up]
    return lax.ppermute(array[-1], "space", up), lax.ppermute(array[0], "space", down)


def put_shifted(stack, slot, row, sign):
    cols, channels = row.shape
    wide = row.astype(F32)
    place = lax.broadcasted_iota(jnp.int32, (cols, channels), 0)
    later = jnp.where(place == cols - 1, 0.0, pltpu.roll(wide, cols - 1, 0)).astype(BF16)
    earlier = jnp.where(place == 0, 0.0, pltpu.roll(wide, 1, 0)).astype(BF16)
    first, last = (earlier, later) if sign < 0 else (later, earlier)
    stack[slot, :, 0:channels] = first
    stack[slot, :, channels : 2 * channels] = row
    stack[slot, :, 2 * channels :] = last


def put_halo(stack, before, after, rows, peers, sign):
    here = lax.axis_index("space")
    zero = jnp.zeros(before.shape, BF16)
    put_shifted(stack, 0, jnp.where(here > 0, before[...], zero), sign)
    put_shifted(stack, rows + 1, jnp.where(here < peers - 1, after[...], zero), sign)


def grads_kernel(peers, feat, top, lat_w, out_w, cot, before, after, merged, grad_top, *rest):
    outs, stack = rest[:-1], rest[-1]
    rows, cols, channels = cot.shape
    cells = rows * cols
    half = cols // 2
    in_channels = lat_w.shape[0]
    upper = lax.broadcasted_iota(jnp.int32, (cols, half), 0)
    spread = jnp.where(upper // 2 == lax.broadcasted_iota(jnp.int32, (cols, half), 1), 1.0, 0.0).astype(BF16)
    lateral = jnp.dot(feat[...], lat_w[...], preferred_element_type=F32)
    for q in range(rows // 2):
        lifted = jnp.dot(spread, top[q], preferred_element_type=F32)
        for r in (2 * q, 2 * q + 1):
            merged[r * cols : (r + 1) * cols, :] = (lateral[r * cols : (r + 1) * cols] + lifted).astype(BF16)
    for r in range(rows):
        put_shifted(stack, r + 1, cot[r], 1)
    put_halo(stack, before, after, rows, peers, 1)

    def put(start, block):
        if len(outs) == 1:
            outs[0][start : start + block.shape[0], :] = block
            return
        here = lax.axis_index("space")
        left, right = block[:, : channels // 2], block[:, channels // 2 :]
        mine, theirs = outs
        mine[start : start + block.shape[0], :] = jnp.where(here == 0, left, right)
        theirs[start : start + block.shape[0], :] = jnp.where(here == 0, right, left).astype(BF16)

    merged_t = jnp.transpose(merged[...])
    for i in range(3):
        strip = stack[2 - i : 2 - i + rows].reshape(cells, 3 * channels)
        part = jnp.dot(merged_t, strip, preferred_element_type=F32)
        for j in range(3):
            put((3 * i + j) * channels, part[:, j * channels : (j + 1) * channels])
    total = jnp.zeros((cells, channels), F32)
    for i in range(3):
        strip = stack[2 - i : 2 - i + rows].reshape(cells, 3 * channels)
        taps = jnp.concatenate([out_w[3 * i + j] for j in range(3)], axis=1)
        total = total + lax.dot_general(strip, taps, (((1,), (1,)), ((), ())), preferred_element_type=F32)
    grad = total.astype(BF16)
    lower = lax.broadcasted_iota(jnp.int32, (half, 2 * cols), 1)
    lower = jnp.where(lower >= cols, lower - cols, lower)
    pool = jnp.where(lower // 2 == lax.broadcasted_iota(jnp.int32, (half, 2 * cols), 0), 1.0, 0.0).astype(BF16)
    for q in range(rows // 2):
        pair = grad[2 * q * cols : (2 * q + 2) * cols]
        grad_top[q] = jnp.dot(pool, pair, preferred_element_type=F32).astype(BF16)
    feat_t = jnp.transpose(feat[...])
    put(9 * channels, jnp.dot(feat_t, grad, preferred_element_type=F32))


def forward_kernel(peers, merged, out_w, before, after, out, stack):
    rows, cols, channels = merged.shape
    for r in range(rows):
        put_shifted(stack, r + 1, merged[r], -1)
    put_halo(stack, before, after, rows, peers, -1)
    total = jnp.zeros((rows * cols, channels), F32)
    for i in range(3):
        strip = stack[i : i + rows].reshape(rows * cols, 3 * channels)
        taps = out_w[3 * i : 3 * i + 3].reshape(3 * channels, channels)
        total = total + jnp.dot(strip, taps, preferred_element_type=F32)
    out[...] = total.astype(BF16).reshape(out.shape)


def sum_everywhere(mine, theirs, scale):
    length, width = mine.shape
    parts = lax.axis_size("dp")
    swap = [(0, 1), (1, 0)]
    got = lax.ppermute(theirs, "space", swap)
    pair = (mine + got.astype(F32)).astype(BF16)
    share = -(-length // (16 * parts)) * 16
    pair = jnp.pad(pair, ((0, share * parts - length), (0, 0))).reshape(parts, share, width)
    terms = lax.all_to_all(pair, "dp", 0, 0, tiled=True)
    total = (jnp.sum(terms.astype(F32), axis=0) * scale).astype(BF16)
    copies = jnp.broadcast_to(total[None], terms.shape)
    whole = lax.all_to_all(copies, "dp", 0, 0, tiled=True).reshape(parts * share, width)[:length]
    other = lax.ppermute(whole, "space", swap)
    first = lax.axis_index("space") == 0
    return jnp.concatenate([jnp.where(first, whole, other), jnp.where(first, other, whole)], axis=1)


def local(features, top_down, lateral_weight, out_kernel, cotangent):
    images, rows, cols, in_channels = features.shape
    channels = lateral_weight.shape[1]
    cells = rows * cols
    peers = lax.axis_size("space")
    length = 9 * channels + in_channels
    taps = out_kernel.reshape(9, channels, channels)
    params = pltpu.CompilerParams(vmem_limit_bytes=48 * 2**20)
    halves = peers == 2
    if halves:
        sums = [jax.ShapeDtypeStruct((length, channels // 2), kind) for kind in (F32, BF16)]
    else:
        sums = [jax.ShapeDtypeStruct((length, channels), F32)]
    outs, tops, parts = [], [], None
    for image in range(images):
        cot = cotangent[image]
        cot_before, cot_after = neighbour_rows(cot)
        merged, grad_top, *part = pl.pallas_call(
            functools.partial(grads_kernel, peers),
            out_shape=[
                jax.ShapeDtypeStruct((cells, channels), BF16),
                jax.ShapeDtypeStruct((rows // 2, cols // 2, channels), BF16),
                *sums,
            ],
            scratch_shapes=[pltpu.VMEM((rows + 2, cols, 3 * channels), BF16)],
            compiler_params=params,
            cost_estimate=pl.CostEstimate(
                flops=2 * cells * channels * (18 * channels + 2 * in_channels), bytes_accessed=6 * 2**20, transcendentals=0
            ),
        )(
            features[image].reshape(cells, in_channels),
            top_down[image],
            lateral_weight,
            taps,
            cot,
            cot_before,
            cot_after,
        )
        merged = merged.reshape(rows, cols, channels)
        before, after = neighbour_rows(merged)
        outs.append(
            pl.pallas_call(
                functools.partial(forward_kernel, peers),
                out_shape=jax.ShapeDtypeStruct((rows, cols, channels), BF16),
                scratch_shapes=[pltpu.VMEM((rows + 2, cols, 3 * channels), BF16)],
                compiler_params=params,
                cost_estimate=pl.CostEstimate(
                    flops=2 * cells * channels * 9 * channels, bytes_accessed=2 * 2**20, transcendentals=0
                ),
            )(merged, taps, before, after)
        )
        tops.append(grad_top)
        parts = part if parts is None else [
            (a.astype(F32) + b.astype(F32)).astype(a.dtype) for a, b in zip(parts, part)
        ]
    scale = 1.0 / (images * lax.axis_size("dp"))
    if halves:
        total = sum_everywhere(*parts, scale)
    else:
        total = (lax.psum(parts[0], ("dp", "space")) * scale).astype(BF16)
    grad_kernel = total[: 9 * channels].reshape(3, 3, channels, channels)
    return jnp.stack(outs), jnp.stack(tops), grad_kernel, total[9 * channels :]


def solution(mesh):
    return jax.shard_map(
        local,
        mesh=mesh,
        in_specs=(
            P("dp", "space", None, None),
            P("dp", "space", None, None),
            P(),
            P(),
            P("dp", "space", None, None),
        ),
        out_specs=(P("dp", "space", None, None), P("dp", "space", None, None), P(), P()),
        check_vma=False,
    )
```

```python
import functools

import jax
import jax.numpy as jnp
from jax import lax
from jax.experimental import pallas as pl
from jax.experimental.pallas import tpu as pltpu
from jax.sharding import PartitionSpec as P

F32 = jnp.float32
BF16 = jnp.bfloat16


def neighbour_rows(array):
    peers = lax.axis_size("space")
    rows = array.shape[0]
    if peers == 1:
        return array[0], array[0]
    if peers == 2:
        here = lax.axis_index("space")
        edge = lax.dynamic_index_in_dim(array, (1 - here) * (rows - 1), 0, keepdims=False)
        got = lax.ppermute(edge, "space", [(0, 1), (1, 0)])
        return got, got
    up = [(i, i + 1) for i in range(peers - 1)]
    down = [(j, i) for i, j in up]
    return lax.ppermute(array[-1], "space", up), lax.ppermute(array[0], "space", down)


def put_shifted(stack, slot, row, sign):
    cols, channels = row.shape
    wide = row.astype(F32)
    place = lax.broadcasted_iota(jnp.int32, (cols, channels), 0)
    later = jnp.where(place == cols - 1, 0.0, pltpu.roll(wide, cols - 1, 0)).astype(BF16)
    earlier = jnp.where(place == 0, 0.0, pltpu.roll(wide, 1, 0)).astype(BF16)
    first, last = (earlier, later) if sign < 0 else (later, earlier)
    stack[slot, :, 0:channels] = first
    stack[slot, :, channels : 2 * channels] = row
    stack[slot, :, 2 * channels :] = last


def put_halo(stack, before, after, rows, peers, sign):
    here = lax.axis_index("space")
    zero = jnp.zeros(before.shape, BF16)
    put_shifted(stack, 0, jnp.where(here > 0, before[...], zero), sign)
    put_shifted(stack, rows + 1, jnp.where(here < peers - 1, after[...], zero), sign)


def grads_kernel(peers, *refs):
    far, (before, after, merged, grad_top), rest = refs[:5], refs[5:9], refs[9:]
    outs, stack, near, sems = rest[:-7], rest[-7], rest[-6:-1], rest[-1]
    copies = [pltpu.make_async_copy(a, b, sems.at[i]) for i, (a, b) in enumerate(zip(far, near))]
    for copy in copies:
        copy.start()
    feat, lat_w, top, cot, out_w = near
    for copy in copies[:3]:
        copy.wait()
    rows, cols, channels = cot.shape
    cells = rows * cols
    half = cols // 2
    in_channels = lat_w.shape[0]
    upper = lax.broadcasted_iota(jnp.int32, (cols, half), 0)
    spread = jnp.where(upper // 2 == lax.broadcasted_iota(jnp.int32, (cols, half), 1), 1.0, 0.0).astype(BF16)
    lateral = jnp.dot(feat[...], lat_w[...], preferred_element_type=F32)
    for q in range(rows // 2):
        lifted = jnp.dot(spread, top[q], preferred_element_type=F32)
        for r in (2 * q, 2 * q + 1):
            merged[r * cols : (r + 1) * cols, :] = (lateral[r * cols : (r + 1) * cols] + lifted).astype(BF16)
    copies[3].wait()
    for r in range(rows):
        put_shifted(stack, r + 1, cot[r], 1)
    put_halo(stack, before, after, rows, peers, 1)

    def put(start, block):
        if len(outs) == 1:
            outs[0][start : start + block.shape[0], :] = block
            return
        here = lax.axis_index("space")
        left, right = block[:, : channels // 2], block[:, channels // 2 :]
        mine, theirs = outs
        mine[start : start + block.shape[0], :] = jnp.where(here == 0, left, right)
        theirs[start : start + block.shape[0], :] = jnp.where(here == 0, right, left).astype(BF16)

    merged_t = jnp.transpose(merged[...])
    for i in range(3):
        strip = stack[2 - i : 2 - i + rows].reshape(cells, 3 * channels)
        part = jnp.dot(merged_t, strip, preferred_element_type=F32)
        for j in range(3):
            put((3 * i + j) * channels, part[:, j * channels : (j + 1) * channels])
    copies[4].wait()
    total = jnp.zeros((cells, channels), F32)
    for i in range(3):
        strip = stack[2 - i : 2 - i + rows].reshape(cells, 3 * channels)
        taps = jnp.concatenate([out_w[3 * i + j] for j in range(3)], axis=1)
        total = total + lax.dot_general(strip, taps, (((1,), (1,)), ((), ())), preferred_element_type=F32)
    grad = total.astype(BF16)
    lower = lax.broadcasted_iota(jnp.int32, (half, 2 * cols), 1)
    lower = jnp.where(lower >= cols, lower - cols, lower)
    pool = jnp.where(lower // 2 == lax.broadcasted_iota(jnp.int32, (half, 2 * cols), 0), 1.0, 0.0).astype(BF16)
    for q in range(rows // 2):
        pair = grad[2 * q * cols : (2 * q + 2) * cols]
        grad_top[q] = jnp.dot(pool, pair, preferred_element_type=F32).astype(BF16)
    feat_t = jnp.transpose(feat[...])
    put(9 * channels, jnp.dot(feat_t, grad, preferred_element_type=F32))


def forward_kernel(peers, merged, out_w, before, after, out, stack):
    rows, cols, channels = merged.shape
    for r in range(rows):
        put_shifted(stack, r + 1, merged[r], -1)
    put_halo(stack, before, after, rows, peers, -1)
    total = jnp.zeros((rows * cols, channels), F32)
    for i in range(3):
        strip = stack[i : i + rows].reshape(rows * cols, 3 * channels)
        taps = out_w[3 * i : 3 * i + 3].reshape(3 * channels, channels)
        total = total + jnp.dot(strip, taps, preferred_element_type=F32)
    out[...] = total.astype(BF16).reshape(out.shape)


def part_places():
    here = lax.axis_index("dp")
    return here % 4, here // 4


def piece(ref, index, length):
    return ref.at[pl.ds(pl.multiple_of(index * length, 16), length), :]


def split_kernel(sizes, mine, got, *outs):
    start = 0
    for place, size, quarter in zip(part_places(), sizes, (outs[:4], outs[4:])):
        share = size // 4
        for k in range(4):
            rows = pl.ds(pl.multiple_of(start + (place ^ k) * share, 16), share)
            quarter[k][...] = (mine[rows, :] + got[rows, :].astype(F32)).astype(quarter[k].dtype)
        start += size


def resplit_kernel(*refs):
    plane, line = part_places()
    outs, scratch = refs[8:16], refs[16:]
    for place, terms, quarter, total in ((line, refs[0:4], outs[:4], scratch[0]), (plane, refs[4:8], outs[4:], scratch[1])):
        total[...] = terms[0][...] + sum(term[...].astype(F32) for term in terms[1:])
        for k in range(4):
            quarter[k][...] = piece(total, place ^ k, quarter[k].shape[0])[...].astype(quarter[k].dtype)


def finish_kernel(scale, *refs):
    for terms, out in ((refs[0:4], refs[8]), (refs[4:8], refs[9])):
        total = terms[0][...] + sum(term[...].astype(F32) for term in terms[1:])
        out[...] = (total * scale).astype(BF16)


def join_kernel(*refs):
    plane, line = part_places()
    for place, terms, out in ((line, refs[0:4], refs[8]), (plane, refs[4:8], refs[9])):
        for k in range(4):
            piece(out, place ^ k, terms[k].shape[0])[...] = terms[k][...]


def place_kernel(sizes, *refs):
    plane, line = part_places()
    side = lax.axis_index("space")
    kernel_out, lateral_out, sems = refs[16:]
    edge = kernel_out.shape[0]
    waits = []
    for columns, quarters in ((side, refs[:8]), (1 - side, refs[8:16])):
        lanes = pl.ds(pl.multiple_of(columns * 128, 128), 128)
        for part, (place, size) in enumerate(zip((plane, line), sizes)):
            share = size // 4
            for k in range(4):
                index, sem, source = place ^ k, sems.at[len(waits)], quarters[4 * part + k]
                if part == 0:
                    rows = pl.ds(pl.multiple_of(index * share, 16), share)
                    copy = pltpu.make_async_copy(source, kernel_out.at[rows, lanes], sem)
                    copy.start()
                else:
                    inside = (edge - sizes[0]) // share

                    @pl.when(index < inside)
                    def _():
                        rows = pl.ds(pl.multiple_of(sizes[0] + index * share, 16), share)
                        pltpu.make_async_copy(source, kernel_out.at[rows, lanes], sem).start()

                    @pl.when(index >= inside)
                    def _():
                        rows = pl.ds(pl.multiple_of((index - inside) * share, 16), share)
                        pltpu.make_async_copy(source, lateral_out.at[rows, lanes], sem).start()

                    copy = pltpu.make_async_copy(source, lateral_out.at[pl.ds(0, share), lanes], sem)
                waits.append(copy)
    for copy in waits:
        copy.wait()


def exchange(pieces, group):
    moves = {"plane": lambda d, k: d ^ k, "line": lambda d, k: d ^ (4 * k)}[group]
    return [pieces[0]] + [
        lax.ppermute(pieces[k], "dp", [(d, moves(d, k)) for d in range(16)]) for k in (1, 2, 3)
    ]


def call(kernel, shapes, scratch=(), **more):
    return pl.pallas_call(
        kernel,
        out_shape=[jax.ShapeDtypeStruct(shape, kind) for shape, kind in shapes],
        scratch_shapes=list(scratch),
        compiler_params=pltpu.CompilerParams(vmem_limit_bytes=32 * 2**20),
        **more,
    )


def sum_everywhere(mine, theirs, scale, edge):
    length, width = mine.shape
    sizes = (7 * length // 11, 4 * length // 11)
    shares = [size // 4 for size in sizes]
    ends = [share // 4 for share in shares]
    swap = [(0, 1), (1, 0)]
    got = lax.ppermute(theirs, "space", swap)
    first = call(
        functools.partial(split_kernel, sizes),
        [((share, width), F32 if k == 0 else BF16) for share in shares for k in range(4)],
    )(mine, got)
    part_a = exchange(first[:4], "plane")
    part_b = exchange(first[4:], "line")
    second = call(
        resplit_kernel,
        [((end, width), F32 if k == 0 else BF16) for end in ends for k in range(4)],
        [pltpu.VMEM((share, width), F32) for share in shares],
    )(*part_a, *part_b)
    part_a = exchange(second[:4], "line")
    part_b = exchange(second[4:], "plane")
    part_a, part_b = call(
        functools.partial(finish_kernel, scale), [((end, width), BF16) for end in ends]
    )(*part_a, *part_b)
    part_a = exchange([part_a] * 4, "line")
    part_b = exchange([part_b] * 4, "plane")
    part_a, part_b = call(join_kernel, [((share, width), BF16) for share in shares])(*part_a, *part_b)
    pieces = exchange([part_a] * 4, "plane") + exchange([part_b] * 4, "line")
    others = [lax.ppermute(one, "space", swap) for one in pieces]
    return call(
        functools.partial(place_kernel, sizes),
        [((edge, 2 * width), BF16), ((length - edge, 2 * width), BF16)],
        [pltpu.SemaphoreType.DMA((16,))],
        out_specs=[pl.BlockSpec(memory_space=pltpu.HBM)] * 2,
    )(*pieces, *others)


def local(features, top_down, lateral_weight, out_kernel, cotangent):
    images, rows, cols, in_channels = features.shape
    channels = lateral_weight.shape[1]
    cells = rows * cols
    peers = lax.axis_size("space")
    length = 9 * channels + in_channels
    taps = out_kernel.reshape(9, channels, channels)
    params = pltpu.CompilerParams(vmem_limit_bytes=48 * 2**20)
    halves = peers == 2 and lax.axis_size("dp") == 16 and (channels, in_channels) == (256, 512)
    if halves:
        sums = [jax.ShapeDtypeStruct((length, channels // 2), kind) for kind in (F32, BF16)]
    else:
        sums = [jax.ShapeDtypeStruct((length, channels), F32)]
    outs, tops, parts = [], [], None
    for image in range(images):
        cot = cotangent[image]
        cot_before, cot_after = neighbour_rows(cot)
        arrays = (features[image].reshape(cells, in_channels), lateral_weight, top_down[image], cot, taps)
        merged, grad_top, *part = pl.pallas_call(
            functools.partial(grads_kernel, peers),
            out_shape=[
                jax.ShapeDtypeStruct((cells, channels), BF16),
                jax.ShapeDtypeStruct((rows // 2, cols // 2, channels), BF16),
                *sums,
            ],
            in_specs=[pl.BlockSpec(memory_space=pltpu.HBM)] * 5 + [pl.BlockSpec(memory_space=pltpu.VMEM)] * 2,
            scratch_shapes=[
                pltpu.VMEM((rows + 2, cols, 3 * channels), BF16),
                *[pltpu.VMEM(array.shape, BF16) for array in arrays],
                pltpu.SemaphoreType.DMA((5,)),
            ],
            compiler_params=params,
            cost_estimate=pl.CostEstimate(
                flops=2 * cells * channels * (18 * channels + 2 * in_channels), bytes_accessed=6 * 2**20, transcendentals=0
            ),
        )(*arrays, cot_before, cot_after)
        merged = merged.reshape(rows, cols, channels)
        before, after = neighbour_rows(merged)
        outs.append(
            pl.pallas_call(
                functools.partial(forward_kernel, peers),
                out_shape=jax.ShapeDtypeStruct((rows, cols, channels), BF16),
                scratch_shapes=[pltpu.VMEM((rows + 2, cols, 3 * channels), BF16)],
                compiler_params=params,
                cost_estimate=pl.CostEstimate(
                    flops=2 * cells * channels * 9 * channels, bytes_accessed=2 * 2**20, transcendentals=0
                ),
            )(merged, taps, before, after)
        )
        tops.append(grad_top)
        parts = part if parts is None else [
            (a.astype(F32) + b.astype(F32)).astype(a.dtype) for a, b in zip(parts, part)
        ]
    scale = 1.0 / (images * lax.axis_size("dp"))
    if halves:
        grad_kernel, grad_lateral = sum_everywhere(*parts, scale, 9 * channels)
    else:
        total = (lax.psum(parts[0], ("dp", "space")) * scale).astype(BF16)
        grad_kernel, grad_lateral = total[: 9 * channels], total[9 * channels :]
    return jnp.stack(outs), jnp.stack(tops), grad_kernel.reshape(out_kernel.shape), grad_lateral


def solution(mesh):
    return jax.shard_map(
        local,
        mesh=mesh,
        in_specs=(
            P("dp", "space", None, None),
            P("dp", "space", None, None),
            P(),
            P(),
            P("dp", "space", None, None),
        ),
        out_specs=(P("dp", "space", None, None), P("dp", "space", None, None), P(), P()),
        check_vma=False,
    )
```

```python
import functools

import jax
import jax.numpy as jnp
from jax import lax
from jax.experimental import pallas as pl
from jax.experimental.pallas import tpu as pltpu
from jax.sharding import PartitionSpec as P

F32 = jnp.float32
BF16 = jnp.bfloat16


def neighbour_rows(array):
    peers = lax.axis_size("space")
    rows = array.shape[0]
    if peers == 1:
        return array[0], array[0]
    if peers == 2:
        here = lax.axis_index("space")
        edge = lax.dynamic_index_in_dim(array, (1 - here) * (rows - 1), 0, keepdims=False)
        got = lax.ppermute(edge, "space", [(0, 1), (1, 0)])
        return got, got
    up = [(i, i + 1) for i in range(peers - 1)]
    down = [(j, i) for i, j in up]
    return lax.ppermute(array[-1], "space", up), lax.ppermute(array[0], "space", down)


def put_shifted(stack, slot, row, sign):
    cols, channels = row.shape
    wide = row.astype(F32)
    place = lax.broadcasted_iota(jnp.int32, (cols, channels), 0)
    later = jnp.where(place == cols - 1, 0.0, pltpu.roll(wide, cols - 1, 0)).astype(BF16)
    earlier = jnp.where(place == 0, 0.0, pltpu.roll(wide, 1, 0)).astype(BF16)
    first, last = (earlier, later) if sign < 0 else (later, earlier)
    stack[slot, :, 0:channels] = first
    stack[slot, :, channels : 2 * channels] = row
    stack[slot, :, 2 * channels :] = last


def put_halo(stack, before, after, rows, peers, sign):
    here = lax.axis_index("space")
    zero = jnp.zeros(before.shape, BF16)
    put_shifted(stack, 0, jnp.where(here > 0, before, zero), sign)
    put_shifted(stack, rows + 1, jnp.where(here < peers - 1, after, zero), sign)


def grads_kernel(peers, *refs):
    far, (before, after, merged, grad_top), rest = refs[:5], refs[5:9], refs[9:]
    outs, stack, near, sems = rest[:-7], rest[-7], rest[-6:-1], rest[-1]
    copies = [pltpu.make_async_copy(a, b, sems.at[i]) for i, (a, b) in enumerate(zip(far, near))]
    for copy in copies:
        copy.start()
    feat, lat_w, top, cot, out_w = near
    for copy in copies[:3]:
        copy.wait()
    rows, cols, channels = cot.shape
    cells = rows * cols
    half = cols // 2
    in_channels = lat_w.shape[0]
    upper = lax.broadcasted_iota(jnp.int32, (cols, half), 0)
    spread = jnp.where(upper // 2 == lax.broadcasted_iota(jnp.int32, (cols, half), 1), 1.0, 0.0).astype(BF16)
    lateral = jnp.dot(feat[...], lat_w[...], preferred_element_type=F32)
    for q in range(rows // 2):
        lifted = jnp.dot(spread, top[q], preferred_element_type=F32)
        for r in (2 * q, 2 * q + 1):
            merged[r * cols : (r + 1) * cols, :] = (lateral[r * cols : (r + 1) * cols] + lifted).astype(BF16)
    copies[3].wait()
    for r in range(rows):
        put_shifted(stack, r + 1, cot[r], 1)
    put_halo(stack, before[...], after[...], rows, peers, 1)

    def put(start, block):
        if len(outs) == 1:
            outs[0][start : start + block.shape[0], :] = block
            return
        here = lax.axis_index("space")
        left, right = block[:, : channels // 2], block[:, channels // 2 :]
        mine, theirs = outs
        mine[start : start + block.shape[0], :] = jnp.where(here == 0, left, right)
        theirs[start : start + block.shape[0], :] = jnp.where(here == 0, right, left).astype(BF16)

    if len(outs) == 2:
        here = lax.axis_index("space")
        edge = jnp.where(here == 0, merged[cells - cols :, :], merged[:cols, :])
        start = 9 * channels + in_channels
        outs[1][start : start + cols, :] = edge[:, : channels // 2]
        outs[1][start + cols :, :] = edge[:, channels // 2 :]
    merged_t = jnp.transpose(merged[...])
    for i in range(3):
        strip = stack[2 - i : 2 - i + rows].reshape(cells, 3 * channels)
        part = jnp.dot(merged_t, strip, preferred_element_type=F32)
        for j in range(3):
            put((3 * i + j) * channels, part[:, j * channels : (j + 1) * channels])
    copies[4].wait()
    total = jnp.zeros((cells, channels), F32)
    for i in range(3):
        strip = stack[2 - i : 2 - i + rows].reshape(cells, 3 * channels)
        taps = jnp.concatenate([out_w[3 * i + j] for j in range(3)], axis=1)
        total = total + lax.dot_general(strip, taps, (((1,), (1,)), ((), ())), preferred_element_type=F32)
    grad = total.astype(BF16)
    lower = lax.broadcasted_iota(jnp.int32, (half, 2 * cols), 1)
    lower = jnp.where(lower >= cols, lower - cols, lower)
    pool = jnp.where(lower // 2 == lax.broadcasted_iota(jnp.int32, (half, 2 * cols), 0), 1.0, 0.0).astype(BF16)
    for q in range(rows // 2):
        pair = grad[2 * q * cols : (2 * q + 2) * cols]
        grad_top[q] = jnp.dot(pool, pair, preferred_element_type=F32).astype(BF16)
    feat_t = jnp.transpose(feat[...])
    put(9 * channels, jnp.dot(feat_t, grad, preferred_element_type=F32))


def forward_kernel(peers, merged, out_w, *refs):
    edges, (out, stack) = refs[:-2], refs[-2:]
    rows, cols, channels = merged.shape
    for r in range(rows):
        put_shifted(stack, r + 1, merged[r], -1)
    if len(edges) == 1:
        start = edges[0].shape[0] - 2 * cols
        edge = jnp.concatenate([edges[0][start : start + cols, :], edges[0][start + cols :, :]], axis=1)
        put_halo(stack, edge, edge, rows, peers, -1)
    else:
        put_halo(stack, edges[0][...], edges[1][...], rows, peers, -1)
    total = jnp.zeros((rows * cols, channels), F32)
    for i in range(3):
        strip = stack[i : i + rows].reshape(rows * cols, 3 * channels)
        taps = out_w[3 * i : 3 * i + 3].reshape(3 * channels, channels)
        total = total + jnp.dot(strip, taps, preferred_element_type=F32)
    out[...] = total.astype(BF16).reshape(out.shape)


def place_kernel(mine, other, kernel_out, lateral_out, sems):
    side = lax.axis_index("space")
    edge, rest = kernel_out.shape[0], lateral_out.shape[0]
    copies = []
    for columns, half in ((side, mine), (1 - side, other)):
        lanes = pl.ds(pl.multiple_of(columns * 128, 128), 128)
        copies.append((half.at[pl.ds(0, edge), :], kernel_out.at[:, lanes]))
        copies.append((half.at[pl.ds(edge, rest), :], lateral_out.at[:, lanes]))
    copies = [pltpu.make_async_copy(source, to, sems.at[i]) for i, (source, to) in enumerate(copies)]
    for copy in copies:
        copy.start()
    for copy in copies:
        copy.wait()


def peer_groups():
    plane = [[4 * z + q for q in range(4)] for z in range(4)]
    line = [[4 * z + q for z in range(4)] for q in range(4)]
    pick = lambda chips, core: [[2 * chip + core for chip in group] for group in chips]
    return pick(plane, 0) + pick(line, 1), pick(line, 0) + pick(plane, 1)


def swap_pieces(pieces, groups):
    return lax.all_to_all(pieces, ("dp", "space"), 0, 0, axis_index_groups=groups, tiled=True)


def sum_everywhere(mine, got, scale, edge):
    length, width = mine.shape
    swap = [(0, 1), (1, 0)]
    first, second = peer_groups()
    pair = (mine + got[:length].astype(F32)).astype(BF16).reshape(4, length // 4, width)
    total = jnp.sum(swap_pieces(pair, first).astype(F32), axis=0).astype(BF16).reshape(4, length // 16, width)
    total = (jnp.sum(swap_pieces(total, second).astype(F32), axis=0) * scale).astype(BF16)
    total = swap_pieces(jnp.broadcast_to(total[None], (4, *total.shape)), second).reshape(length // 4, width)
    total = swap_pieces(jnp.broadcast_to(total[None], (4, *total.shape)), first).reshape(length, width)
    other = lax.ppermute(total, "space", swap)
    return pl.pallas_call(
        place_kernel,
        out_shape=[jax.ShapeDtypeStruct((rows, 2 * width), BF16) for rows in (edge, length - edge)],
        out_specs=[pl.BlockSpec(memory_space=pltpu.HBM)] * 2,
        scratch_shapes=[pltpu.SemaphoreType.DMA((4,))],
    )(total, other)


def local(features, top_down, lateral_weight, out_kernel, cotangent):
    images, rows, cols, in_channels = features.shape
    channels = lateral_weight.shape[1]
    cells = rows * cols
    peers = lax.axis_size("space")
    length = 9 * channels + in_channels
    taps = out_kernel.reshape(9, channels, channels)
    params = pltpu.CompilerParams(vmem_limit_bytes=48 * 2**20)
    halves = peers == 2 and lax.axis_size("dp") == 16 and images == 1 and (channels, in_channels) == (256, 512)
    if halves:
        sums = [
            jax.ShapeDtypeStruct((length, channels // 2), F32),
            jax.ShapeDtypeStruct((length + 2 * cols, channels // 2), BF16),
        ]
    else:
        sums = [jax.ShapeDtypeStruct((length, channels), F32)]
    outs, tops, parts = [], [], None
    for image in range(images):
        cot = cotangent[image]
        cot_before, cot_after = neighbour_rows(cot)
        arrays = (features[image].reshape(cells, in_channels), lateral_weight, top_down[image], cot, taps)
        arrays = [pltpu.with_memory_space_constraint(array, pltpu.HBM) for array in arrays]
        merged, grad_top, *part = pl.pallas_call(
            functools.partial(grads_kernel, peers),
            out_shape=[
                jax.ShapeDtypeStruct((cells, channels), BF16),
                jax.ShapeDtypeStruct((rows // 2, cols // 2, channels), BF16),
                *sums,
            ],
            in_specs=[pl.BlockSpec(memory_space=pltpu.HBM)] * 5 + [pl.BlockSpec(memory_space=pltpu.VMEM)] * 2,
            scratch_shapes=[
                pltpu.VMEM((rows + 2, cols, 3 * channels), BF16),
                *[pltpu.VMEM(array.shape, BF16) for array in arrays],
                pltpu.SemaphoreType.DMA((5,)),
            ],
            compiler_params=params,
            cost_estimate=pl.CostEstimate(
                flops=2 * cells * channels * (18 * channels + 2 * in_channels), bytes_accessed=6 * 2**20, transcendentals=0
            ),
        )(*arrays, cot_before, cot_after)
        merged = merged.reshape(rows, cols, channels)
        if halves:
            part[1] = lax.ppermute(part[1], "space", [(0, 1), (1, 0)])
        edges = (part[1],) if halves else neighbour_rows(merged)
        outs.append(
            pl.pallas_call(
                functools.partial(forward_kernel, peers),
                out_shape=jax.ShapeDtypeStruct((rows, cols, channels), BF16),
                scratch_shapes=[pltpu.VMEM((rows + 2, cols, 3 * channels), BF16)],
                compiler_params=params,
                cost_estimate=pl.CostEstimate(
                    flops=2 * cells * channels * 9 * channels, bytes_accessed=2 * 2**20, transcendentals=0
                ),
            )(merged, taps, *edges)
        )
        tops.append(grad_top)
        parts = part if parts is None else [a + b for a, b in zip(parts, part)]
    scale = 1.0 / (images * lax.axis_size("dp"))
    if halves:
        grad_kernel, grad_lateral = sum_everywhere(*parts, scale, 9 * channels)
    else:
        total = (lax.psum(parts[0], ("dp", "space")) * scale).astype(BF16)
        grad_kernel, grad_lateral = total[: 9 * channels], total[9 * channels :]
    return jnp.stack(outs), jnp.stack(tops), grad_kernel.reshape(out_kernel.shape), grad_lateral


def solution(mesh):
    return jax.shard_map(
        local,
        mesh=mesh,
        in_specs=(
            P("dp", "space", None, None),
            P("dp", "space", None, None),
            P(),
            P(),
            P("dp", "space", None, None),
        ),
        out_specs=(P("dp", "space", None, None), P("dp", "space", None, None), P(), P()),
        check_vma=False,
    )
```

```python
import functools

import jax
import jax.numpy as jnp
from jax import lax
from jax.experimental import pallas as pl
from jax.experimental.pallas import tpu as pltpu
from jax.sharding import PartitionSpec as P

F32 = jnp.float32
BF16 = jnp.bfloat16


def neighbour_rows(array):
    peers = lax.axis_size("space")
    rows = array.shape[0]
    if peers == 1:
        return array[0], array[0]
    if peers == 2:
        here = lax.axis_index("space")
        edge = lax.dynamic_index_in_dim(array, (1 - here) * (rows - 1), 0, keepdims=False)
        got = lax.ppermute(edge, "space", [(0, 1), (1, 0)])
        return got, got
    up = [(i, i + 1) for i in range(peers - 1)]
    down = [(j, i) for i, j in up]
    return lax.ppermute(array[-1], "space", up), lax.ppermute(array[0], "space", down)


def put_shifted(stack, slot, row, sign):
    cols, channels = row.shape
    wide = row.astype(F32)
    place = lax.broadcasted_iota(jnp.int32, (cols, channels), 0)
    later = jnp.where(place == cols - 1, 0.0, pltpu.roll(wide, cols - 1, 0)).astype(BF16)
    earlier = jnp.where(place == 0, 0.0, pltpu.roll(wide, 1, 0)).astype(BF16)
    first, last = (earlier, later) if sign < 0 else (later, earlier)
    stack[slot, :, 0:channels] = first
    stack[slot, :, channels : 2 * channels] = row
    stack[slot, :, 2 * channels :] = last


def put_halo(stack, before, after, rows, peers, sign):
    here = lax.axis_index("space")
    zero = jnp.zeros(before.shape, BF16)
    put_shifted(stack, 0, jnp.where(here > 0, before, zero), sign)
    put_shifted(stack, rows + 1, jnp.where(here < peers - 1, after, zero), sign)


def grads_kernel(peers, *refs):
    far, (before, after, merged, grad_top), rest = refs[:5], refs[5:9], refs[9:]
    outs, stack, near, sems = rest[:-7], rest[-7], rest[-6:-1], rest[-1]
    copies = [pltpu.make_async_copy(a, b, sems.at[i]) for i, (a, b) in enumerate(zip(far, near))]
    for copy in copies:
        copy.start()
    feat, lat_w, top, cot, out_w = near
    for copy in copies[:3]:
        copy.wait()
    rows, cols, channels = cot.shape
    cells = rows * cols
    half = cols // 2
    in_channels = lat_w.shape[0]
    upper = lax.broadcasted_iota(jnp.int32, (cols, half), 0)
    spread = jnp.where(upper // 2 == lax.broadcasted_iota(jnp.int32, (cols, half), 1), 1.0, 0.0).astype(BF16)
    lateral = jnp.dot(feat[...], lat_w[...], preferred_element_type=F32)
    for q in range(rows // 2):
        lifted = jnp.dot(spread, top[q], preferred_element_type=F32)
        for r in (2 * q, 2 * q + 1):
            merged[r * cols : (r + 1) * cols, :] = (lateral[r * cols : (r + 1) * cols] + lifted).astype(BF16)
    copies[3].wait()
    for r in range(rows):
        put_shifted(stack, r + 1, cot[r], 1)
    put_halo(stack, before[...], after[...], rows, peers, 1)

    def put(start, block):
        if len(outs) == 1:
            outs[0][start : start + block.shape[0], :] = block
            return
        here = lax.axis_index("space")
        left, right = block[:, : channels // 2], block[:, channels // 2 :]
        mine, theirs = outs
        mine[start : start + block.shape[0], :] = jnp.where(here == 0, left, right)
        theirs[start : start + block.shape[0], :] = jnp.where(here == 0, right, left).astype(BF16)

    if len(outs) == 2:
        here = lax.axis_index("space")
        edge = jnp.where(here == 0, merged[cells - cols :, :], merged[:cols, :])
        start = 9 * channels + in_channels
        outs[1][start : start + cols, :] = edge[:, : channels // 2]
        outs[1][start + cols :, :] = edge[:, channels // 2 :]
    merged_t = jnp.transpose(merged[...])
    for i in range(3):
        strip = stack[2 - i : 2 - i + rows].reshape(cells, 3 * channels)
        part = jnp.dot(merged_t, strip, preferred_element_type=F32)
        for j in range(3):
            put((3 * i + j) * channels, part[:, j * channels : (j + 1) * channels])
    copies[4].wait()
    total = jnp.zeros((cells, channels), F32)
    for i in range(3):
        strip = stack[2 - i : 2 - i + rows].reshape(cells, 3 * channels)
        taps = jnp.concatenate([out_w[3 * i + j] for j in range(3)], axis=1)
        total = total + lax.dot_general(strip, taps, (((1,), (1,)), ((), ())), preferred_element_type=F32)
    grad = total.astype(BF16)
    lower = lax.broadcasted_iota(jnp.int32, (half, 2 * cols), 1)
    lower = jnp.where(lower >= cols, lower - cols, lower)
    pool = jnp.where(lower // 2 == lax.broadcasted_iota(jnp.int32, (half, 2 * cols), 0), 1.0, 0.0).astype(BF16)
    for q in range(rows // 2):
        pair = grad[2 * q * cols : (2 * q + 2) * cols]
        grad_top[q] = jnp.dot(pool, pair, preferred_element_type=F32).astype(BF16)
    feat_t = jnp.transpose(feat[...])
    put(9 * channels, jnp.dot(feat_t, grad, preferred_element_type=F32))


def forward_kernel(peers, merged, out_w, *refs):
    edges, (out, stack, near, sem) = refs[:-4], refs[-4:]
    rows, cols, channels = merged.shape
    for r in range(rows):
        put_shifted(stack, r + 1, merged[r], -1)
    if len(edges) == 1:
        start = edges[0].shape[0] - 2 * cols
        edge = jnp.concatenate([edges[0][start : start + cols, :], edges[0][start + cols :, :]], axis=1)
        put_halo(stack, edge, edge, rows, peers, -1)
    else:
        put_halo(stack, edges[0][...], edges[1][...], rows, peers, -1)
    total = jnp.zeros((rows * cols, channels), F32)
    for i in range(3):
        strip = stack[i : i + rows].reshape(rows * cols, 3 * channels)
        taps = out_w[3 * i : 3 * i + 3].reshape(3 * channels, channels)
        total = total + jnp.dot(strip, taps, preferred_element_type=F32)
    near[...] = total.astype(BF16).reshape(out.shape)
    copy = pltpu.make_async_copy(near, out, sem)
    copy.start()
    copy.wait()


def places():
    chip, core = lax.axis_index("dp"), lax.axis_index("space")
    x, y = chip % 2, (chip // 2) % 2
    return jnp.where(core == 0, x, y), jnp.where(core == 0, y, x), chip // 4


def block(index, length):
    return pl.ds(pl.multiple_of(index * length, 16), length)


def wide(ref):
    return ref[...].astype(F32)


def start_kernel(mine, got, for_both, for_first, for_second, own):
    first, second, _ = places()
    share = own.shape[0]
    for out, a, b in (
        (for_both, 1 - first, 1 - second),
        (for_first, 1 - first, second),
        (for_second, first, 1 - second),
        (own, first, second),
    ):
        rows = block(2 * a + b, share)
        out[...] = (mine[rows, :] + got[rows, :].astype(F32)).astype(out.dtype)


def add_kernel(mine, got, out):
    out[...] = (mine[...] + wide(got)).astype(out.dtype)


def line_kernel(mine, got_first, got_second, own, *sends):
    *_, z = places()
    share = own.shape[0]
    for k, out in enumerate((own, *sends)):
        rows = block(z ^ k, share)
        total = mine[rows, :] + got_first[rows, :].astype(F32) + got_second[rows, :].astype(F32)
        out[...] = total.astype(out.dtype)


def finish_kernel(scale, mine, *refs):
    total = mine[...]
    for got in refs[:-1]:
        total = total + wide(got)
    refs[-1][...] = (total * scale).astype(BF16)


def join_kernel(*refs):
    *_, z = places()
    for k, part in enumerate(refs[:-1]):
        refs[-1][block(z ^ k, part.shape[0]), :] = part[...]


def place_kernel(*refs):
    first, second, _ = places()
    side = lax.axis_index("space")
    kernel_out, lateral_out, sems = refs[8:]
    edge, share = kernel_out.shape[0], refs[0].shape[0]
    inside = edge - 3 * share
    waits = []
    for columns, quarters, a, b in ((side, refs[:4], first, second), (1 - side, refs[4:8], second, first)):
        lanes = pl.ds(pl.multiple_of(columns * 128, 128), 128)
        for quarter, (i, j) in zip(quarters, ((0, 0), (0, 1), (1, 0), (1, 1))):
            index = 2 * (a if i == 0 else 1 - a) + (b if j == 0 else 1 - b)
            base = pl.multiple_of(index * share, 16)
            head, tail = quarter.at[pl.ds(0, inside), :], quarter.at[pl.ds(inside, share - inside), :]
            sem = sems.at[len(waits)]
            copy = pltpu.make_async_copy(head, kernel_out.at[pl.ds(base, inside), lanes], sem)
            copy.start()
            waits.append(copy)
            sem = sems.at[len(waits)]

            @pl.when(index < 3)
            def _():
                rows = pl.ds(base + inside, share - inside)
                pltpu.make_async_copy(tail, kernel_out.at[rows, lanes], sem).start()

            @pl.when(index == 3)
            def _():
                pltpu.make_async_copy(tail, lateral_out.at[:, lanes], sem).start()

            waits.append(pltpu.make_async_copy(tail, lateral_out.at[:, lanes], sem))
    for copy in waits:
        copy.wait()


def exchange(array, step):
    pairs = []
    for chip in range(16):
        for core in range(2):
            flip = {"first": 1 + core, "second": 2 - core}.get(step) or 4 * step
            pairs.append((2 * chip + core, 2 * (chip ^ flip) + core))
    return lax.ppermute(array, ("dp", "space"), pairs)


def swap(array):
    return lax.ppermute(array, "space", [(0, 1), (1, 0)])


def call(kernel, *shapes, **more):
    return pl.pallas_call(
        kernel, out_shape=[jax.ShapeDtypeStruct(shape, kind) for shape, kind in shapes], **more
    )


def sum_everywhere(mine, got, scale, edge):
    length, width = mine.shape
    quarter, part = (length // 4, width), (length // 16, width)
    for_both, for_first, for_second, own = call(start_kernel, (quarter, BF16), (quarter, BF16), (quarter, F32), (quarter, F32))(mine, got)
    got_both = exchange(for_both, "first")
    got_first = exchange(for_first, "first")
    [for_second] = call(add_kernel, (quarter, BF16))(for_second, got_both)
    got_second = exchange(for_second, "second")
    own, *sends = call(line_kernel, (part, F32), *[(part, BF16)] * 3)(own, got_first, got_second)
    parts = [exchange(sends[k - 1], k) for k in (3, 2, 1)]
    [total] = call(functools.partial(finish_kernel, scale), (part, BF16))(own, *parts)
    parts = [exchange(total, k) for k in (3, 2, 1)]
    [here] = call(join_kernel, (quarter, BF16))(total, *parts[::-1])
    from_second = exchange(here, "second")
    from_first = exchange(here, "first")
    from_both = exchange(from_second, "first")
    quarters = [here, from_second, from_first, from_both]
    return call(
        place_kernel,
        ((edge, 2 * width), BF16),
        ((length - edge, 2 * width), BF16),
        out_specs=[pl.BlockSpec(memory_space=pltpu.HBM)] * 2,
        scratch_shapes=[pltpu.SemaphoreType.DMA((16,))],
    )(*quarters, *[swap(one) for one in quarters])


def local(features, top_down, lateral_weight, out_kernel, cotangent):
    images, rows, cols, in_channels = features.shape
    channels = lateral_weight.shape[1]
    cells = rows * cols
    peers = lax.axis_size("space")
    length = 9 * channels + in_channels
    taps = out_kernel.reshape(9, channels, channels)
    params = pltpu.CompilerParams(vmem_limit_bytes=48 * 2**20)
    halves = peers == 2 and lax.axis_size("dp") == 16 and images == 1 and (channels, in_channels) == (256, 512)
    if halves:
        sums = [
            jax.ShapeDtypeStruct((length, channels // 2), F32),
            jax.ShapeDtypeStruct((length + 2 * cols, channels // 2), BF16),
        ]
    else:
        sums = [jax.ShapeDtypeStruct((length, channels), F32)]
    outs, tops, parts = [], [], None
    for image in range(images):
        cot = cotangent[image]
        cot_before, cot_after = neighbour_rows(cot)
        arrays = (features[image].reshape(cells, in_channels), lateral_weight, top_down[image], cot, taps)
        arrays = [pltpu.with_memory_space_constraint(array, pltpu.HBM) for array in arrays]
        merged, grad_top, *part = pl.pallas_call(
            functools.partial(grads_kernel, peers),
            out_shape=[
                jax.ShapeDtypeStruct((cells, channels), BF16),
                jax.ShapeDtypeStruct((rows // 2, cols // 2, channels), BF16),
                *sums,
            ],
            in_specs=[pl.BlockSpec(memory_space=pltpu.HBM)] * 5 + [pl.BlockSpec(memory_space=pltpu.VMEM)] * 2,
            scratch_shapes=[
                pltpu.VMEM((rows + 2, cols, 3 * channels), BF16),
                *[pltpu.VMEM(array.shape, BF16) for array in arrays],
                pltpu.SemaphoreType.DMA((5,)),
            ],
            compiler_params=params,
            cost_estimate=pl.CostEstimate(
                flops=2 * cells * channels * (18 * channels + 2 * in_channels), bytes_accessed=6 * 2**20, transcendentals=0
            ),
        )(*arrays, cot_before, cot_after)
        merged = merged.reshape(rows, cols, channels)
        if halves:
            part[1] = swap(part[1])
        edges = (part[1],) if halves else neighbour_rows(merged)
        outs.append(
            pl.pallas_call(
                functools.partial(forward_kernel, peers),
                out_shape=jax.ShapeDtypeStruct((rows, cols, channels), BF16),
                out_specs=pl.BlockSpec(memory_space=pltpu.HBM),
                scratch_shapes=[
                    pltpu.VMEM((rows + 2, cols, 3 * channels), BF16),
                    pltpu.VMEM((rows, cols, channels), BF16),
                    pltpu.SemaphoreType.DMA,
                ],
                compiler_params=params,
                cost_estimate=pl.CostEstimate(
                    flops=2 * cells * channels * 9 * channels, bytes_accessed=2 * 2**20, transcendentals=0
                ),
            )(merged, taps, *edges)
        )
        tops.append(grad_top)
        parts = part if parts is None else [a + b for a, b in zip(parts, part)]
    scale = 1.0 / (images * lax.axis_size("dp"))
    if halves:
        grad_kernel, grad_lateral = sum_everywhere(*parts, scale, 9 * channels)
    else:
        total = (lax.psum(parts[0], ("dp", "space")) * scale).astype(BF16)
        grad_kernel, grad_lateral = total[: 9 * channels], total[9 * channels :]
    return jnp.stack(outs), jnp.stack(tops), grad_kernel.reshape(out_kernel.shape), grad_lateral


def solution(mesh):
    return jax.shard_map(
        local,
        mesh=mesh,
        in_specs=(
            P("dp", "space", None, None),
            P("dp", "space", None, None),
            P(),
            P(),
            P("dp", "space", None, None),
        ),
        out_specs=(P("dp", "space", None, None), P("dp", "space", None, None), P(), P()),
        check_vma=False,
    )
```

```python
import functools

import jax
import jax.numpy as jnp
from jax import lax
from jax.experimental import pallas as pl
from jax.experimental.pallas import tpu as pltpu
from jax.sharding import PartitionSpec as P

F32 = jnp.float32
BF16 = jnp.bfloat16


def neighbour_rows(array):
    peers = lax.axis_size("space")
    rows = array.shape[0]
    if peers == 1:
        return array[0], array[0]
    if peers == 2:
        here = lax.axis_index("space")
        edge = lax.dynamic_index_in_dim(array, (1 - here) * (rows - 1), 0, keepdims=False)
        got = lax.ppermute(edge, "space", [(0, 1), (1, 0)])
        return got, got
    up = [(i, i + 1) for i in range(peers - 1)]
    down = [(j, i) for i, j in up]
    return lax.ppermute(array[-1], "space", up), lax.ppermute(array[0], "space", down)


def put_shifted(stack, slot, row, sign):
    cols, channels = row.shape
    wide = row.astype(F32)
    place = lax.broadcasted_iota(jnp.int32, (cols, channels), 0)
    later = jnp.where(place == cols - 1, 0.0, pltpu.roll(wide, cols - 1, 0)).astype(BF16)
    earlier = jnp.where(place == 0, 0.0, pltpu.roll(wide, 1, 0)).astype(BF16)
    first, last = (earlier, later) if sign < 0 else (later, earlier)
    stack[slot, :, 0:channels] = first
    stack[slot, :, channels : 2 * channels] = row
    stack[slot, :, 2 * channels :] = last


def put_halo(stack, before, after, rows, peers, sign):
    here = lax.axis_index("space")
    zero = jnp.zeros(before.shape, BF16)
    put_shifted(stack, 0, jnp.where(here > 0, before, zero), sign)
    put_shifted(stack, rows + 1, jnp.where(here < peers - 1, after, zero), sign)


def merge_kernel(*refs):
    far, (merged, merged_t, stack), near, sems = refs[:4], refs[4:7], refs[7:11], refs[11]
    copies = [pltpu.make_async_copy(a, b, sems.at[i]) for i, (a, b) in enumerate(zip(far, near))]
    for copy in copies:
        copy.start()
    cot, lat_w, top, feat = near
    rows, cols, channels = cot.shape
    half = cols // 2
    copies[0].wait()
    for r in range(rows):
        put_shifted(stack, r, cot[r], 1)
    for copy in copies[1:]:
        copy.wait()
    upper = lax.broadcasted_iota(jnp.int32, (cols, half), 0)
    spread = jnp.where(upper // 2 == lax.broadcasted_iota(jnp.int32, (cols, half), 1), 1.0, 0.0).astype(BF16)
    lateral = jnp.dot(feat[...], lat_w[...], preferred_element_type=F32)
    for q in range(rows // 2):
        lifted = jnp.dot(spread, top[q], preferred_element_type=F32)
        for r in (2 * q, 2 * q + 1):
            merged[r * cols : (r + 1) * cols, :] = (lateral[r * cols : (r + 1) * cols] + lifted).astype(BF16)
    merged_t[...] = jnp.transpose(merged[...])


def grads_kernel(peers, packed, stack, merged, merged_t, before, after, feat_far, taps_far, grad_top, *rest):
    outs, halo, feat, out_w, sems = rest[:-4], *rest[-4:]
    copies = [pltpu.make_async_copy(feat_far, feat, sems.at[0]), pltpu.make_async_copy(taps_far, out_w, sems.at[1])]
    for copy in copies:
        copy.start()
    rows, cols, deep = stack.shape
    channels, cells = merged_t.shape
    in_channels = feat.shape[1]
    half = cols // 2
    put_halo(halo, before[...], after[...], 0, peers, 1)
    strips = [
        jnp.concatenate([stack[1:], halo[1:]], axis=0),
        stack[...],
        jnp.concatenate([halo[:1], stack[: rows - 1]], axis=0),
    ]
    strips = [strip.reshape(cells, deep) for strip in strips]

    def put(start, block):
        if not packed:
            outs[0][start : start + block.shape[0], :] = block
            return
        here = lax.axis_index("space")
        left, right = block[:, : channels // 2], block[:, channels // 2 :]
        mine, theirs = outs
        mine[start : start + block.shape[0], :] = jnp.where(here == 0, left, right)
        theirs[start : start + block.shape[0], :] = jnp.where(here == 0, right, left).astype(BF16)

    if packed:
        here = lax.axis_index("space")
        edge = jnp.where(here == 0, merged[cells - cols :, :], merged[:cols, :])
        start = 9 * channels + in_channels
        outs[1][start : start + cols, :] = edge[:, : channels // 2]
        outs[1][start + cols :, :] = edge[:, channels // 2 :]
    for i in range(3):
        part = jnp.dot(merged_t[...], strips[i], preferred_element_type=F32)
        for j in range(3):
            put((3 * i + j) * channels, part[:, j * channels : (j + 1) * channels])
    for copy in copies:
        copy.wait()
    total = jnp.zeros((cells, channels), F32)
    for i in range(3):
        taps = jnp.concatenate([out_w[3 * i + j] for j in range(3)], axis=1)
        total = total + lax.dot_general(strips[i], taps, (((1,), (1,)), ((), ())), preferred_element_type=F32)
    grad = total.astype(BF16)
    lower = lax.broadcasted_iota(jnp.int32, (half, 2 * cols), 1)
    lower = jnp.where(lower >= cols, lower - cols, lower)
    pool = jnp.where(lower // 2 == lax.broadcasted_iota(jnp.int32, (half, 2 * cols), 0), 1.0, 0.0).astype(BF16)
    for q in range(rows // 2):
        pair = grad[2 * q * cols : (2 * q + 2) * cols]
        grad_top[q] = jnp.dot(pool, pair, preferred_element_type=F32).astype(BF16)
    put(9 * channels, jnp.dot(jnp.transpose(feat[...]), grad, preferred_element_type=F32))


def forward_kernel(peers, merged, out_w, *refs):
    edges, (out, stack, near, sem) = refs[:-4], refs[-4:]
    rows, cols, channels = merged.shape
    for r in range(rows):
        put_shifted(stack, r + 1, merged[r], -1)
    if len(edges) == 1:
        start = edges[0].shape[0] - 2 * cols
        edge = jnp.concatenate([edges[0][start : start + cols, :], edges[0][start + cols :, :]], axis=1)
        put_halo(stack, edge, edge, rows, peers, -1)
    else:
        put_halo(stack, edges[0][...], edges[1][...], rows, peers, -1)
    total = jnp.zeros((rows * cols, channels), F32)
    for i in range(3):
        strip = stack[i : i + rows].reshape(rows * cols, 3 * channels)
        taps = out_w[3 * i : 3 * i + 3].reshape(3 * channels, channels)
        total = total + jnp.dot(strip, taps, preferred_element_type=F32)
    near[...] = total.astype(BF16).reshape(out.shape)
    copy = pltpu.make_async_copy(near, out, sem)
    copy.start()
    copy.wait()


def place_kernel(gathered, kernel_out, lateral_out, sems):
    edge, share = kernel_out.shape[0], gathered.shape[1]
    copies = []
    for device in range(gathered.shape[0]):
        chip, core = device // 2, device % 2
        index = 4 * (chip % 4) + chip // 4 if core == 0 else chip
        lanes = pl.ds(core * 128, 128)
        start, stop = index * share, (index + 1) * share
        if start < edge:
            size = min(stop, edge) - start
            copies.append((gathered.at[device, pl.ds(0, size), :], kernel_out.at[pl.ds(start, size), lanes]))
        if stop > edge:
            skip = max(edge - start, 0)
            rows = pl.ds(start + skip - edge, share - skip)
            copies.append((gathered.at[device, pl.ds(skip, share - skip), :], lateral_out.at[rows, lanes]))
    copies = [pltpu.make_async_copy(source, to, sems.at[i]) for i, (source, to) in enumerate(copies)]
    for copy in copies:
        copy.start()
    for copy in copies:
        copy.wait()


def peer_groups():
    plane = [[4 * z + q for q in range(4)] for z in range(4)]
    line = [[4 * z + q for z in range(4)] for q in range(4)]
    pick = lambda chips, core: [[2 * chip + core for chip in group] for group in chips]
    return pick(plane, 0) + pick(line, 1), pick(line, 0) + pick(plane, 1)


def swap_pieces(pieces, groups):
    return lax.all_to_all(pieces, ("dp", "space"), 0, 0, axis_index_groups=groups, tiled=True)


def sum_everywhere(mine, got, scale, edge):
    length, width = mine.shape
    first, second = peer_groups()
    pair = (mine + got[:length].astype(F32)).astype(BF16).reshape(4, length // 4, width)
    total = jnp.sum(swap_pieces(pair, first).astype(F32), axis=0).astype(BF16).reshape(4, length // 16, width)
    total = (jnp.sum(swap_pieces(total, second).astype(F32), axis=0) * scale).astype(BF16)
    gathered = pltpu.with_memory_space_constraint(lax.all_gather(total, ("dp", "space")), pltpu.HBM)
    return pl.pallas_call(
        place_kernel,
        out_shape=[jax.ShapeDtypeStruct((rows, 2 * width), BF16) for rows in (edge, length - edge)],
        in_specs=[pl.BlockSpec(memory_space=pltpu.HBM)],
        out_specs=[pl.BlockSpec(memory_space=pltpu.HBM)] * 2,
        scratch_shapes=[pltpu.SemaphoreType.DMA((34,))],
        compiler_params=pltpu.CompilerParams(vmem_limit_bytes=8 * 2**20),
    )(gathered)


def local(features, top_down, lateral_weight, out_kernel, cotangent):
    images, rows, cols, in_channels = features.shape
    channels = lateral_weight.shape[1]
    cells = rows * cols
    peers = lax.axis_size("space")
    length = 9 * channels + in_channels
    taps = out_kernel.reshape(9, channels, channels)
    params = pltpu.CompilerParams(vmem_limit_bytes=32 * 2**20)
    halves = peers == 2 and lax.axis_size("dp") == 16 and images == 1 and (channels, in_channels) == (256, 512)
    if halves:
        sums = [
            jax.ShapeDtypeStruct((length, channels // 2), F32),
            jax.ShapeDtypeStruct((length + 2 * cols, channels // 2), BF16),
        ]
    else:
        sums = [jax.ShapeDtypeStruct((length, channels), F32)]
    outs, tops, parts = [], [], None
    for image in range(images):
        cot = cotangent[image]
        cot_before, cot_after = neighbour_rows(cot)
        arrays = (cot, lateral_weight, top_down[image], features[image].reshape(cells, in_channels), taps)
        arrays = [pltpu.with_memory_space_constraint(array, pltpu.HBM) for array in arrays]
        merged, merged_t, stack = pl.pallas_call(
            merge_kernel,
            out_shape=[
                jax.ShapeDtypeStruct(shape, BF16)
                for shape in ((cells, channels), (channels, cells), (rows, cols, 3 * channels))
            ],
            in_specs=[pl.BlockSpec(memory_space=pltpu.HBM)] * 4,
            scratch_shapes=[*[pltpu.VMEM(array.shape, BF16) for array in arrays[:4]], pltpu.SemaphoreType.DMA((4,))],
            compiler_params=params,
            cost_estimate=pl.CostEstimate(
                flops=2 * cells * channels * 4 * in_channels, bytes_accessed=4 * 2**20, transcendentals=0
            ),
        )(*arrays[:4])
        grad_top, *part = pl.pallas_call(
            functools.partial(grads_kernel, peers, halves),
            out_shape=[jax.ShapeDtypeStruct((rows // 2, cols // 2, channels), BF16), *sums],
            in_specs=[pl.BlockSpec(memory_space=pltpu.VMEM)] * 5 + [pl.BlockSpec(memory_space=pltpu.HBM)] * 2,
            scratch_shapes=[
                pltpu.VMEM((2, cols, 3 * channels), BF16),
                *[pltpu.VMEM(array.shape, BF16) for array in arrays[3:]],
                pltpu.SemaphoreType.DMA((2,)),
            ],
            compiler_params=params,
            cost_estimate=pl.CostEstimate(
                flops=2 * cells * channels * (18 * channels + in_channels), bytes_accessed=6 * 2**20, transcendentals=0
            ),
        )(stack, merged, merged_t, cot_before, cot_after, *arrays[3:])
        merged = merged.reshape(rows, cols, channels)
        if halves:
            part[1] = lax.ppermute(part[1], "space", [(0, 1), (1, 0)])
        edges = (part[1],) if halves else neighbour_rows(merged)
        outs.append(
            pl.pallas_call(
                functools.partial(forward_kernel, peers),
                out_shape=jax.ShapeDtypeStruct((rows, cols, channels), BF16),
                out_specs=pl.BlockSpec(memory_space=pltpu.HBM),
                scratch_shapes=[
                    pltpu.VMEM((rows + 2, cols, 3 * channels), BF16),
                    pltpu.VMEM((rows, cols, channels), BF16),
                    pltpu.SemaphoreType.DMA,
                ],
                compiler_params=params,
                cost_estimate=pl.CostEstimate(
                    flops=2 * cells * channels * 9 * channels, bytes_accessed=2 * 2**20, transcendentals=0
                ),
            )(merged, taps, *edges)
        )
        tops.append(grad_top)
        parts = part if parts is None else [a + b for a, b in zip(parts, part)]
    scale = 1.0 / (images * lax.axis_size("dp"))
    if halves:
        grad_kernel, grad_lateral = sum_everywhere(*parts, scale, 9 * channels)
    else:
        total = (lax.psum(parts[0], ("dp", "space")) * scale).astype(BF16)
        grad_kernel, grad_lateral = total[: 9 * channels], total[9 * channels :]
    return jnp.stack(outs), jnp.stack(tops), grad_kernel.reshape(out_kernel.shape), grad_lateral


def solution(mesh):
    return jax.shard_map(
        local,
        mesh=mesh,
        in_specs=(
            P("dp", "space", None, None),
            P("dp", "space", None, None),
            P(),
            P(),
            P("dp", "space", None, None),
        ),
        out_specs=(P("dp", "space", None, None), P("dp", "space", None, None), P(), P()),
        check_vma=False,
    )
```

```python
import functools

import jax
import jax.numpy as jnp
from jax import lax
from jax.experimental import pallas as pl
from jax.experimental.pallas import tpu as pltpu
from jax.sharding import PartitionSpec as P

F32 = jnp.float32
BF16 = jnp.bfloat16


def neighbour_rows(array):
    peers = lax.axis_size("space")
    rows = array.shape[0]
    if peers == 1:
        return array[0], array[0]
    if peers == 2:
        here = lax.axis_index("space")
        edge = lax.dynamic_index_in_dim(array, (1 - here) * (rows - 1), 0, keepdims=False)
        got = lax.ppermute(edge, "space", [(0, 1), (1, 0)])
        return got, got
    up = [(i, i + 1) for i in range(peers - 1)]
    down = [(j, i) for i, j in up]
    return lax.ppermute(array[-1], "space", up), lax.ppermute(array[0], "space", down)


def put_shifted(stack, slot, row, sign):
    cols, channels = row.shape
    wide = row.astype(F32)
    place = lax.broadcasted_iota(jnp.int32, (cols, channels), 0)
    later = jnp.where(place == cols - 1, 0.0, pltpu.roll(wide, cols - 1, 0)).astype(BF16)
    earlier = jnp.where(place == 0, 0.0, pltpu.roll(wide, 1, 0)).astype(BF16)
    first, last = (earlier, later) if sign < 0 else (later, earlier)
    stack[slot, :, 0:channels] = first
    stack[slot, :, channels : 2 * channels] = row
    stack[slot, :, 2 * channels :] = last


def put_halo(stack, before, after, rows, peers, sign):
    here = lax.axis_index("space")
    zero = jnp.zeros(before.shape, BF16)
    put_shifted(stack, 0, jnp.where(here > 0, before, zero), sign)
    put_shifted(stack, rows + 1, jnp.where(here < peers - 1, after, zero), sign)


def merge_kernel(*refs):
    far, (merged, merged_t, stack), near, sems = refs[:4], refs[4:7], refs[7:11], refs[11]
    copies = [pltpu.make_async_copy(a, b, sems.at[i]) for i, (a, b) in enumerate(zip(far, near))]
    for copy in copies:
        copy.start()
    cot, lat_w, top, feat = near
    rows, cols, channels = cot.shape
    half = cols // 2
    copies[0].wait()
    for r in range(rows):
        put_shifted(stack, r, cot[r], 1)
    for copy in copies[1:]:
        copy.wait()
    upper = lax.broadcasted_iota(jnp.int32, (cols, half), 0)
    spread = jnp.where(upper // 2 == lax.broadcasted_iota(jnp.int32, (cols, half), 1), 1.0, 0.0).astype(BF16)
    lateral = jnp.dot(feat[...], lat_w[...], preferred_element_type=F32)
    for q in range(rows // 2):
        lifted = jnp.dot(spread, top[q], preferred_element_type=F32)
        for r in (2 * q, 2 * q + 1):
            merged[r * cols : (r + 1) * cols, :] = (lateral[r * cols : (r + 1) * cols] + lifted).astype(BF16)
    merged_t[...] = jnp.transpose(merged[...])


def strips_of(stack, halo):
    rows, cols, deep = stack.shape
    strips = [
        jnp.concatenate([stack[1:], halo[1:]], axis=0),
        stack[...],
        jnp.concatenate([halo[:1], stack[: rows - 1]], axis=0),
    ]
    return [strip.reshape(rows * cols, deep) for strip in strips]


def put_sums(outs, start, values):
    rows = slice(start, start + values.shape[0])
    if len(outs) == 1:
        outs[0][rows, :] = values
        return
    here = lax.axis_index("space")
    half = values.shape[1] // 2
    mine, theirs = outs
    mine[rows, :] = jnp.where(here == 0, values[:, :half], values[:, half:])
    theirs[rows, :] = jnp.where(here == 0, values[:, half:], values[:, :half]).astype(BF16)


def kernel_grad_kernel(peers, stack, merged, merged_t, before, after, halo, *outs):
    cols = stack.shape[1]
    channels, cells = merged_t.shape
    put_halo(halo, before[...], after[...], 0, peers, 1)
    if len(outs) == 2:
        here = lax.axis_index("space")
        edge = jnp.where(here == 0, merged[cells - cols :, :], merged[:cols, :])
        start = 9 * channels
        outs[1][start : start + cols, :] = edge[:, : channels // 2]
        outs[1][start + cols :, :] = edge[:, channels // 2 :]
    for i, strip in enumerate(strips_of(stack, halo)):
        part = jnp.dot(merged_t[...], strip, preferred_element_type=F32)
        for j in range(3):
            put_sums(outs, (3 * i + j) * channels, part[:, j * channels : (j + 1) * channels])


def data_grad_kernel(stack, halo, feat_far, taps_far, grad_top, *rest):
    outs, feat, out_w, sems = rest[:-3], *rest[-3:]
    copies = [pltpu.make_async_copy(taps_far, out_w, sems.at[0]), pltpu.make_async_copy(feat_far, feat, sems.at[1])]
    for copy in copies:
        copy.start()
    rows, cols, deep = stack.shape
    cells, channels, half = rows * cols, deep // 3, cols // 2
    strips = strips_of(stack, halo)
    copies[0].wait()
    total = jnp.zeros((cells, channels), F32)
    for i in range(3):
        taps = jnp.concatenate([out_w[3 * i + j] for j in range(3)], axis=1)
        total = total + lax.dot_general(strips[i], taps, (((1,), (1,)), ((), ())), preferred_element_type=F32)
    grad = total.astype(BF16)
    copies[1].wait()
    put_sums(outs, 0, jnp.dot(jnp.transpose(feat[...]), grad, preferred_element_type=F32))
    lower = lax.broadcasted_iota(jnp.int32, (half, 2 * cols), 1)
    lower = jnp.where(lower >= cols, lower - cols, lower)
    pool = jnp.where(lower // 2 == lax.broadcasted_iota(jnp.int32, (half, 2 * cols), 0), 1.0, 0.0).astype(BF16)
    for q in range(rows // 2):
        pair = grad[2 * q * cols : (2 * q + 2) * cols]
        grad_top[q] = jnp.dot(pool, pair, preferred_element_type=F32).astype(BF16)


def forward_kernel(peers, merged, out_w, *refs):
    edges, (out, stack, near, sem) = refs[:-4], refs[-4:]
    rows, cols, channels = merged.shape
    for r in range(rows):
        put_shifted(stack, r + 1, merged[r], -1)
    if len(edges) == 1:
        start = edges[0].shape[0] - 2 * cols
        edge = jnp.concatenate([edges[0][start : start + cols, :], edges[0][start + cols :, :]], axis=1)
        put_halo(stack, edge, edge, rows, peers, -1)
    else:
        put_halo(stack, edges[0][...], edges[1][...], rows, peers, -1)
    total = jnp.zeros((rows * cols, channels), F32)
    for i in range(3):
        strip = stack[i : i + rows].reshape(rows * cols, 3 * channels)
        taps = out_w[3 * i : 3 * i + 3].reshape(3 * channels, channels)
        total = total + jnp.dot(strip, taps, preferred_element_type=F32)
    near[...] = total.astype(BF16).reshape(out.shape)
    copy = pltpu.make_async_copy(near, out, sem)
    copy.start()
    copy.wait()


def place_kernel(mine, other, kernel_out, lateral_out, sems):
    side = lax.axis_index("space")
    edge, rest = kernel_out.shape[0], lateral_out.shape[0]
    copies = []
    for columns, half in ((side, mine), (1 - side, other)):
        lanes = pl.ds(pl.multiple_of(columns * 128, 128), 128)
        for start in range(0, edge, rest // 2):
            size = min(rest // 2, edge - start)
            copies.append((half.at[pl.ds(start, size), :], kernel_out.at[pl.ds(start, size), lanes]))
        copies.append((half.at[pl.ds(edge, rest), :], lateral_out.at[:, lanes]))
    copies = [pltpu.make_async_copy(source, to, sems.at[i]) for i, (source, to) in enumerate(copies)]
    for copy in copies:
        copy.start()
    for copy in copies:
        copy.wait()


def peer_groups():
    plane = [[4 * z + q for q in range(4)] for z in range(4)]
    line = [[4 * z + q for z in range(4)] for q in range(4)]
    pick = lambda chips, core: [[2 * chip + core for chip in group] for group in chips]
    return pick(plane, 0) + pick(line, 1), pick(line, 0) + pick(plane, 1)


def swap_pieces(pieces, groups):
    return lax.all_to_all(pieces, ("dp", "space"), 0, 0, axis_index_groups=groups, tiled=True)


def swap(array):
    return lax.ppermute(array, "space", [(0, 1), (1, 0)])


def sum_everywhere(pair, scale, edge):
    length, width = pair.shape
    first, second = peer_groups()
    quarter = (length // 4, width)
    copies = lambda array: jnp.broadcast_to(array[None], (4, *array.shape))
    terms = swap_pieces(pair.reshape(4, *quarter), first)
    terms = swap_pieces(copies(jnp.sum(terms.astype(F32), axis=0).astype(BF16)), second)
    total = (jnp.sum(terms.astype(F32), axis=0) * scale).astype(BF16)
    total = swap_pieces(copies(total), first).reshape(length, width)
    return pl.pallas_call(
        place_kernel,
        out_shape=[jax.ShapeDtypeStruct((rows, 2 * width), BF16) for rows in (edge, length - edge)],
        out_specs=[pl.BlockSpec(memory_space=pltpu.HBM)] * 2,
        scratch_shapes=[pltpu.SemaphoreType.DMA((20,))],
        compiler_params=pltpu.CompilerParams(vmem_limit_bytes=8 * 2**20),
    )(total, swap(total))


def local(features, top_down, lateral_weight, out_kernel, cotangent):
    images, rows, cols, in_channels = features.shape
    channels = lateral_weight.shape[1]
    cells = rows * cols
    peers = lax.axis_size("space")
    taps = out_kernel.reshape(9, channels, channels)
    params = pltpu.CompilerParams(vmem_limit_bytes=32 * 2**20)
    halves = peers == 2 and lax.axis_size("dp") == 16 and images == 1 and (channels, in_channels) == (256, 512)

    def sums(length, extra):
        if not halves:
            return [jax.ShapeDtypeStruct((length, channels), F32)]
        return [
            jax.ShapeDtypeStruct((length, channels // 2), F32),
            jax.ShapeDtypeStruct((length + extra, channels // 2), BF16),
        ]

    outs, tops, parts = [], [], None
    for image in range(images):
        cot = cotangent[image]
        cot_before, cot_after = neighbour_rows(cot)
        arrays = (cot, lateral_weight, top_down[image], features[image].reshape(cells, in_channels), taps)
        arrays = [pltpu.with_memory_space_constraint(array, pltpu.HBM) for array in arrays]
        merged, merged_t, stack = pl.pallas_call(
            merge_kernel,
            out_shape=[
                jax.ShapeDtypeStruct(shape, BF16)
                for shape in ((cells, channels), (channels, cells), (rows, cols, 3 * channels))
            ],
            in_specs=[pl.BlockSpec(memory_space=pltpu.HBM)] * 4,
            scratch_shapes=[*[pltpu.VMEM(array.shape, BF16) for array in arrays[:4]], pltpu.SemaphoreType.DMA((4,))],
            compiler_params=params,
            cost_estimate=pl.CostEstimate(
                flops=2 * cells * channels * 4 * in_channels, bytes_accessed=4 * 2**20, transcendentals=0
            ),
        )(*arrays[:4])
        halo, *kernel_part = pl.pallas_call(
            functools.partial(kernel_grad_kernel, peers),
            out_shape=[jax.ShapeDtypeStruct((2, cols, 3 * channels), BF16), *sums(9 * channels, 2 * cols)],
            compiler_params=params,
            cost_estimate=pl.CostEstimate(
                flops=2 * cells * channels * 9 * channels, bytes_accessed=4 * 2**20, transcendentals=0
            ),
        )(stack, merged, merged_t, cot_before, cot_after)
        if halves:
            kernel_part[1] = swap(kernel_part[1])
        grad_top, *lateral_part = pl.pallas_call(
            data_grad_kernel,
            out_shape=[jax.ShapeDtypeStruct((rows // 2, cols // 2, channels), BF16), *sums(in_channels, 0)],
            in_specs=[pl.BlockSpec(memory_space=pltpu.VMEM)] * 2 + [pl.BlockSpec(memory_space=pltpu.HBM)] * 2,
            scratch_shapes=[
                *[pltpu.VMEM(array.shape, BF16) for array in arrays[3:]],
                pltpu.SemaphoreType.DMA((2,)),
            ],
            compiler_params=params,
            cost_estimate=pl.CostEstimate(
                flops=2 * cells * channels * (9 * channels + in_channels), bytes_accessed=4 * 2**20, transcendentals=0
            ),
        )(stack, halo, *arrays[3:])
        if halves:
            lateral_part[1] = swap(lateral_part[1])
        merged = merged.reshape(rows, cols, channels)
        edges = kernel_part[1:] if halves else neighbour_rows(merged)
        outs.append(
            pl.pallas_call(
                functools.partial(forward_kernel, peers),
                out_shape=jax.ShapeDtypeStruct((rows, cols, channels), BF16),
                out_specs=pl.BlockSpec(memory_space=pltpu.HBM),
                scratch_shapes=[
                    pltpu.VMEM((rows + 2, cols, 3 * channels), BF16),
                    pltpu.VMEM((rows, cols, channels), BF16),
                    pltpu.SemaphoreType.DMA,
                ],
                compiler_params=params,
                cost_estimate=pl.CostEstimate(
                    flops=2 * cells * channels * 9 * channels, bytes_accessed=2 * 2**20, transcendentals=0
                ),
            )(merged, taps, *edges)
        )
        tops.append(grad_top)
        if halves:
            parts = [
                (mine + got[: mine.shape[0]].astype(F32)).astype(BF16) for mine, got in (kernel_part, lateral_part)
            ]
        else:
            parts = [kernel_part[0], lateral_part[0]] if parts is None else [
                a + b for a, b in zip(parts, (kernel_part[0], lateral_part[0]))
            ]
    scale = 1.0 / (images * lax.axis_size("dp"))
    if halves:
        grad_kernel, grad_lateral = sum_everywhere(jnp.concatenate(parts), scale, 9 * channels)
    else:
        grad_kernel, grad_lateral = [(total * scale).astype(BF16) for total in lax.psum(parts, ("dp", "space"))]
    return jnp.stack(outs), jnp.stack(tops), grad_kernel.reshape(out_kernel.shape), grad_lateral


def solution(mesh):
    return jax.shard_map(
        local,
        mesh=mesh,
        in_specs=(
            P("dp", "space", None, None),
            P("dp", "space", None, None),
            P(),
            P(),
            P("dp", "space", None, None),
        ),
        out_specs=(P("dp", "space", None, None), P("dp", "space", None, None), P(), P()),
        check_vma=False,
    )
```

```python
import functools

import jax
import jax.numpy as jnp
from jax import lax
from jax.experimental import pallas as pl
from jax.experimental.pallas import tpu as pltpu
from jax.sharding import PartitionSpec as P

F32 = jnp.float32
BF16 = jnp.bfloat16


def neighbour_rows(array):
    peers = lax.axis_size("space")
    rows = array.shape[0]
    if peers == 1:
        return array[0], array[0]
    if peers == 2:
        here = lax.axis_index("space")
        edge = lax.dynamic_index_in_dim(array, (1 - here) * (rows - 1), 0, keepdims=False)
        got = lax.ppermute(edge, "space", [(0, 1), (1, 0)])
        return got, got
    up = [(i, i + 1) for i in range(peers - 1)]
    down = [(j, i) for i, j in up]
    return lax.ppermute(array[-1], "space", up), lax.ppermute(array[0], "space", down)


def put_shifted(stack, slot, row, sign):
    cols, channels = row.shape
    wide = row.astype(F32)
    place = lax.broadcasted_iota(jnp.int32, (cols, channels), 0)
    later = jnp.where(place == cols - 1, 0.0, pltpu.roll(wide, cols - 1, 0)).astype(BF16)
    earlier = jnp.where(place == 0, 0.0, pltpu.roll(wide, 1, 0)).astype(BF16)
    first, last = (earlier, later) if sign < 0 else (later, earlier)
    stack[slot, :, 0:channels] = first
    stack[slot, :, channels : 2 * channels] = row
    stack[slot, :, 2 * channels :] = last


def put_halo(stack, before, after, rows, peers, sign):
    here = lax.axis_index("space")
    zero = jnp.zeros(before.shape, BF16)
    put_shifted(stack, 0, jnp.where(here > 0, before, zero), sign)
    put_shifted(stack, rows + 1, jnp.where(here < peers - 1, after, zero), sign)


def merge_kernel(*refs):
    far, (merged, merged_t, stack, feat_t, out_w), near, sems = refs[:5], refs[5:10], refs[10:14], refs[14]
    near = (*near, out_w)
    copies = [pltpu.make_async_copy(a, b, sems.at[i]) for i, (a, b) in enumerate(zip(far, near))]
    for copy in copies:
        copy.start()
    cot, lat_w, top, feat, _ = near
    rows, cols, channels = cot.shape
    half = cols // 2
    copies[0].wait()
    for r in range(rows):
        put_shifted(stack, r, cot[r], 1)
    for copy in copies[1:4]:
        copy.wait()
    upper = lax.broadcasted_iota(jnp.int32, (cols, half), 0)
    spread = jnp.where(upper // 2 == lax.broadcasted_iota(jnp.int32, (cols, half), 1), 1.0, 0.0).astype(BF16)
    lateral = jnp.dot(feat[...], lat_w[...], preferred_element_type=F32)
    for q in range(rows // 2):
        lifted = jnp.dot(spread, top[q], preferred_element_type=F32)
        for r in (2 * q, 2 * q + 1):
            merged[r * cols : (r + 1) * cols, :] = (lateral[r * cols : (r + 1) * cols] + lifted).astype(BF16)
    merged_t[...] = jnp.transpose(merged[...])
    feat_t[...] = jnp.transpose(feat[...])
    copies[4].wait()


def strips_of(stack, halo):
    rows, cols, deep = stack.shape
    strips = [
        jnp.concatenate([stack[1:], halo[1:]], axis=0),
        stack[...],
        jnp.concatenate([halo[:1], stack[: rows - 1]], axis=0),
    ]
    return [strip.reshape(rows * cols, deep) for strip in strips]


def put_sums(outs, start, values):
    rows = slice(start, start + values.shape[0])
    if len(outs) == 1:
        outs[0][rows, :] = values
        return
    here = lax.axis_index("space")
    half = values.shape[1] // 2
    mine, theirs = outs
    mine[rows, :] = jnp.where(here == 0, values[:, :half], values[:, half:])
    theirs[rows, :] = jnp.where(here == 0, values[:, half:], values[:, :half]).astype(BF16)


def kernel_grad_kernel(peers, stack, merged, merged_t, before, after, halo, *outs):
    cols = stack.shape[1]
    channels, cells = merged_t.shape
    put_halo(halo, before[...], after[...], 0, peers, 1)
    if len(outs) == 2:
        here = lax.axis_index("space")
        edge = jnp.where(here == 0, merged[cells - cols :, :], merged[:cols, :])
        start = 9 * channels
        outs[1][start : start + cols, :] = edge[:, : channels // 2]
        outs[1][start + cols :, :] = edge[:, channels // 2 :]
    for i, strip in enumerate(strips_of(stack, halo)):
        part = jnp.dot(merged_t[...], strip, preferred_element_type=F32)
        for j in range(3):
            put_sums(outs, (3 * i + j) * channels, part[:, j * channels : (j + 1) * channels])


def data_grad_kernel(stack, halo, feat_t, out_w, grad_top, *outs):
    rows, cols, deep = stack.shape
    channels, half = deep // 3, cols // 2
    cells = jnp.concatenate(strips_of(stack, halo), axis=1)
    taps = jnp.concatenate([out_w[tap] for tap in range(9)], axis=1)
    total = lax.dot_general(cells, taps, (((1,), (1,)), ((), ())), preferred_element_type=F32)
    grad = total.astype(BF16)
    put_sums(outs, 0, jnp.dot(feat_t[...], grad, preferred_element_type=F32))
    lower = lax.broadcasted_iota(jnp.int32, (half, 2 * cols), 1)
    lower = jnp.where(lower >= cols, lower - cols, lower)
    pool = jnp.where(lower // 2 == lax.broadcasted_iota(jnp.int32, (half, 2 * cols), 0), 1.0, 0.0).astype(BF16)
    for q in range(rows // 2):
        pair = grad[2 * q * cols : (2 * q + 2) * cols]
        grad_top[q] = jnp.dot(pool, pair, preferred_element_type=F32).astype(BF16)


def forward_kernel(peers, merged, out_w, *refs):
    edges, (out, stack, near, sem) = refs[:-4], refs[-4:]
    rows, cols, channels = merged.shape
    for r in range(rows):
        put_shifted(stack, r + 1, merged[r], -1)
    if len(edges) == 1:
        start = edges[0].shape[0] - 2 * cols
        edge = jnp.concatenate([edges[0][start : start + cols, :], edges[0][start + cols :, :]], axis=1)
        put_halo(stack, edge, edge, rows, peers, -1)
    else:
        put_halo(stack, edges[0][...], edges[1][...], rows, peers, -1)
    cells = jnp.concatenate([stack[i : i + rows].reshape(rows * cols, 3 * channels) for i in range(3)], axis=1)
    total = jnp.dot(cells, out_w[...].reshape(9 * channels, channels), preferred_element_type=F32)
    near[...] = total.astype(BF16).reshape(out.shape)
    copy = pltpu.make_async_copy(near, out, sem)
    copy.start()
    copy.wait()


def places():
    chip, core = lax.axis_index("dp"), lax.axis_index("space")
    plane, line = chip % 4, chip // 4
    return jnp.where(core == 0, plane, line), jnp.where(core == 0, line, plane)


def block(index, length):
    return pl.ds(pl.multiple_of(index * length, 16), length)


def cut_kernel(mine_a, got_a, mine_b, got_b, *refs):
    outs, total = refs[:4], refs[4]
    start = 0
    for mine, got in ((mine_a, got_a), (mine_b, got_b)):
        rows = mine.shape[0]
        total[start : start + rows, :] = mine[...] + got[:rows, :].astype(F32)
        start += rows
    place, _ = places()
    for k, out in enumerate(outs):
        out[...] = total[block(place ^ k, out.shape[0]), :].astype(out.dtype)


def add_kernel(own, one, two, three, *refs):
    refs[-1][...] = (own[...] + one[...].astype(F32) + two[...].astype(F32) + three[...].astype(F32)).astype(BF16)


def finish_kernel(scale, own, one, two, three, out):
    near = own[...].astype(F32) + one[...].astype(F32)
    far = two[...].astype(F32) + three[...].astype(F32)
    out[...] = ((near + far) * scale).astype(BF16)


def place_kernel(*refs):
    kernel_out, lateral_out, sems = refs[8:]
    side = lax.axis_index("space")
    edge, share = kernel_out.shape[0], refs[0].shape[0]
    inside = edge - 3 * share
    waits = []
    for columns, quarters, place in zip((side, 1 - side), (refs[:4], refs[4:8]), places()):
        lanes = pl.ds(pl.multiple_of(columns * 128, 128), 128)
        for k, quarter in enumerate(quarters):
            index = place ^ k
            base = pl.multiple_of(index * share, 16)
            head, tail = quarter.at[pl.ds(0, inside), :], quarter.at[pl.ds(inside, share - inside), :]
            copy = pltpu.make_async_copy(head, kernel_out.at[pl.ds(base, inside), lanes], sems.at[len(waits)])
            copy.start()
            waits.append(copy)
            sem = sems.at[len(waits)]

            @pl.when(index < 3)
            def _():
                rows = pl.ds(base + inside, share - inside)
                pltpu.make_async_copy(tail, kernel_out.at[rows, lanes], sem).start()

            @pl.when(index == 3)
            def _():
                pltpu.make_async_copy(tail, lateral_out.at[:, lanes], sem).start()

            waits.append(pltpu.make_async_copy(tail, lateral_out.at[:, lanes], sem))
    for copy in waits:
        copy.wait()


def exchange(pieces, step):
    came = {}
    for k in (3, 2, 1):
        pairs = []
        for chip in range(16):
            for core in range(2):
                flip = k if core == step else 4 * k
                pairs.append((2 * chip + core, 2 * (chip ^ flip) + core))
        came[k] = lax.ppermute(pieces[k - 1], ("dp", "space"), pairs)
    return [came[k] for k in (1, 2, 3)]


def swap(array):
    return lax.ppermute(array, "space", [(0, 1), (1, 0)])


def call(kernel, *shapes, **more):
    return pl.pallas_call(
        kernel,
        out_shape=[jax.ShapeDtypeStruct(shape, kind) for shape, kind in shapes],
        compiler_params=pltpu.CompilerParams(vmem_limit_bytes=12 * 2**20),
        **more,
    )


def sum_everywhere(kernel_part, lateral_part, scale, after):
    edge, width = kernel_part[0].shape
    length = edge + lateral_part[0].shape[0]
    quarter = (length // 4, width)
    own, *pieces = call(
        cut_kernel, (quarter, F32), *[(quarter, BF16)] * 3, scratch_shapes=[pltpu.VMEM((length, width), F32)]
    )(*kernel_part, *lateral_part)
    vmem, far = pl.BlockSpec(memory_space=pltpu.VMEM), pl.BlockSpec(memory_space=pltpu.HBM)
    after = pltpu.with_memory_space_constraint(after, pltpu.HBM)
    [total] = call(add_kernel, (quarter, BF16), in_specs=[vmem] * 4 + [far])(own, *exchange(pieces, 0), after)
    [total] = call(functools.partial(finish_kernel, scale), (quarter, BF16))(total, *exchange([total] * 3, 1))
    quarters = [total, *exchange([total] * 3, 0)]
    return call(
        place_kernel,
        ((edge, 2 * width), BF16),
        ((length - edge, 2 * width), BF16),
        out_specs=[far] * 2,
        scratch_shapes=[pltpu.SemaphoreType.DMA((16,))],
    )(*quarters, *[swap(one) for one in quarters])


def local(features, top_down, lateral_weight, out_kernel, cotangent):
    images, rows, cols, in_channels = features.shape
    channels = lateral_weight.shape[1]
    cells = rows * cols
    peers = lax.axis_size("space")
    taps = out_kernel.reshape(9, channels, channels)
    params = pltpu.CompilerParams(vmem_limit_bytes=32 * 2**20)
    halves = peers == 2 and lax.axis_size("dp") == 16 and images == 1 and (channels, in_channels) == (256, 512)

    def sums(length, extra):
        if not halves:
            return [jax.ShapeDtypeStruct((length, channels), F32)]
        return [
            jax.ShapeDtypeStruct((length, channels // 2), F32),
            jax.ShapeDtypeStruct((length + extra, channels // 2), BF16),
        ]

    outs, tops, parts = [], [], None
    for image in range(images):
        cot = cotangent[image]
        cot_before, cot_after = neighbour_rows(cot)
        arrays = (cot, lateral_weight, top_down[image], features[image].reshape(cells, in_channels), taps)
        arrays = [pltpu.with_memory_space_constraint(array, pltpu.HBM) for array in arrays]
        merged, merged_t, stack, feat_t, near_taps = pl.pallas_call(
            merge_kernel,
            out_shape=[
                jax.ShapeDtypeStruct(shape, BF16)
                for shape in (
                    (cells, channels),
                    (channels, cells),
                    (rows, cols, 3 * channels),
                    (in_channels, cells),
                    taps.shape,
                )
            ],
            in_specs=[pl.BlockSpec(memory_space=pltpu.HBM)] * 5,
            scratch_shapes=[*[pltpu.VMEM(array.shape, BF16) for array in arrays[:4]], pltpu.SemaphoreType.DMA((5,))],
            compiler_params=params,
            cost_estimate=pl.CostEstimate(
                flops=2 * cells * channels * 4 * in_channels, bytes_accessed=4 * 2**20, transcendentals=0
            ),
        )(*arrays)
        halo, *kernel_part = pl.pallas_call(
            functools.partial(kernel_grad_kernel, peers),
            out_shape=[jax.ShapeDtypeStruct((2, cols, 3 * channels), BF16), *sums(9 * channels, 2 * cols)],
            compiler_params=params,
            cost_estimate=pl.CostEstimate(
                flops=2 * cells * channels * 9 * channels, bytes_accessed=4 * 2**20, transcendentals=0
            ),
        )(stack, merged, merged_t, cot_before, cot_after)
        if halves:
            kernel_part[1] = swap(kernel_part[1])
        grad_top, *lateral_part = pl.pallas_call(
            data_grad_kernel,
            out_shape=[jax.ShapeDtypeStruct((rows // 2, cols // 2, channels), BF16), *sums(in_channels, 0)],
            compiler_params=params,
            cost_estimate=pl.CostEstimate(
                flops=2 * cells * channels * (9 * channels + in_channels), bytes_accessed=4 * 2**20, transcendentals=0
            ),
        )(stack, halo, feat_t, near_taps)
        if halves:
            lateral_part[1] = swap(lateral_part[1])
        merged = merged.reshape(rows, cols, channels)
        edges = kernel_part[1:] if halves else neighbour_rows(merged)
        outs.append(
            pl.pallas_call(
                functools.partial(forward_kernel, peers),
                out_shape=jax.ShapeDtypeStruct((rows, cols, channels), BF16),
                out_specs=pl.BlockSpec(memory_space=pltpu.HBM),
                scratch_shapes=[
                    pltpu.VMEM((rows + 2, cols, 3 * channels), BF16),
                    pltpu.VMEM((rows, cols, channels), BF16),
                    pltpu.SemaphoreType.DMA,
                ],
                compiler_params=params,
                cost_estimate=pl.CostEstimate(
                    flops=2 * cells * channels * 9 * channels, bytes_accessed=2 * 2**20, transcendentals=0
                ),
            )(merged, near_taps, *edges)
        )
        tops.append(grad_top)
        if not halves:
            part = [kernel_part[0], lateral_part[0]]
            parts = part if parts is None else [a + b for a, b in zip(parts, part)]
    scale = 1.0 / (images * lax.axis_size("dp"))
    if halves:
        grad_kernel, grad_lateral = sum_everywhere(kernel_part, lateral_part, scale, outs[0])
    else:
        grad_kernel, grad_lateral = [(total * scale).astype(BF16) for total in lax.psum(parts, ("dp", "space"))]
    return jnp.stack(outs), jnp.stack(tops), grad_kernel.reshape(out_kernel.shape), grad_lateral


def solution(mesh):
    return jax.shard_map(
        local,
        mesh=mesh,
        in_specs=(
            P("dp", "space", None, None),
            P("dp", "space", None, None),
            P(),
            P(),
            P("dp", "space", None, None),
        ),
        out_specs=(P("dp", "space", None, None), P("dp", "space", None, None), P(), P()),
        check_vma=False,
    )
```

```python
import functools

import jax
import jax.numpy as jnp
from jax import lax
from jax.experimental import pallas as pl
from jax.experimental.pallas import tpu as pltpu
from jax.sharding import PartitionSpec as P

F32 = jnp.float32
BF16 = jnp.bfloat16


def neighbour_rows(array):
    peers = lax.axis_size("space")
    rows = array.shape[0]
    if peers == 1:
        return array[0], array[0]
    if peers == 2:
        here = lax.axis_index("space")
        edge = lax.dynamic_index_in_dim(array, (1 - here) * (rows - 1), 0, keepdims=False)
        got = lax.ppermute(edge, "space", [(0, 1), (1, 0)])
        return got, got
    up = [(i, i + 1) for i in range(peers - 1)]
    down = [(j, i) for i, j in up]
    return lax.ppermute(array[-1], "space", up), lax.ppermute(array[0], "space", down)


def put_shifted(stack, slot, row, sign):
    cols, channels = row.shape
    wide = row.astype(F32)
    place = lax.broadcasted_iota(jnp.int32, (cols, channels), 0)
    later = jnp.where(place == cols - 1, 0.0, pltpu.roll(wide, cols - 1, 0)).astype(BF16)
    earlier = jnp.where(place == 0, 0.0, pltpu.roll(wide, 1, 0)).astype(BF16)
    first, last = (earlier, later) if sign < 0 else (later, earlier)
    stack[slot, :, 0:channels] = first
    stack[slot, :, channels : 2 * channels] = row
    stack[slot, :, 2 * channels :] = last


def put_halo(stack, before, after, rows, peers, sign):
    here = lax.axis_index("space")
    zero = jnp.zeros(before.shape, BF16)
    put_shifted(stack, 0, jnp.where(here > 0, before, zero), sign)
    put_shifted(stack, rows + 1, jnp.where(here < peers - 1, after, zero), sign)


def merge_kernel(*refs):
    far, (merged, merged_t, stack, feat, out_w), near, sems = refs[:5], refs[5:10], refs[10:13], refs[13]
    near = (*near, feat, out_w)
    copies = [pltpu.make_async_copy(a, b, sems.at[i]) for i, (a, b) in enumerate(zip(far, near))]
    for copy in copies:
        copy.start()
    cot, lat_w, top = near[:3]
    rows, cols, channels = cot.shape
    half = cols // 2
    copies[0].wait()
    for r in range(rows):
        put_shifted(stack, r, cot[r], 1)
    for copy in copies[1:4]:
        copy.wait()
    upper = lax.broadcasted_iota(jnp.int32, (cols, half), 0)
    spread = jnp.where(upper // 2 == lax.broadcasted_iota(jnp.int32, (cols, half), 1), 1.0, 0.0).astype(BF16)
    lateral = jnp.dot(feat[...], lat_w[...], preferred_element_type=F32)
    for q in range(rows // 2):
        lifted = jnp.dot(spread, top[q], preferred_element_type=F32)
        for r in (2 * q, 2 * q + 1):
            merged[r * cols : (r + 1) * cols, :] = (lateral[r * cols : (r + 1) * cols] + lifted).astype(BF16)
    merged_t[...] = jnp.transpose(merged[...])
    copies[4].wait()


def strips_of(stack, halo):
    rows, cols, deep = stack.shape
    strips = [
        jnp.concatenate([stack[1:], halo[1:]], axis=0),
        stack[...],
        jnp.concatenate([halo[:1], stack[: rows - 1]], axis=0),
    ]
    return [strip.reshape(rows * cols, deep) for strip in strips]


def put_sums(outs, start, values):
    rows = slice(start, start + values.shape[0])
    if len(outs) == 1:
        outs[0][rows, :] = values
        return
    here = lax.axis_index("space")
    half = values.shape[1] // 2
    mine, theirs = outs
    mine[rows, :] = jnp.where(here == 0, values[:, :half], values[:, half:])
    theirs[rows, :] = jnp.where(here == 0, values[:, half:], values[:, :half]).astype(BF16)


def kernel_grad_kernel(peers, stack, merged, merged_t, before, after, halo, *outs):
    cols = stack.shape[1]
    channels, cells = merged_t.shape
    put_halo(halo, before[...], after[...], 0, peers, 1)
    if len(outs) == 2:
        here = lax.axis_index("space")
        edge = jnp.where(here == 0, merged[cells - cols :, :], merged[:cols, :])
        start = 9 * channels
        outs[1][start : start + cols, :] = edge[:, : channels // 2]
        outs[1][start + cols :, :] = edge[:, channels // 2 :]
    for i, strip in enumerate(strips_of(stack, halo)):
        part = jnp.dot(merged_t[...], strip, preferred_element_type=F32)
        for j in range(3):
            put_sums(outs, (3 * i + j) * channels, part[:, j * channels : (j + 1) * channels])


def data_grad_kernel(stack, halo, feat, out_w, grad, *outs):
    cells = jnp.concatenate(strips_of(stack, halo), axis=1)
    taps = jnp.concatenate([out_w[tap] for tap in range(9)], axis=1)
    total = lax.dot_general(cells, taps, (((1,), (1,)), ((), ())), preferred_element_type=F32)
    grad[...] = total.astype(BF16)
    put_sums(outs, 0, jnp.dot(jnp.transpose(feat[...]), grad[...], preferred_element_type=F32))


def forward_kernel(peers, merged, out_w, grad, *refs):
    edges, (out, grad_top, stack, near, sem) = refs[:-5], refs[-5:]
    rows, cols, channels = merged.shape
    half = cols // 2
    for r in range(rows):
        put_shifted(stack, r + 1, merged[r], -1)
    if len(edges) == 1:
        start = edges[0].shape[0] - 2 * cols
        edge = jnp.concatenate([edges[0][start : start + cols, :], edges[0][start + cols :, :]], axis=1)
        put_halo(stack, edge, edge, rows, peers, -1)
    else:
        put_halo(stack, edges[0][...], edges[1][...], rows, peers, -1)
    cells = jnp.concatenate([stack[i : i + rows].reshape(rows * cols, 3 * channels) for i in range(3)], axis=1)
    total = jnp.dot(cells, out_w[...].reshape(9 * channels, channels), preferred_element_type=F32)
    near[...] = total.astype(BF16).reshape(out.shape)
    copy = pltpu.make_async_copy(near, out, sem)
    copy.start()
    lower = lax.broadcasted_iota(jnp.int32, (half, 2 * cols), 1)
    lower = jnp.where(lower >= cols, lower - cols, lower)
    pool = jnp.where(lower // 2 == lax.broadcasted_iota(jnp.int32, (half, 2 * cols), 0), 1.0, 0.0).astype(BF16)
    for q in range(rows // 2):
        pair = grad[2 * q * cols : (2 * q + 2) * cols, :]
        grad_top[q] = jnp.dot(pool, pair, preferred_element_type=F32).astype(BF16)
    copy.wait()


def places():
    chip, core = lax.axis_index("dp"), lax.axis_index("space")
    plane, line = chip % 4, chip // 4
    return jnp.where(core == 0, plane, line), jnp.where(core == 0, line, plane)


def block(index, length):
    return pl.ds(pl.multiple_of(index * length, 16), length)


def cut_kernel(mine, got, *refs):
    place, _ = places()
    for k, out in zip((0, 3, 2, 1), refs):
        rows = block(place ^ k, out.shape[0])
        out[...] = (mine[rows, :] + got[rows, :].astype(F32)).astype(out.dtype)


def add_kernel(own_a, own_b, three_a, two_a, one_a, one_b, two_b, three_b, out):
    start = 0
    for own, one, two, three in ((own_a, one_a, two_a, three_a), (own_b, one_b, two_b, three_b)):
        rows = slice(start, start + own.shape[0])
        total = own[...] + one[...].astype(F32) + two[...].astype(F32) + three[...].astype(F32)
        out[rows, :] = total.astype(BF16)
        start += own.shape[0]


def finish_kernel(scale, own, one, two, three, _, out):
    near = own[...].astype(F32) + one[...].astype(F32)
    far = two[...].astype(F32) + three[...].astype(F32)
    out[...] = ((near + far) * scale).astype(BF16)


def place_kernel(*refs):
    results, sems = refs[8:10], refs[10]
    side = lax.axis_index("space")
    copies = []
    for columns, quarters, place in zip((side, 1 - side), (refs[:4], refs[4:8]), places()):
        lanes = pl.ds(pl.multiple_of(columns * 128, 128), 128)
        for k, quarter in enumerate(quarters):
            start = 0
            for result in results:
                share = result.shape[0] // 4
                to = result.at[block(place ^ k, share), lanes]
                copies.append(pltpu.make_async_copy(quarter.at[pl.ds(start, share), :], to, sems.at[len(copies)]))
                start += share
    for copy in copies:
        copy.start()
    for copy in copies:
        copy.wait()


def exchange(array, step, k):
    pairs = []
    for chip in range(16):
        for core in range(2):
            flip = k if core == step else 4 * k
            pairs.append((2 * chip + core, 2 * (chip ^ flip) + core))
    return lax.ppermute(array, ("dp", "space"), pairs)


def swap(array):
    return lax.ppermute(array, "space", [(0, 1), (1, 0)])


def call(kernel, *shapes, **more):
    return pl.pallas_call(
        kernel,
        out_shape=[jax.ShapeDtypeStruct(shape, kind) for shape, kind in shapes],
        compiler_params=pltpu.CompilerParams(vmem_limit_bytes=12 * 2**20),
        **more,
    )


def sum_everywhere(parts, scale, after):
    lengths, width = [mine.shape[0] for mine, _ in parts], parts[0][0].shape[1]
    vmem, far = pl.BlockSpec(memory_space=pltpu.VMEM), pl.BlockSpec(memory_space=pltpu.HBM)
    after = pltpu.with_memory_space_constraint(after, pltpu.HBM)
    share_a, share_b, quarter = [(length // 4, width) for length in (*lengths, sum(lengths))]
    own_a, *pieces = call(cut_kernel, (share_a, F32), *[(share_a, BF16)] * 3)(*parts[0])
    three_a, two_a, one_a = [exchange(piece, 0, k) for piece, k in zip(pieces, (3, 2, 1))]
    own_b, *pieces = call(cut_kernel, (share_b, F32), *[(share_b, BF16)] * 3)(*parts[1])
    three_b, two_b, one_b = [exchange(piece, 0, k) for piece, k in zip(pieces, (3, 2, 1))]
    [total] = call(add_kernel, (quarter, BF16))(own_a, own_b, three_a, two_a, one_a, one_b, two_b, three_b)
    three, two, one = [exchange(total, 1, k) for k in (3, 2, 1)]
    finish = call(functools.partial(finish_kernel, scale), (quarter, BF16), in_specs=[vmem] * 4 + [far])
    [total] = finish(total, one, two, three, after)
    three, two, one = [exchange(total, 0, k) for k in (3, 2, 1)]
    quarters = [total, one, two, three]
    return call(
        place_kernel,
        *[((length, 2 * width), BF16) for length in lengths],
        out_specs=[far] * 2,
        scratch_shapes=[pltpu.SemaphoreType.DMA((16,))],
    )(*quarters, *[swap(one) for one in quarters])


def local(features, top_down, lateral_weight, out_kernel, cotangent):
    images, rows, cols, in_channels = features.shape
    channels = lateral_weight.shape[1]
    cells = rows * cols
    peers = lax.axis_size("space")
    taps = out_kernel.reshape(9, channels, channels)
    params = pltpu.CompilerParams(vmem_limit_bytes=32 * 2**20)
    halves = peers == 2 and lax.axis_size("dp") == 16 and images == 1 and (channels, in_channels) == (256, 512)

    def sums(length, extra):
        if not halves:
            return [jax.ShapeDtypeStruct((length, channels), F32)]
        return [
            jax.ShapeDtypeStruct((length, channels // 2), F32),
            jax.ShapeDtypeStruct((length + extra, channels // 2), BF16),
        ]

    outs, tops, parts = [], [], None
    for image in range(images):
        cot = cotangent[image]
        cot_before, cot_after = neighbour_rows(cot)
        arrays = (cot, lateral_weight, top_down[image], features[image].reshape(cells, in_channels), taps)
        arrays = [pltpu.with_memory_space_constraint(array, pltpu.HBM) for array in arrays]
        merged, merged_t, stack, near_feat, near_taps = pl.pallas_call(
            merge_kernel,
            out_shape=[
                jax.ShapeDtypeStruct(shape, BF16)
                for shape in (
                    (cells, channels),
                    (channels, cells),
                    (rows, cols, 3 * channels),
                    (cells, in_channels),
                    taps.shape,
                )
            ],
            in_specs=[pl.BlockSpec(memory_space=pltpu.HBM)] * 5,
            scratch_shapes=[*[pltpu.VMEM(array.shape, BF16) for array in arrays[:3]], pltpu.SemaphoreType.DMA((5,))],
            compiler_params=params,
            cost_estimate=pl.CostEstimate(
                flops=2 * cells * channels * 4 * in_channels, bytes_accessed=4 * 2**20, transcendentals=0
            ),
        )(*arrays)
        halo, *kernel_part = pl.pallas_call(
            functools.partial(kernel_grad_kernel, peers),
            out_shape=[jax.ShapeDtypeStruct((2, cols, 3 * channels), BF16), *sums(9 * channels, 2 * cols)],
            compiler_params=params,
            cost_estimate=pl.CostEstimate(
                flops=2 * cells * channels * 9 * channels, bytes_accessed=4 * 2**20, transcendentals=0
            ),
        )(stack, merged, merged_t, cot_before, cot_after)
        if halves:
            kernel_part[1] = swap(kernel_part[1])
        grad, *lateral_part = pl.pallas_call(
            data_grad_kernel,
            out_shape=[jax.ShapeDtypeStruct((cells, channels), BF16), *sums(in_channels, 0)],
            compiler_params=params,
            cost_estimate=pl.CostEstimate(
                flops=2 * cells * channels * (9 * channels + in_channels), bytes_accessed=4 * 2**20, transcendentals=0
            ),
        )(stack, halo, near_feat, near_taps)
        if halves:
            lateral_part[1] = swap(lateral_part[1])
        merged = merged.reshape(rows, cols, channels)
        edges = kernel_part[1:] if halves else neighbour_rows(merged)
        out, grad_top = pl.pallas_call(
            functools.partial(forward_kernel, peers),
            out_shape=[
                jax.ShapeDtypeStruct((rows, cols, channels), BF16),
                jax.ShapeDtypeStruct((rows // 2, cols // 2, channels), BF16),
            ],
            out_specs=[pl.BlockSpec(memory_space=pltpu.HBM), pl.BlockSpec(memory_space=pltpu.VMEM)],
            scratch_shapes=[
                pltpu.VMEM((rows + 2, cols, 3 * channels), BF16),
                pltpu.VMEM((rows, cols, channels), BF16),
                pltpu.SemaphoreType.DMA,
            ],
            compiler_params=params,
            cost_estimate=pl.CostEstimate(
                flops=2 * cells * channels * 9 * channels, bytes_accessed=2 * 2**20, transcendentals=0
            ),
        )(merged, near_taps, grad, *edges)
        outs.append(out)
        tops.append(grad_top)
        if not halves:
            part = [kernel_part[0], lateral_part[0]]
            parts = part if parts is None else [a + b for a, b in zip(parts, part)]
    scale = 1.0 / (images * lax.axis_size("dp"))
    if halves:
        grad_kernel, grad_lateral = sum_everywhere((kernel_part, lateral_part), scale, outs[0])
    else:
        grad_kernel, grad_lateral = [(total * scale).astype(BF16) for total in lax.psum(parts, ("dp", "space"))]
    return jnp.stack(outs), jnp.stack(tops), grad_kernel.reshape(out_kernel.shape), grad_lateral


def solution(mesh):
    return jax.shard_map(
        local,
        mesh=mesh,
        in_specs=(
            P("dp", "space", None, None),
            P("dp", "space", None, None),
            P(),
            P(),
            P("dp", "space", None, None),
        ),
        out_specs=(P("dp", "space", None, None), P("dp", "space", None, None), P(), P()),
        check_vma=False,
    )
```

```python
import functools

import jax
import jax.numpy as jnp
from jax import lax
from jax.experimental import pallas as pl
from jax.experimental.pallas import tpu as pltpu
from jax.sharding import PartitionSpec as P

F32 = jnp.float32
BF16 = jnp.bfloat16


def neighbour_rows(array):
    peers = lax.axis_size("space")
    if peers == 1:
        return array[-1:], array[:1]
    if peers == 2:
        got = lax.ppermute(array, "space", [(0, 1), (1, 0)])
        return got, got
    up = [(i, i + 1) for i in range(peers - 1)]
    down = [(j, i) for i, j in up]
    return lax.ppermute(array[-1:], "space", up), lax.ppermute(array[:1], "space", down)


def put_shifted(stack, slot, row, sign):
    cols, channels = row.shape
    wide = row.astype(F32)
    place = lax.broadcasted_iota(jnp.int32, (cols, channels), 0)
    later = jnp.where(place == cols - 1, 0.0, pltpu.roll(wide, cols - 1, 0)).astype(BF16)
    earlier = jnp.where(place == 0, 0.0, pltpu.roll(wide, 1, 0)).astype(BF16)
    first, last = (earlier, later) if sign < 0 else (later, earlier)
    stack[slot, :, 0:channels] = first
    stack[slot, :, channels : 2 * channels] = row
    stack[slot, :, 2 * channels :] = last


def put_halo(stack, before, after, rows, peers, sign):
    here = lax.axis_index("space")
    zero = jnp.zeros(before.shape, BF16)
    put_shifted(stack, 0, jnp.where(here > 0, before, zero), sign)
    put_shifted(stack, rows + 1, jnp.where(here < peers - 1, after, zero), sign)


def merge_kernel(*refs):
    far, (merged, merged_t, stack, feat, out_w), near, sems = refs[:5], refs[5:10], refs[10:13], refs[13]
    near = (*near, feat, out_w)
    copies = [pltpu.make_async_copy(a, b, sems.at[i]) for i, (a, b) in enumerate(zip(far, near))]
    for copy in copies:
        copy.start()
    cot, lat_w, top = near[:3]
    rows, cols, channels = cot.shape
    half = cols // 2
    copies[0].wait()
    for r in range(rows):
        put_shifted(stack, r, cot[r], 1)
    for copy in copies[1:4]:
        copy.wait()
    upper = lax.broadcasted_iota(jnp.int32, (cols, half), 0)
    spread = jnp.where(upper // 2 == lax.broadcasted_iota(jnp.int32, (cols, half), 1), 1.0, 0.0).astype(BF16)
    lateral = jnp.dot(feat[...], lat_w[...], preferred_element_type=F32)
    for q in range(rows // 2):
        lifted = jnp.dot(spread, top[q], preferred_element_type=F32)
        for r in (2 * q, 2 * q + 1):
            merged[r * cols : (r + 1) * cols, :] = (lateral[r * cols : (r + 1) * cols] + lifted).astype(BF16)
    merged_t[...] = jnp.transpose(merged[...])
    copies[4].wait()


def strips_of(stack, halo):
    rows, cols, deep = stack.shape
    strips = [
        jnp.concatenate([stack[1:], halo[1:]], axis=0),
        stack[...],
        jnp.concatenate([halo[:1], stack[: rows - 1]], axis=0),
    ]
    return [strip.reshape(rows * cols, deep) for strip in strips]


def put_sums(outs, start, values):
    rows = slice(start, start + values.shape[0])
    if len(outs) == 1:
        outs[0][rows, :] = values
        return
    here = lax.axis_index("space")
    half = values.shape[1] // 2
    mine, theirs = outs
    mine[rows, :] = jnp.where(here == 0, values[:, :half], values[:, half:])
    theirs[rows, :] = jnp.where(here == 0, values[:, half:], values[:, :half]).astype(BF16)


def kernel_grad_kernel(peers, stack, merged, merged_t, before, after, halo, *outs):
    cols = stack.shape[1]
    channels, cells = merged_t.shape
    put_halo(halo, before[before.shape[0] - 1], after[0], 0, peers, 1)
    if len(outs) == 2:
        here = lax.axis_index("space")
        edge = jnp.where(here == 0, merged[cells - cols :, :], merged[:cols, :])
        start = 9 * channels
        outs[1][start : start + cols, :] = edge[:, : channels // 2]
        outs[1][start + cols :, :] = edge[:, channels // 2 :]
    for i, strip in enumerate(strips_of(stack, halo)):
        part = jnp.dot(merged_t[...], strip, preferred_element_type=F32)
        for j in range(3):
            put_sums(outs, (3 * i + j) * channels, part[:, j * channels : (j + 1) * channels])


def data_grad_kernel(stack, halo, feat, out_w, grad, *outs):
    cells = jnp.concatenate(strips_of(stack, halo), axis=1)
    taps = jnp.concatenate([out_w[tap] for tap in range(9)], axis=1)
    total = lax.dot_general(cells, taps, (((1,), (1,)), ((), ())), preferred_element_type=F32)
    grad[...] = total.astype(BF16)
    put_sums(outs, 0, jnp.dot(jnp.transpose(feat[...]), grad[...], preferred_element_type=F32))


def forward_kernel(peers, merged, out_w, grad, *refs):
    edges, (out, grad_top, stack, near, sem) = refs[:-5], refs[-5:]
    rows, cols, channels = merged.shape
    half = cols // 2
    for r in range(rows):
        put_shifted(stack, r + 1, merged[r], -1)
    if len(edges) == 1:
        start = edges[0].shape[0] - 2 * cols
        edge = jnp.concatenate([edges[0][start : start + cols, :], edges[0][start + cols :, :]], axis=1)
        put_halo(stack, edge, edge, rows, peers, -1)
    else:
        put_halo(stack, edges[0][edges[0].shape[0] - 1], edges[1][0], rows, peers, -1)
    cells = jnp.concatenate([stack[i : i + rows].reshape(rows * cols, 3 * channels) for i in range(3)], axis=1)
    total = jnp.dot(cells, out_w[...].reshape(9 * channels, channels), preferred_element_type=F32)
    near[...] = total.astype(BF16).reshape(out.shape)
    copy = pltpu.make_async_copy(near, out, sem)
    copy.start()
    lower = lax.broadcasted_iota(jnp.int32, (half, 2 * cols), 1)
    lower = jnp.where(lower >= cols, lower - cols, lower)
    pool = jnp.where(lower // 2 == lax.broadcasted_iota(jnp.int32, (half, 2 * cols), 0), 1.0, 0.0).astype(BF16)
    for q in range(rows // 2):
        pair = grad[2 * q * cols : (2 * q + 2) * cols, :]
        grad_top[q] = jnp.dot(pool, pair, preferred_element_type=F32).astype(BF16)
    copy.wait()


def places():
    chip, core = lax.axis_index("dp"), lax.axis_index("space")
    plane, line = chip % 4, chip // 4
    return jnp.where(core == 0, plane, line), jnp.where(core == 0, line, plane)


def block(index, length):
    return pl.ds(pl.multiple_of(index * length, 16), length)


def cut_kernel(mine, got, *refs):
    place, _ = places()
    share = mine.shape[0] // 4
    for k, out in zip((0, 3, 2, 1), refs[-4:]):
        rows = block(place ^ k, share)
        start = out.shape[0] - share
        if start:
            out[:start, :] = refs[0][...]
        out[start:, :] = (mine[rows, :] + got[rows, :].astype(F32)).astype(out.dtype)


def add_early_kernel(own, three, two, out):
    out[...] = own[...] + three[...].astype(F32) + two[...].astype(F32)


def add_kernel(part_a, own_b, one, three_b, two_b, out):
    edge = part_a.shape[0]
    out[:edge, :] = (part_a[...] + one[:edge, :].astype(F32)).astype(BF16)
    total = own_b[...] + one[edge:, :].astype(F32) + two_b[...].astype(F32) + three_b[...].astype(F32)
    out[edge:, :] = total.astype(BF16)


def finish_kernel(scale, own, one, two, three, _, out):
    near = own[...].astype(F32) + one[...].astype(F32)
    far = two[...].astype(F32) + three[...].astype(F32)
    out[...] = ((near + far) * scale).astype(BF16)


def place_kernel(*refs):
    results, sems = refs[8:10], refs[10]
    side = lax.axis_index("space")
    copies = []
    for columns, quarters, place in zip((side, 1 - side), (refs[:4], refs[4:8]), places()):
        lanes = pl.ds(pl.multiple_of(columns * 128, 128), 128)
        for k, quarter in enumerate(quarters):
            start = 0
            for result in results:
                share = result.shape[0] // 4
                to = result.at[block(place ^ k, share), lanes]
                copies.append(pltpu.make_async_copy(quarter.at[pl.ds(start, share), :], to, sems.at[len(copies)]))
                start += share
    for copy in copies:
        copy.start()
    for copy in copies:
        copy.wait()


def exchange(array, step, k):
    pairs = []
    for chip in range(16):
        for core in range(2):
            flip = k if core == step else 4 * k
            pairs.append((2 * chip + core, 2 * (chip ^ flip) + core))
    return lax.ppermute(array, ("dp", "space"), pairs)


def swap(array):
    return lax.ppermute(array, "space", [(0, 1), (1, 0)])


def call(kernel, *shapes, **more):
    return pl.pallas_call(
        kernel,
        out_shape=[jax.ShapeDtypeStruct(shape, kind) for shape, kind in shapes],
        compiler_params=pltpu.CompilerParams(vmem_limit_bytes=12 * 2**20),
        **more,
    )


def sum_everywhere(parts, scale, after):
    lengths, width = [mine.shape[0] for mine, _ in parts], parts[0][0].shape[1]
    vmem, far = pl.BlockSpec(memory_space=pltpu.VMEM), pl.BlockSpec(memory_space=pltpu.HBM)
    after = pltpu.with_memory_space_constraint(after, pltpu.HBM)
    share_a, share_b, quarter = [(length // 4, width) for length in (*lengths, sum(lengths))]
    own_a, three, two, one_a = call(cut_kernel, (share_a, F32), *[(share_a, BF16)] * 3)(*parts[0])
    three, two = exchange(three, 0, 3), exchange(two, 0, 2)
    slow = pl.CostEstimate(flops=3 * 2**28, bytes_accessed=2**10, transcendentals=0)
    [part_a] = call(add_early_kernel, (share_a, F32), cost_estimate=slow)(own_a, three, two)
    own_b, three, two, one = call(cut_kernel, (share_b, F32), *[(share_b, BF16)] * 2, (quarter, BF16))(*parts[1], one_a)
    one, three, two = exchange(one, 0, 1), exchange(three, 0, 3), exchange(two, 0, 2)
    [total] = call(add_kernel, (quarter, BF16))(part_a, own_b, one, three, two)
    three, two, one = [exchange(total, 1, k) for k in (3, 2, 1)]
    finish = call(functools.partial(finish_kernel, scale), (quarter, BF16), in_specs=[vmem] * 4 + [far])
    [total] = finish(total, one, two, three, after)
    three, two, one = [exchange(total, 0, k) for k in (3, 2, 1)]
    quarters = [total, one, two, three]
    return call(
        place_kernel,
        *[((length, 2 * width), BF16) for length in lengths],
        out_specs=[far] * 2,
        scratch_shapes=[pltpu.SemaphoreType.DMA((16,))],
    )(*quarters, *[swap(one) for one in quarters])


def local(features, top_down, lateral_weight, out_kernel, cotangent):
    images, rows, cols, in_channels = features.shape
    channels = lateral_weight.shape[1]
    cells = rows * cols
    peers = lax.axis_size("space")
    taps = out_kernel.reshape(9, channels, channels)
    params = pltpu.CompilerParams(vmem_limit_bytes=32 * 2**20)
    halves = peers == 2 and lax.axis_size("dp") == 16 and images == 1 and (channels, in_channels) == (256, 512)

    def sums(length, extra):
        if not halves:
            return [jax.ShapeDtypeStruct((length, channels), F32)]
        return [
            jax.ShapeDtypeStruct((length, channels // 2), F32),
            jax.ShapeDtypeStruct((length + extra, channels // 2), BF16),
        ]

    outs, tops, parts = [], [], None
    for image in range(images):
        cot = cotangent[image]
        cot_before, cot_after = neighbour_rows(cot)
        arrays = (cot, lateral_weight, top_down[image], features[image].reshape(cells, in_channels), taps)
        arrays = [pltpu.with_memory_space_constraint(array, pltpu.HBM) for array in arrays]
        merged, merged_t, stack, near_feat, near_taps = pl.pallas_call(
            merge_kernel,
            out_shape=[
                jax.ShapeDtypeStruct(shape, BF16)
                for shape in (
                    (cells, channels),
                    (channels, cells),
                    (rows, cols, 3 * channels),
                    (cells, in_channels),
                    taps.shape,
                )
            ],
            in_specs=[pl.BlockSpec(memory_space=pltpu.HBM)] * 5,
            scratch_shapes=[*[pltpu.VMEM(array.shape, BF16) for array in arrays[:3]], pltpu.SemaphoreType.DMA((5,))],
            compiler_params=params,
            cost_estimate=pl.CostEstimate(
                flops=2 * cells * channels * 4 * in_channels, bytes_accessed=4 * 2**20, transcendentals=0
            ),
        )(*arrays)
        halo, *kernel_part = pl.pallas_call(
            functools.partial(kernel_grad_kernel, peers),
            out_shape=[jax.ShapeDtypeStruct((2, cols, 3 * channels), BF16), *sums(9 * channels, 2 * cols)],
            compiler_params=params,
            cost_estimate=pl.CostEstimate(
                flops=2 * cells * channels * 9 * channels, bytes_accessed=4 * 2**20, transcendentals=0
            ),
        )(stack, merged, merged_t, cot_before, cot_after)
        if halves:
            kernel_part[1] = swap(kernel_part[1])
        grad, *lateral_part = pl.pallas_call(
            data_grad_kernel,
            out_shape=[jax.ShapeDtypeStruct((cells, channels), BF16), *sums(in_channels, 0)],
            compiler_params=params,
            cost_estimate=pl.CostEstimate(
                flops=2 * cells * channels * (9 * channels + in_channels), bytes_accessed=4 * 2**20, transcendentals=0
            ),
        )(stack, halo, near_feat, near_taps)
        if halves:
            lateral_part[1] = swap(lateral_part[1])
        merged = merged.reshape(rows, cols, channels)
        edges = kernel_part[1:] if halves else neighbour_rows(merged)
        out, grad_top = pl.pallas_call(
            functools.partial(forward_kernel, peers),
            out_shape=[
                jax.ShapeDtypeStruct((rows, cols, channels), BF16),
                jax.ShapeDtypeStruct((rows // 2, cols // 2, channels), BF16),
            ],
            out_specs=[pl.BlockSpec(memory_space=pltpu.HBM), pl.BlockSpec(memory_space=pltpu.VMEM)],
            scratch_shapes=[
                pltpu.VMEM((rows + 2, cols, 3 * channels), BF16),
                pltpu.VMEM((rows, cols, channels), BF16),
                pltpu.SemaphoreType.DMA,
            ],
            compiler_params=params,
            cost_estimate=pl.CostEstimate(
                flops=2 * cells * channels * 9 * channels, bytes_accessed=2 * 2**20, transcendentals=0
            ),
        )(merged, near_taps, grad, *edges)
        outs.append(out)
        tops.append(grad_top)
        if not halves:
            part = [kernel_part[0], lateral_part[0]]
            parts = part if parts is None else [a + b for a, b in zip(parts, part)]
    scale = 1.0 / (images * lax.axis_size("dp"))
    if halves:
        grad_kernel, grad_lateral = sum_everywhere((kernel_part, lateral_part), scale, outs[0])
    else:
        grad_kernel, grad_lateral = [(total * scale).astype(BF16) for total in lax.psum(parts, ("dp", "space"))]
    return jnp.stack(outs), jnp.stack(tops), grad_kernel.reshape(out_kernel.shape), grad_lateral


def solution(mesh):
    return jax.shard_map(
        local,
        mesh=mesh,
        in_specs=(
            P("dp", "space", None, None),
            P("dp", "space", None, None),
            P(),
            P(),
            P("dp", "space", None, None),
        ),
        out_specs=(P("dp", "space", None, None), P("dp", "space", None, None), P(), P()),
        check_vma=False,
    )
```

```python
import functools

import jax
import jax.numpy as jnp
from jax import lax
from jax.experimental import pallas as pl
from jax.experimental.pallas import tpu as pltpu
from jax.sharding import PartitionSpec as P

F32 = jnp.float32
BF16 = jnp.bfloat16


def neighbour_rows(array):
    peers = lax.axis_size("space")
    if peers == 1:
        return array[-1:], array[:1]
    if peers == 2:
        got = lax.ppermute(array, "space", [(0, 1), (1, 0)])
        return got, got
    up = [(i, i + 1) for i in range(peers - 1)]
    down = [(j, i) for i, j in up]
    return lax.ppermute(array[-1:], "space", up), lax.ppermute(array[:1], "space", down)


def put_shifted(stack, slot, row, sign):
    cols, channels = row.shape
    wide = row.astype(F32)
    place = lax.broadcasted_iota(jnp.int32, (cols, channels), 0)
    later = jnp.where(place == cols - 1, 0.0, pltpu.roll(wide, cols - 1, 0)).astype(BF16)
    earlier = jnp.where(place == 0, 0.0, pltpu.roll(wide, 1, 0)).astype(BF16)
    first, last = (earlier, later) if sign < 0 else (later, earlier)
    stack[slot, :, 0:channels] = first
    stack[slot, :, channels : 2 * channels] = row
    stack[slot, :, 2 * channels :] = last


def put_halo(stack, before, after, rows, peers, sign):
    here = lax.axis_index("space")
    zero = jnp.zeros(before.shape, BF16)
    put_shifted(stack, 0, jnp.where(here > 0, before, zero), sign)
    put_shifted(stack, rows + 1, jnp.where(here < peers - 1, after, zero), sign)


def merge_kernel(*refs):
    far, (merged, merged_t, stack, feat, out_w), near, sems = refs[:5], refs[5:10], refs[10:13], refs[13]
    near = (*near, feat, out_w)
    copies = [pltpu.make_async_copy(a, b, sems.at[i]) for i, (a, b) in enumerate(zip(far, near))]
    for copy in copies:
        copy.start()
    cot, lat_w, top = near[:3]
    rows, cols, channels = cot.shape
    half = cols // 2
    copies[0].wait()
    for r in range(rows):
        put_shifted(stack, r, cot[r], 1)
    for copy in copies[1:4]:
        copy.wait()
    upper = lax.broadcasted_iota(jnp.int32, (cols, half), 0)
    spread = jnp.where(upper // 2 == lax.broadcasted_iota(jnp.int32, (cols, half), 1), 1.0, 0.0).astype(BF16)
    lateral = jnp.dot(feat[...], lat_w[...], preferred_element_type=F32)
    for q in range(rows // 2):
        lifted = jnp.dot(spread, top[q], preferred_element_type=F32)
        for r in (2 * q, 2 * q + 1):
            merged[r * cols : (r + 1) * cols, :] = (lateral[r * cols : (r + 1) * cols] + lifted).astype(BF16)
    merged_t[...] = jnp.transpose(merged[...])
    copies[4].wait()


def strips_of(stack, halo):
    rows, cols, deep = stack.shape
    strips = [
        jnp.concatenate([stack[1:], halo[1:]], axis=0),
        stack[...],
        jnp.concatenate([halo[:1], stack[: rows - 1]], axis=0),
    ]
    return [strip.reshape(rows * cols, deep) for strip in strips]


def put_sums(outs, start, values):
    rows = slice(start, start + values.shape[0])
    if len(outs) == 1:
        outs[0][rows, :] = values
        return
    here = lax.axis_index("space")
    half = values.shape[1] // 2
    mine, theirs = outs
    mine[rows, :] = jnp.where(here == 0, values[:, :half], values[:, half:])
    theirs[rows, :] = jnp.where(here == 0, values[:, half:], values[:, :half]).astype(BF16)


def put_taps(outs, start, merged_t, strip):
    channels = merged_t.shape[0]
    part = jnp.dot(merged_t[...], strip, preferred_element_type=F32)
    for j in range(3):
        put_sums(outs, start + j * channels, part[:, j * channels : (j + 1) * channels])


def first_grads_kernel(peers, stack, merged, merged_t, before, after, halo, *outs):
    cols = stack.shape[1]
    channels, cells = merged_t.shape
    put_halo(halo, before[before.shape[0] - 1], after[0], 0, peers, 1)
    if len(outs) == 2:
        here = lax.axis_index("space")
        edge = jnp.where(here == 0, merged[cells - cols :, :], merged[:cols, :])
        start = 6 * channels
        outs[1][start : start + cols, :] = edge[:, : channels // 2]
        outs[1][start + cols :, :] = edge[:, channels // 2 :]
    strips = strips_of(stack, halo)
    for i in range(2):
        put_taps(outs, 3 * i * channels, merged_t, strips[i])


def last_grads_kernel(stack, merged_t, halo, feat, out_w, grad, *outs):
    channels = merged_t.shape[0]
    strips = strips_of(stack, halo)
    put_taps(outs, 0, merged_t, strips[2])
    cells = jnp.concatenate(strips, axis=1)
    taps = jnp.concatenate([out_w[tap] for tap in range(9)], axis=1)
    total = lax.dot_general(cells, taps, (((1,), (1,)), ((), ())), preferred_element_type=F32)
    grad[...] = total.astype(BF16)
    put_sums(outs, 3 * channels, jnp.dot(jnp.transpose(feat[...]), grad[...], preferred_element_type=F32))


def forward_kernel(peers, merged, out_w, grad, *refs):
    edges, (out, grad_top, stack, near, sem) = refs[:-5], refs[-5:]
    rows, cols, channels = merged.shape
    half = cols // 2
    for r in range(rows):
        put_shifted(stack, r + 1, merged[r], -1)
    if len(edges) == 1:
        start = edges[0].shape[0] - 2 * cols
        edge = jnp.concatenate([edges[0][start : start + cols, :], edges[0][start + cols :, :]], axis=1)
        put_halo(stack, edge, edge, rows, peers, -1)
    else:
        put_halo(stack, edges[0][edges[0].shape[0] - 1], edges[1][0], rows, peers, -1)
    cells = jnp.concatenate([stack[i : i + rows].reshape(rows * cols, 3 * channels) for i in range(3)], axis=1)
    total = jnp.dot(cells, out_w[...].reshape(9 * channels, channels), preferred_element_type=F32)
    near[...] = total.astype(BF16).reshape(out.shape)
    copy = pltpu.make_async_copy(near, out, sem)
    copy.start()
    lower = lax.broadcasted_iota(jnp.int32, (half, 2 * cols), 1)
    lower = jnp.where(lower >= cols, lower - cols, lower)
    pool = jnp.where(lower // 2 == lax.broadcasted_iota(jnp.int32, (half, 2 * cols), 0), 1.0, 0.0).astype(BF16)
    for q in range(rows // 2):
        pair = grad[2 * q * cols : (2 * q + 2) * cols, :]
        grad_top[q] = jnp.dot(pool, pair, preferred_element_type=F32).astype(BF16)
    copy.wait()


def places():
    chip, core = lax.axis_index("dp"), lax.axis_index("space")
    plane, line = chip % 4, chip // 4
    return jnp.where(core == 0, plane, line), jnp.where(core == 0, line, plane)


def block(index, length):
    return pl.ds(pl.multiple_of(index * length, 16), length)


def cut_kernel(segments, mine, got, *refs):
    place, _ = places()
    for k, out in zip((0, 3, 2, 1), refs):
        start, to = 0, 0
        for length in segments:
            share = length // 4
            rows = pl.ds(pl.multiple_of(start + (place ^ k) * share, 16), share)
            out[to : to + share, :] = (mine[rows, :] + got[rows, :].astype(F32)).astype(out.dtype)
            start, to = start + length, to + share


def add_kernel(own, three, two, one, *refs):
    out = refs[-1]
    total = own[...] + one[...].astype(F32) + two[...].astype(F32) + three[...].astype(F32)
    out[...] = total.astype(BF16)


def finish_kernel(scale, own, one, two, three, *refs):
    near = own[...].astype(F32) + one[...].astype(F32)
    far = two[...].astype(F32) + three[...].astype(F32)
    out = refs[-1]
    start = out.shape[0] - own.shape[0]
    if start:
        out[:start, :] = refs[0][...]
    out[start:, :] = ((near + far) * scale).astype(BF16)


def place_kernel(segments, *refs):
    results, sems = refs[8:10], refs[10]
    side = lax.axis_index("space")
    copies = []
    for columns, quarters, place in zip((side, 1 - side), (refs[:4], refs[4:8]), places()):
        lanes = pl.ds(pl.multiple_of(columns * 128, 128), 128)
        for k, quarter in enumerate(quarters):
            start = 0
            for result, first, length in segments:
                share = length // 4
                rows = pl.ds(pl.multiple_of(first + (place ^ k) * share, 16), share)
                to = results[result].at[rows, lanes]
                copies.append(pltpu.make_async_copy(quarter.at[pl.ds(start, share), :], to, sems.at[len(copies)]))
                start += share
    for copy in copies:
        copy.start()
    for copy in copies:
        copy.wait()


def exchange(array, step, k):
    pairs = []
    for chip in range(16):
        for core in range(2):
            flip = k if core == step else 4 * k
            pairs.append((2 * chip + core, 2 * (chip ^ flip) + core))
    return lax.ppermute(array, ("dp", "space"), pairs)


def swap(array):
    return lax.ppermute(array, "space", [(0, 1), (1, 0)])


def call(kernel, *shapes, **more):
    return pl.pallas_call(
        kernel,
        out_shape=[jax.ShapeDtypeStruct(shape, kind) for shape, kind in shapes],
        compiler_params=pltpu.CompilerParams(vmem_limit_bytes=12 * 2**20),
        **more,
    )


def sum_everywhere(parts, splits, scale, after):
    width = parts[0][0].shape[1]
    vmem, far = pl.BlockSpec(memory_space=pltpu.VMEM), pl.BlockSpec(memory_space=pltpu.HBM)
    after = pltpu.with_memory_space_constraint(after, pltpu.HBM)
    slow = pl.CostEstimate(flops=2**30, bytes_accessed=2**10, transcendentals=0)
    shares = [(sum(split) // 4, width) for split in splits]
    terms = []
    for part, split, share in zip(parts, splits, shares):
        own, *pieces = call(functools.partial(cut_kernel, split), (share, F32), *[(share, BF16)] * 3)(*part)
        terms.append([own] + [exchange(piece, 0, k) for piece, k in zip(pieces, (3, 2, 1))])
    sums = []
    for number, share in enumerate(shares):
        extra = [after] if number == 0 else []
        [total] = call(
            add_kernel, (share, BF16), in_specs=[vmem] * 4 + [far] * len(extra), cost_estimate=slow
        )(*terms[number], *extra)
        three, two, one = [exchange(total, 1, k) for k in (3, 2, 1)]
        sums.append((total, one, two, three))
    finish = functools.partial(finish_kernel, scale)
    [first] = call(finish, (shares[0], BF16), cost_estimate=slow)(*sums[0])
    [joint] = call(finish, ((sum(rows for rows, _ in shares), width), BF16))(*sums[1], first)
    three, two, one = [exchange(joint, 0, k) for k in (3, 2, 1)]
    quarters = [joint, one, two, three]
    (length_a,), (length_b, length_c) = splits
    return call(
        functools.partial(place_kernel, ((0, 0, length_a), (0, length_a, length_b), (1, 0, length_c))),
        ((length_a + length_b, 2 * width), BF16),
        ((length_c, 2 * width), BF16),
        out_specs=[far] * 2,
        scratch_shapes=[pltpu.SemaphoreType.DMA((24,))],
    )(*quarters, *[swap(one) for one in quarters])


def local(features, top_down, lateral_weight, out_kernel, cotangent):
    images, rows, cols, in_channels = features.shape
    channels = lateral_weight.shape[1]
    cells = rows * cols
    peers = lax.axis_size("space")
    taps = out_kernel.reshape(9, channels, channels)
    params = pltpu.CompilerParams(vmem_limit_bytes=32 * 2**20)
    halves = peers == 2 and lax.axis_size("dp") == 16 and images == 1 and (channels, in_channels) == (256, 512)

    def sums(length, extra):
        if not halves:
            return [jax.ShapeDtypeStruct((length, channels), F32)]
        return [
            jax.ShapeDtypeStruct((length, channels // 2), F32),
            jax.ShapeDtypeStruct((length + extra, channels // 2), BF16),
        ]

    outs, tops, parts = [], [], None
    for image in range(images):
        cot = cotangent[image]
        cot_before, cot_after = neighbour_rows(cot)
        arrays = (cot, lateral_weight, top_down[image], features[image].reshape(cells, in_channels), taps)
        arrays = [pltpu.with_memory_space_constraint(array, pltpu.HBM) for array in arrays]
        merged, merged_t, stack, near_feat, near_taps = pl.pallas_call(
            merge_kernel,
            out_shape=[
                jax.ShapeDtypeStruct(shape, BF16)
                for shape in (
                    (cells, channels),
                    (channels, cells),
                    (rows, cols, 3 * channels),
                    (cells, in_channels),
                    taps.shape,
                )
            ],
            in_specs=[pl.BlockSpec(memory_space=pltpu.HBM)] * 5,
            scratch_shapes=[*[pltpu.VMEM(array.shape, BF16) for array in arrays[:3]], pltpu.SemaphoreType.DMA((5,))],
            compiler_params=params,
            cost_estimate=pl.CostEstimate(
                flops=2 * cells * channels * 4 * in_channels, bytes_accessed=4 * 2**20, transcendentals=0
            ),
        )(*arrays)
        halo, *first_part = pl.pallas_call(
            functools.partial(first_grads_kernel, peers),
            out_shape=[jax.ShapeDtypeStruct((2, cols, 3 * channels), BF16), *sums(6 * channels, 2 * cols)],
            compiler_params=params,
            cost_estimate=pl.CostEstimate(
                flops=2 * cells * channels * 6 * channels, bytes_accessed=4 * 2**20, transcendentals=0
            ),
        )(stack, merged, merged_t, cot_before, cot_after)
        if halves:
            first_part[1] = swap(first_part[1])
        grad, *last_part = pl.pallas_call(
            last_grads_kernel,
            out_shape=[jax.ShapeDtypeStruct((cells, channels), BF16), *sums(3 * channels + in_channels, 0)],
            compiler_params=params,
            cost_estimate=pl.CostEstimate(
                flops=2 * cells * channels * (12 * channels + in_channels), bytes_accessed=4 * 2**20, transcendentals=0
            ),
        )(stack, merged_t, halo, near_feat, near_taps)
        if halves:
            last_part[1] = swap(last_part[1])
        merged = merged.reshape(rows, cols, channels)
        edges = first_part[1:] if halves else neighbour_rows(merged)
        out, grad_top = pl.pallas_call(
            functools.partial(forward_kernel, peers),
            out_shape=[
                jax.ShapeDtypeStruct((rows, cols, channels), BF16),
                jax.ShapeDtypeStruct((rows // 2, cols // 2, channels), BF16),
            ],
            out_specs=[pl.BlockSpec(memory_space=pltpu.HBM), pl.BlockSpec(memory_space=pltpu.VMEM)],
            scratch_shapes=[
                pltpu.VMEM((rows + 2, cols, 3 * channels), BF16),
                pltpu.VMEM((rows, cols, channels), BF16),
                pltpu.SemaphoreType.DMA,
            ],
            compiler_params=params,
            cost_estimate=pl.CostEstimate(
                flops=2 * cells * channels * 9 * channels, bytes_accessed=2 * 2**20, transcendentals=0
            ),
        )(merged, near_taps, grad, *edges)
        outs.append(out)
        tops.append(grad_top)
        if not halves:
            part = [first_part[0], last_part[0]]
            parts = part if parts is None else [a + b for a, b in zip(parts, part)]
    scale = 1.0 / (images * lax.axis_size("dp"))
    if halves:
        splits = (6 * channels,), (3 * channels, in_channels)
        grad_kernel, grad_lateral = sum_everywhere((first_part, last_part), splits, scale, outs[0])
    else:
        total = jnp.concatenate(lax.psum(parts, ("dp", "space")))
        total = (total * scale).astype(BF16)
        grad_kernel, grad_lateral = total[: 9 * channels], total[9 * channels :]
    return jnp.stack(outs), jnp.stack(tops), grad_kernel.reshape(out_kernel.shape), grad_lateral


def solution(mesh):
    return jax.shard_map(
        local,
        mesh=mesh,
        in_specs=(
            P("dp", "space", None, None),
            P("dp", "space", None, None),
            P(),
            P(),
            P("dp", "space", None, None),
        ),
        out_specs=(P("dp", "space", None, None), P("dp", "space", None, None), P(), P()),
        check_vma=False,
    )
```

```python
import functools

import jax
import jax.numpy as jnp
from jax import lax
from jax.experimental import pallas as pl
from jax.experimental.pallas import tpu as pltpu
from jax.sharding import PartitionSpec as P

F32 = jnp.float32
BF16 = jnp.bfloat16


def neighbour_rows(array):
    peers = lax.axis_size("space")
    if peers == 1:
        return array[-1:], array[:1]
    if peers == 2:
        got = lax.ppermute(array, "space", [(0, 1), (1, 0)])
        return got, got
    up = [(i, i + 1) for i in range(peers - 1)]
    down = [(j, i) for i, j in up]
    return lax.ppermute(array[-1:], "space", up), lax.ppermute(array[:1], "space", down)


def put_shifted(stack, slot, row, sign):
    cols, channels = row.shape
    wide = row.astype(F32)
    place = lax.broadcasted_iota(jnp.int32, (cols, channels), 0)
    later = jnp.where(place == cols - 1, 0.0, pltpu.roll(wide, cols - 1, 0)).astype(BF16)
    earlier = jnp.where(place == 0, 0.0, pltpu.roll(wide, 1, 0)).astype(BF16)
    first, last = (earlier, later) if sign < 0 else (later, earlier)
    stack[slot, :, 0:channels] = first
    stack[slot, :, channels : 2 * channels] = row
    stack[slot, :, 2 * channels :] = last


def put_halo(stack, before, after, rows, peers, sign):
    here = lax.axis_index("space")
    zero = jnp.zeros(before.shape, BF16)
    put_shifted(stack, 0, jnp.where(here > 0, before, zero), sign)
    put_shifted(stack, rows + 1, jnp.where(here < peers - 1, after, zero), sign)


def merge_kernel(*refs):
    far, (merged, merged_t, stack, feat), near, sems = refs[:4], refs[4:8], refs[8:11], refs[11]
    near = (*near, feat)
    copies = [pltpu.make_async_copy(a, b, sems.at[i]) for i, (a, b) in enumerate(zip(far, near))]
    for copy in copies:
        copy.start()
    cot, lat_w, top = near[:3]
    rows, cols, channels = cot.shape
    half = cols // 2
    copies[0].wait()
    for r in range(rows):
        put_shifted(stack, r, cot[r], 1)
    for copy in copies[1:]:
        copy.wait()
    upper = lax.broadcasted_iota(jnp.int32, (cols, half), 0)
    spread = jnp.where(upper // 2 == lax.broadcasted_iota(jnp.int32, (cols, half), 1), 1.0, 0.0).astype(BF16)
    lateral = jnp.dot(feat[...], lat_w[...], preferred_element_type=F32)
    for q in range(rows // 2):
        lifted = jnp.dot(spread, top[q], preferred_element_type=F32)
        for r in (2 * q, 2 * q + 1):
            merged[r * cols : (r + 1) * cols, :] = (lateral[r * cols : (r + 1) * cols] + lifted).astype(BF16)
    merged_t[...] = jnp.transpose(merged[...])


def strips_of(stack, halo):
    rows, cols, deep = stack.shape
    strips = [
        jnp.concatenate([stack[1:], halo[1:]], axis=0),
        stack[...],
        jnp.concatenate([halo[:1], stack[: rows - 1]], axis=0),
    ]
    return [strip.reshape(rows * cols, deep) for strip in strips]


def put_sums(outs, start, values):
    rows = slice(start, start + values.shape[0])
    if len(outs) == 1:
        outs[0][rows, :] = values
        return
    here = lax.axis_index("space")
    half = values.shape[1] // 2
    mine, theirs = outs
    mine[rows, :] = jnp.where(here == 0, values[:, :half], values[:, half:])
    theirs[rows, :] = jnp.where(here == 0, values[:, half:], values[:, :half]).astype(BF16)


def kernel_grad_kernel(peers, stack, merged, merged_t, before, after, taps_far, out_w, halo, *refs):
    outs, sem = refs[:-1], refs[-1]
    copy = pltpu.make_async_copy(taps_far, out_w, sem)
    copy.start()
    cols = stack.shape[1]
    channels, cells = merged_t.shape
    put_halo(halo, before[before.shape[0] - 1], after[0], 0, peers, 1)
    if len(outs) == 2:
        here = lax.axis_index("space")
        edge = jnp.where(here == 0, merged[cells - cols :, :], merged[:cols, :])
        start = 9 * channels
        outs[1][start : start + cols, :] = edge[:, : channels // 2]
        outs[1][start + cols :, :] = edge[:, channels // 2 :]
    for i, strip in enumerate(strips_of(stack, halo)):
        part = jnp.dot(merged_t[...], strip, preferred_element_type=F32)
        for j in range(3):
            put_sums(outs, (3 * i + j) * channels, part[:, j * channels : (j + 1) * channels])
    copy.wait()


def data_grad_kernel(stack, halo, feat, out_w, grad, *outs):
    cells = jnp.concatenate(strips_of(stack, halo), axis=1)
    taps = jnp.concatenate([out_w[tap] for tap in range(9)], axis=1)
    total = lax.dot_general(cells, taps, (((1,), (1,)), ((), ())), preferred_element_type=F32)
    grad[...] = total.astype(BF16)
    put_sums(outs, 0, jnp.dot(jnp.transpose(feat[...]), grad[...], preferred_element_type=F32))


def forward_kernel(peers, merged, out_w, grad, *refs):
    edges, (out, grad_top, stack, near, sem) = refs[:-5], refs[-5:]
    rows, cols, channels = merged.shape
    half = cols // 2
    for r in range(rows):
        put_shifted(stack, r + 1, merged[r], -1)
    if len(edges) == 1:
        start = edges[0].shape[0] - 2 * cols
        edge = jnp.concatenate([edges[0][start : start + cols, :], edges[0][start + cols :, :]], axis=1)
        put_halo(stack, edge, edge, rows, peers, -1)
    else:
        put_halo(stack, edges[0][edges[0].shape[0] - 1], edges[1][0], rows, peers, -1)
    cells = jnp.concatenate([stack[i : i + rows].reshape(rows * cols, 3 * channels) for i in range(3)], axis=1)
    total = jnp.dot(cells, out_w[...].reshape(9 * channels, channels), preferred_element_type=F32)
    near[...] = total.astype(BF16).reshape(out.shape)
    copy = pltpu.make_async_copy(near, out, sem)
    copy.start()
    lower = lax.broadcasted_iota(jnp.int32, (half, 2 * cols), 1)
    lower = jnp.where(lower >= cols, lower - cols, lower)
    pool = jnp.where(lower // 2 == lax.broadcasted_iota(jnp.int32, (half, 2 * cols), 0), 1.0, 0.0).astype(BF16)
    for q in range(rows // 2):
        pair = grad[2 * q * cols : (2 * q + 2) * cols, :]
        grad_top[q] = jnp.dot(pool, pair, preferred_element_type=F32).astype(BF16)
    copy.wait()


def places():
    chip, core = lax.axis_index("dp"), lax.axis_index("space")
    plane, line = chip % 4, chip // 4
    return jnp.where(core == 0, plane, line), jnp.where(core == 0, line, plane)


def block(index, length):
    return pl.ds(pl.multiple_of(index * length, 16), length)


def cut_kernel(mine, got, *refs):
    place, _ = places()
    share = mine.shape[0] // 4
    for k, out in zip((0, 2, 3, 1), refs[-4:]):
        rows = block(place ^ k, share)
        start = out.shape[0] - share
        if start:
            out[:start, :] = refs[0][...]
        out[start:, :] = (mine[rows, :] + got[rows, :].astype(F32)).astype(out.dtype)


def add_early_kernel(own, two, three, out):
    out[...] = own[...] + three[...].astype(F32) + two[...].astype(F32)


def add_kernel(part_a, own_b, one, two_b, three_b, out):
    edge = part_a.shape[0]
    out[:edge, :] = (part_a[...] + one[:edge, :].astype(F32)).astype(BF16)
    total = own_b[...] + one[edge:, :].astype(F32) + two_b[...].astype(F32) + three_b[...].astype(F32)
    out[edge:, :] = total.astype(BF16)


def finish_kernel(scale, own, one, three, two, _, out):
    near = own[...].astype(F32) + one[...].astype(F32)
    far = two[...].astype(F32) + three[...].astype(F32)
    out[...] = ((near + far) * scale).astype(BF16)


def place_kernel(pair, *refs):
    results, sems = refs[-3:-1], refs[-1]
    side = lax.axis_index("space")
    columns, place = (1 - side, places()[1]) if pair else (side, places()[0])
    lanes = pl.ds(pl.multiple_of(columns * 128, 128), 128)
    copies = []
    for k, quarter in zip((0, 1, 3, 2), refs):
        start = 0
        for result in results:
            share = result.shape[0] // 4
            to = result.at[block(place ^ k, share), lanes]
            copies.append(pltpu.make_async_copy(quarter.at[pl.ds(start, share), :], to, sems.at[len(copies)]))
            start += share
    for copy in copies:
        copy.start()
    for copy in copies:
        copy.wait()


def exchange(array, step, k):
    pairs = []
    for chip in range(16):
        for core in range(2):
            flip = k if core == step else 4 * k
            pairs.append((2 * chip + core, 2 * (chip ^ flip) + core))
    return lax.ppermute(array, ("dp", "space"), pairs)


def swap(array):
    return lax.ppermute(array, "space", [(0, 1), (1, 0)])


def call(kernel, *shapes, **more):
    return pl.pallas_call(
        kernel,
        out_shape=[jax.ShapeDtypeStruct(shape, kind) for shape, kind in shapes],
        compiler_params=pltpu.CompilerParams(vmem_limit_bytes=12 * 2**20),
        **more,
    )


def sum_everywhere(parts, scale, after):
    lengths, width = [mine.shape[0] for mine, _ in parts], parts[0][0].shape[1]
    vmem, far = pl.BlockSpec(memory_space=pltpu.VMEM), pl.BlockSpec(memory_space=pltpu.HBM)
    after = pltpu.with_memory_space_constraint(after, pltpu.HBM)
    share_a, share_b, quarter = [(length // 4, width) for length in (*lengths, sum(lengths))]
    own_a, two, three, one_a = call(cut_kernel, (share_a, F32), *[(share_a, BF16)] * 3)(*parts[0])
    two, three = exchange(two, 0, 2), exchange(three, 0, 3)
    slow = pl.CostEstimate(flops=3 * 2**28, bytes_accessed=2**10, transcendentals=0)
    [part_a] = call(add_early_kernel, (share_a, F32), cost_estimate=slow)(own_a, two, three)
    own_b, two, three, one = call(cut_kernel, (share_b, F32), *[(share_b, BF16)] * 2, (quarter, BF16))(*parts[1], one_a)
    one, two, three = exchange(one, 0, 1), exchange(two, 0, 2), exchange(three, 0, 3)
    [total] = call(add_kernel, (quarter, BF16))(part_a, own_b, one, two, three)
    two, three, one = [exchange(total, 1, k) for k in (2, 3, 1)]
    finish = call(functools.partial(finish_kernel, scale), (quarter, BF16), in_specs=[vmem] * 4 + [far])
    [total] = finish(total, one, three, two, after)
    two, three, one = [exchange(total, 0, k) for k in (2, 3, 1)]
    quarters = [total, one, three, two]
    results = [((length, 2 * width), BF16) for length in lengths]
    place = dict(out_specs=[far] * 2, scratch_shapes=[pltpu.SemaphoreType.DMA((8,))])
    half = call(functools.partial(place_kernel, False), *results, **place)(*quarters)
    place.update(in_specs=[vmem] * 4 + [far] * 2, input_output_aliases={4: 0, 5: 1})
    return call(functools.partial(place_kernel, True), *results, **place)(*[swap(one) for one in quarters], *half)


def local(features, top_down, lateral_weight, out_kernel, cotangent):
    images, rows, cols, in_channels = features.shape
    channels = lateral_weight.shape[1]
    cells = rows * cols
    peers = lax.axis_size("space")
    taps = out_kernel.reshape(9, channels, channels)
    params = pltpu.CompilerParams(vmem_limit_bytes=32 * 2**20)
    halves = peers == 2 and lax.axis_size("dp") == 16 and images == 1 and (channels, in_channels) == (256, 512)

    def sums(length, extra):
        if not halves:
            return [jax.ShapeDtypeStruct((length, channels), F32)]
        return [
            jax.ShapeDtypeStruct((length, channels // 2), F32),
            jax.ShapeDtypeStruct((length + extra, channels // 2), BF16),
        ]

    outs, tops, parts = [], [], None
    for image in range(images):
        cot = cotangent[image]
        cot_before, cot_after = neighbour_rows(cot)
        arrays = (cot, lateral_weight, top_down[image], features[image].reshape(cells, in_channels), taps)
        arrays = [pltpu.with_memory_space_constraint(array, pltpu.HBM) for array in arrays]
        merged, merged_t, stack, near_feat = pl.pallas_call(
            merge_kernel,
            out_shape=[
                jax.ShapeDtypeStruct(shape, BF16)
                for shape in (
                    (cells, channels),
                    (channels, cells),
                    (rows, cols, 3 * channels),
                    (cells, in_channels),
                )
            ],
            in_specs=[pl.BlockSpec(memory_space=pltpu.HBM)] * 4,
            scratch_shapes=[*[pltpu.VMEM(array.shape, BF16) for array in arrays[:3]], pltpu.SemaphoreType.DMA((4,))],
            compiler_params=params,
            cost_estimate=pl.CostEstimate(
                flops=2 * cells * channels * 4 * in_channels, bytes_accessed=4 * 2**20, transcendentals=0
            ),
        )(*arrays[:4])
        near_taps, halo, *kernel_part = pl.pallas_call(
            functools.partial(kernel_grad_kernel, peers),
            out_shape=[
                jax.ShapeDtypeStruct(taps.shape, BF16),
                jax.ShapeDtypeStruct((2, cols, 3 * channels), BF16),
                *sums(9 * channels, 2 * cols),
            ],
            in_specs=[pl.BlockSpec(memory_space=pltpu.VMEM)] * 5 + [pl.BlockSpec(memory_space=pltpu.HBM)],
            scratch_shapes=[pltpu.SemaphoreType.DMA],
            compiler_params=params,
            cost_estimate=pl.CostEstimate(
                flops=2 * cells * channels * 9 * channels, bytes_accessed=4 * 2**20, transcendentals=0
            ),
        )(stack, merged, merged_t, cot_before, cot_after, arrays[4])
        if halves:
            kernel_part[1] = swap(kernel_part[1])
        grad, *lateral_part = pl.pallas_call(
            data_grad_kernel,
            out_shape=[jax.ShapeDtypeStruct((cells, channels), BF16), *sums(in_channels, 0)],
            compiler_params=params,
            cost_estimate=pl.CostEstimate(
                flops=2 * cells * channels * (9 * channels + in_channels), bytes_accessed=4 * 2**20, transcendentals=0
            ),
        )(stack, halo, near_feat, near_taps)
        if halves:
            lateral_part[1] = swap(lateral_part[1])
        merged = merged.reshape(rows, cols, channels)
        edges = kernel_part[1:] if halves else neighbour_rows(merged)
        out, grad_top = pl.pallas_call(
            functools.partial(forward_kernel, peers),
            out_shape=[
                jax.ShapeDtypeStruct((rows, cols, channels), BF16),
                jax.ShapeDtypeStruct((rows // 2, cols // 2, channels), BF16),
            ],
            out_specs=[pl.BlockSpec(memory_space=pltpu.HBM), pl.BlockSpec(memory_space=pltpu.VMEM)],
            scratch_shapes=[
                pltpu.VMEM((rows + 2, cols, 3 * channels), BF16),
                pltpu.VMEM((rows, cols, channels), BF16),
                pltpu.SemaphoreType.DMA,
            ],
            compiler_params=params,
            cost_estimate=pl.CostEstimate(
                flops=2 * cells * channels * 9 * channels, bytes_accessed=2 * 2**20, transcendentals=0
            ),
        )(merged, near_taps, grad, *edges)
        outs.append(out)
        tops.append(grad_top)
        if not halves:
            part = [kernel_part[0], lateral_part[0]]
            parts = part if parts is None else [a + b for a, b in zip(parts, part)]
    scale = 1.0 / (images * lax.axis_size("dp"))
    if halves:
        grad_kernel, grad_lateral = sum_everywhere((kernel_part, lateral_part), scale, outs[0])
    else:
        grad_kernel, grad_lateral = [(total * scale).astype(BF16) for total in lax.psum(parts, ("dp", "space"))]
    return jnp.stack(outs), jnp.stack(tops), grad_kernel.reshape(out_kernel.shape), grad_lateral


def solution(mesh):
    return jax.shard_map(
        local,
        mesh=mesh,
        in_specs=(
            P("dp", "space", None, None),
            P("dp", "space", None, None),
            P(),
            P(),
            P("dp", "space", None, None),
        ),
        out_specs=(P("dp", "space", None, None), P("dp", "space", None, None), P(), P()),
        check_vma=False,
    )
```

```python
import functools

import jax
import jax.numpy as jnp
from jax import lax
from jax.experimental import pallas as pl
from jax.experimental.pallas import tpu as pltpu
from jax.sharding import PartitionSpec as P

F32 = jnp.float32
BF16 = jnp.bfloat16


def neighbour_rows(array):
    peers = lax.axis_size("space")
    if peers == 1:
        return array[-1:], array[:1]
    if peers == 2:
        got = lax.ppermute(array, "space", [(0, 1), (1, 0)])
        return got, got
    up = [(i, i + 1) for i in range(peers - 1)]
    down = [(j, i) for i, j in up]
    return lax.ppermute(array[-1:], "space", up), lax.ppermute(array[:1], "space", down)


def put_shifted(stack, slot, row, sign):
    cols, channels = row.shape
    wide = row.astype(F32)
    place = lax.broadcasted_iota(jnp.int32, (cols, channels), 0)
    later = jnp.where(place == cols - 1, 0.0, pltpu.roll(wide, cols - 1, 0)).astype(BF16)
    earlier = jnp.where(place == 0, 0.0, pltpu.roll(wide, 1, 0)).astype(BF16)
    first, last = (earlier, later) if sign < 0 else (later, earlier)
    stack[slot, :, 0:channels] = first
    stack[slot, :, channels : 2 * channels] = row
    stack[slot, :, 2 * channels :] = last


def put_halo(stack, before, after, rows, peers, sign):
    here = lax.axis_index("space")
    zero = jnp.zeros(before.shape, BF16)
    put_shifted(stack, 0, jnp.where(here > 0, before, zero), sign)
    put_shifted(stack, rows + 1, jnp.where(here < peers - 1, after, zero), sign)


def merge_kernel(*refs):
    far, (merged, merged_t, stack, feat, out_w), near, sems = refs[:5], refs[5:10], refs[10:13], refs[13]
    near = (*near, feat, out_w)
    copies = [pltpu.make_async_copy(a, b, sems.at[i]) for i, (a, b) in enumerate(zip(far, near))]
    for copy in copies:
        copy.start()
    cot, lat_w, top = near[:3]
    rows, cols, channels = cot.shape
    half = cols // 2
    copies[0].wait()
    for r in range(rows):
        put_shifted(stack, r, cot[r], 1)
    for copy in copies[1:4]:
        copy.wait()
    upper = lax.broadcasted_iota(jnp.int32, (cols, half), 0)
    spread = jnp.where(upper // 2 == lax.broadcasted_iota(jnp.int32, (cols, half), 1), 1.0, 0.0).astype(BF16)
    lateral = jnp.dot(feat[...], lat_w[...], preferred_element_type=F32)
    for q in range(rows // 2):
        lifted = jnp.dot(spread, top[q], preferred_element_type=F32)
        for r in (2 * q, 2 * q + 1):
            merged[r * cols : (r + 1) * cols, :] = (lateral[r * cols : (r + 1) * cols] + lifted).astype(BF16)
    merged_t[...] = jnp.transpose(merged[...])
    copies[4].wait()


def strips_of(stack, halo):
    rows, cols, deep = stack.shape
    strips = [
        jnp.concatenate([stack[1:], halo[1:]], axis=0),
        stack[...],
        jnp.concatenate([halo[:1], stack[: rows - 1]], axis=0),
    ]
    return [strip.reshape(rows * cols, deep) for strip in strips]


def put_sums(outs, start, values):
    rows = slice(start, start + values.shape[0])
    if len(outs) == 1:
        outs[0][rows, :] = values
        return
    here = lax.axis_index("space")
    half = values.shape[1] // 2
    mine, theirs = outs
    mine[rows, :] = jnp.where(here == 0, values[:, :half], values[:, half:])
    theirs[rows, :] = jnp.where(here == 0, values[:, half:], values[:, :half]).astype(BF16)


def kernel_grad_kernel(stack, halo, merged_t, out):
    channels = merged_t.shape[0]
    for i, strip in enumerate(strips_of(stack, halo)):
        part = jnp.dot(merged_t[...], strip, preferred_element_type=F32)
        for j in range(3):
            start = (3 * i + j) * channels
            out[start : start + channels, :] = part[:, j * channels : (j + 1) * channels]


def pair_kernel_grad_kernel(stack, merged_t, cot, merged, out, image):
    here = lax.axis_index("space")
    rows, cols, channels = cot.shape
    half = channels // 2
    zero = jnp.zeros((1, cols, 3 * half), BF16)
    image[0:1] = zero
    image[2 * rows + 1 :] = zero
    own, other = 1 + rows * here, 1 + rows * (1 - here)
    for r in range(rows):
        row = cot[r]
        put_shifted(image, other + r, jnp.where(here == 0, row[:, :half], row[:, half:]), 1)
        for j in range(3):
            start = j * channels
            left, right = stack[r, :, start : start + half], stack[r, :, start + half : start + channels]
            image[own + r, :, j * half : (j + 1) * half] = jnp.where(here == 0, left, right)
    cells = []
    for first in (own, other):
        strips = [image[pl.ds(first + 1 - i, rows)].reshape(rows * cols, 3 * half) for i in range(3)]
        cells.append(jnp.concatenate(strips, axis=1))
    left = jnp.concatenate([merged_t[...], jnp.transpose(merged[...])], axis=1)
    part = jnp.dot(left, jnp.concatenate(cells, axis=0), preferred_element_type=F32)
    for tap in range(9):
        out[tap * channels : (tap + 1) * channels, :] = part[:, tap * half : (tap + 1) * half]


def data_grad_kernel(peers, stack, before, after, feat, out_w, grad, halo, *outs):
    put_halo(halo, before[before.shape[0] - 1], after[0], 0, peers, 1)
    cells = jnp.concatenate(strips_of(stack, halo), axis=1)
    taps = jnp.concatenate([out_w[tap] for tap in range(9)], axis=1)
    total = lax.dot_general(cells, taps, (((1,), (1,)), ((), ())), preferred_element_type=F32)
    grad[...] = total.astype(BF16)
    put_sums(outs, 0, jnp.dot(jnp.transpose(feat[...]), grad[...], preferred_element_type=F32))


def forward_kernel(peers, merged, out_w, grad, *refs):
    edges, (out, grad_top, stack, near, sem) = refs[:-5], refs[-5:]
    rows, cols, channels = merged.shape
    half = cols // 2
    for r in range(rows):
        put_shifted(stack, r + 1, merged[r], -1)
    put_halo(stack, edges[0][edges[0].shape[0] - 1], edges[1][0], rows, peers, -1)
    cells = jnp.concatenate([stack[i : i + rows].reshape(rows * cols, 3 * channels) for i in range(3)], axis=1)
    total = jnp.dot(cells, out_w[...].reshape(9 * channels, channels), preferred_element_type=F32)
    near[...] = total.astype(BF16).reshape(out.shape)
    copy = pltpu.make_async_copy(near, out, sem)
    copy.start()
    lower = lax.broadcasted_iota(jnp.int32, (half, 2 * cols), 1)
    lower = jnp.where(lower >= cols, lower - cols, lower)
    pool = jnp.where(lower // 2 == lax.broadcasted_iota(jnp.int32, (half, 2 * cols), 0), 1.0, 0.0).astype(BF16)
    for q in range(rows // 2):
        pair = grad[2 * q * cols : (2 * q + 2) * cols, :]
        grad_top[q] = jnp.dot(pool, pair, preferred_element_type=F32).astype(BF16)
    copy.wait()


def places():
    chip, core = lax.axis_index("dp"), lax.axis_index("space")
    plane, line = chip % 4, chip // 4
    return jnp.where(core == 0, plane, line), jnp.where(core == 0, line, plane)


def block(index, length):
    return pl.ds(pl.multiple_of(index * length, 16), length)


def cut_kernel(kernel_sums, mine, got, *refs):
    place, _ = places()
    edge, share = kernel_sums.shape[0] // 4, mine.shape[0] // 4
    for k, out in zip((0, 3, 2, 1), refs):
        out[:edge, :] = kernel_sums[block(place ^ k, edge), :].astype(out.dtype)
        rows = block(place ^ k, share)
        out[edge:, :] = (mine[rows, :] + got[rows, :].astype(F32)).astype(out.dtype)


def add_kernel(own, three, two, one, out):
    total = own[...] + one[...].astype(F32) + two[...].astype(F32) + three[...].astype(F32)
    out[...] = total.astype(BF16)


def finish_kernel(scale, own, three, two, one, _, out):
    near = own[...].astype(F32) + one[...].astype(F32)
    far = two[...].astype(F32) + three[...].astype(F32)
    out[...] = ((near + far) * scale).astype(BF16)


def place_kernel(pair, *refs):
    results, sems = refs[-3:-1], refs[-1]
    side = lax.axis_index("space")
    columns, place = (1 - side, places()[1]) if pair else (side, places()[0])
    lanes = pl.ds(pl.multiple_of(columns * 128, 128), 128)
    copies = []
    for k, quarter in zip((0, 3, 2, 1), refs):
        start = 0
        for result in results:
            share = result.shape[0] // 4
            to = result.at[block(place ^ k, share), lanes]
            copies.append(pltpu.make_async_copy(quarter.at[pl.ds(start, share), :], to, sems.at[len(copies)]))
            start += share
    for copy in copies:
        copy.start()
    for copy in copies:
        copy.wait()


def exchange(array, step, k):
    pairs = []
    for chip in range(16):
        for core in range(2):
            flip = k if core == step else 4 * k
            pairs.append((2 * chip + core, 2 * (chip ^ flip) + core))
    return lax.ppermute(array, ("dp", "space"), pairs)


def swap(array):
    return lax.ppermute(array, "space", [(0, 1), (1, 0)])


def call(kernel, *shapes, **more):
    return pl.pallas_call(
        kernel,
        out_shape=[jax.ShapeDtypeStruct(shape, kind) for shape, kind in shapes],
        compiler_params=pltpu.CompilerParams(vmem_limit_bytes=12 * 2**20),
        **more,
    )


def sum_everywhere(kernel_sums, lateral_part, scale, after):
    lengths, width = [kernel_sums.shape[0], lateral_part[0].shape[0]], kernel_sums.shape[1]
    vmem, far = pl.BlockSpec(memory_space=pltpu.VMEM), pl.BlockSpec(memory_space=pltpu.HBM)
    after = pltpu.with_memory_space_constraint(after, pltpu.HBM)
    quarter = (sum(lengths) // 4, width)
    own, *pieces = call(cut_kernel, (quarter, F32), *[(quarter, BF16)] * 3)(kernel_sums, *lateral_part)
    three, two, one = [exchange(piece, 0, k) for piece, k in zip(pieces, (3, 2, 1))]
    [total] = call(add_kernel, (quarter, BF16))(own, three, two, one)
    three, two, one = [exchange(total, 1, k) for k in (3, 2, 1)]
    finish = call(functools.partial(finish_kernel, scale), (quarter, BF16), in_specs=[vmem] * 4 + [far])
    [total] = finish(total, three, two, one, after)
    three, two, one = [exchange(total, 0, k) for k in (3, 2, 1)]
    quarters = [total, three, two, one]
    results = [((length, 2 * width), BF16) for length in lengths]
    place = dict(out_specs=[far] * 2, scratch_shapes=[pltpu.SemaphoreType.DMA((8,))])
    half = call(functools.partial(place_kernel, False), *results, **place)(*quarters)
    place.update(in_specs=[vmem] * 4 + [far] * 2, input_output_aliases={4: 0, 5: 1})
    return call(functools.partial(place_kernel, True), *results, **place)(*[swap(one) for one in quarters], *half)


def local(features, top_down, lateral_weight, out_kernel, cotangent):
    images, rows, cols, in_channels = features.shape
    channels = lateral_weight.shape[1]
    cells = rows * cols
    peers = lax.axis_size("space")
    taps = out_kernel.reshape(9, channels, channels)
    params = pltpu.CompilerParams(vmem_limit_bytes=32 * 2**20)
    halves = peers == 2 and lax.axis_size("dp") == 16 and images == 1 and (channels, in_channels) == (256, 512)

    def sums(length):
        if not halves:
            return [jax.ShapeDtypeStruct((length, channels), F32)]
        return [jax.ShapeDtypeStruct((length, channels // 2), kind) for kind in (F32, BF16)]

    outs, tops, parts = [], [], None
    for image in range(images):
        cot = cotangent[image]
        cot_before, cot_after = neighbour_rows(cot)
        arrays = (cot, lateral_weight, top_down[image], features[image].reshape(cells, in_channels), taps)
        arrays = [pltpu.with_memory_space_constraint(array, pltpu.HBM) for array in arrays]
        merged, merged_t, stack, near_feat, near_taps = pl.pallas_call(
            merge_kernel,
            out_shape=[
                jax.ShapeDtypeStruct(shape, BF16)
                for shape in (
                    (cells, channels),
                    (channels, cells),
                    (rows, cols, 3 * channels),
                    (cells, in_channels),
                    taps.shape,
                )
            ],
            in_specs=[pl.BlockSpec(memory_space=pltpu.HBM)] * 5,
            scratch_shapes=[*[pltpu.VMEM(array.shape, BF16) for array in arrays[:3]], pltpu.SemaphoreType.DMA((5,))],
            compiler_params=params,
            cost_estimate=pl.CostEstimate(
                flops=2 * cells * channels * 4 * in_channels, bytes_accessed=4 * 2**20, transcendentals=0
            ),
        )(*arrays)
        merged = merged.reshape(rows, cols, channels)
        edges = neighbour_rows(merged)
        grad, halo, *lateral_part = pl.pallas_call(
            functools.partial(data_grad_kernel, peers),
            out_shape=[
                jax.ShapeDtypeStruct((cells, channels), BF16),
                jax.ShapeDtypeStruct((2, cols, 3 * channels), BF16),
                *sums(in_channels),
            ],
            compiler_params=params,
            cost_estimate=pl.CostEstimate(
                flops=2 * cells * channels * (9 * channels + in_channels), bytes_accessed=4 * 2**20, transcendentals=0
            ),
        )(stack, cot_before, cot_after, near_feat, near_taps)
        kernel_cost = pl.CostEstimate(
            flops=2 * cells * channels * 9 * channels, bytes_accessed=4 * 2**20, transcendentals=0
        )
        if halves:
            lateral_part[1] = swap(lateral_part[1])
            kernel_sums = pl.pallas_call(
                pair_kernel_grad_kernel,
                out_shape=jax.ShapeDtypeStruct((9 * channels, channels // 2), F32),
                scratch_shapes=[pltpu.VMEM((2 * rows + 2, cols, 3 * channels // 2), BF16)],
                compiler_params=params,
                cost_estimate=kernel_cost,
            )(stack, merged_t, cot_after, edges[0].reshape(cells, channels))
        else:
            kernel_sums = pl.pallas_call(
                kernel_grad_kernel,
                out_shape=jax.ShapeDtypeStruct((9 * channels, channels), F32),
                compiler_params=params,
                cost_estimate=kernel_cost,
            )(stack, halo, merged_t)
        out, grad_top = pl.pallas_call(
            functools.partial(forward_kernel, peers),
            out_shape=[
                jax.ShapeDtypeStruct((rows, cols, channels), BF16),
                jax.ShapeDtypeStruct((rows // 2, cols // 2, channels), BF16),
            ],
            out_specs=[pl.BlockSpec(memory_space=pltpu.HBM), pl.BlockSpec(memory_space=pltpu.VMEM)],
            scratch_shapes=[
                pltpu.VMEM((rows + 2, cols, 3 * channels), BF16),
                pltpu.VMEM((rows, cols, channels), BF16),
                pltpu.SemaphoreType.DMA,
            ],
            compiler_params=params,
            cost_estimate=pl.CostEstimate(
                flops=2 * cells * channels * 9 * channels, bytes_accessed=2 * 2**20, transcendentals=0
            ),
        )(merged, near_taps, grad, *edges)
        outs.append(out)
        tops.append(grad_top)
        if not halves:
            part = [kernel_sums, lateral_part[0]]
            parts = part if parts is None else [a + b for a, b in zip(parts, part)]
    scale = 1.0 / (images * lax.axis_size("dp"))
    if halves:
        grad_kernel, grad_lateral = sum_everywhere(kernel_sums, lateral_part, scale, outs[0])
    else:
        grad_kernel, grad_lateral = [(total * scale).astype(BF16) for total in lax.psum(parts, ("dp", "space"))]
    return jnp.stack(outs), jnp.stack(tops), grad_kernel.reshape(out_kernel.shape), grad_lateral


def solution(mesh):
    return jax.shard_map(
        local,
        mesh=mesh,
        in_specs=(
            P("dp", "space", None, None),
            P("dp", "space", None, None),
            P(),
            P(),
            P("dp", "space", None, None),
        ),
        out_specs=(P("dp", "space", None, None), P("dp", "space", None, None), P(), P()),
        check_vma=False,
    )
```

```python
import functools

import jax
import jax.numpy as jnp
from jax import lax
from jax.experimental import pallas as pl
from jax.experimental.pallas import tpu as pltpu
from jax.sharding import PartitionSpec as P

F32 = jnp.float32
BF16 = jnp.bfloat16


def neighbour_rows(array):
    peers = lax.axis_size("space")
    if peers == 1:
        return array[-1:], array[:1]
    if peers == 2:
        got = lax.ppermute(array, "space", [(0, 1), (1, 0)])
        return got, got
    up = [(i, i + 1) for i in range(peers - 1)]
    down = [(j, i) for i, j in up]
    return lax.ppermute(array[-1:], "space", up), lax.ppermute(array[:1], "space", down)


def put_shifted(stack, slot, row, sign, pad):
    cols, channels = row.shape
    zero = jnp.zeros((8, channels), F32)
    pad[0:8, :] = zero
    pad[8 + cols :, :] = zero
    pad[8 : 8 + cols, :] = row.astype(F32)
    earlier, later = pad[7 : 7 + cols, :].astype(BF16), pad[9 : 9 + cols, :].astype(BF16)
    first, last = (earlier, later) if sign < 0 else (later, earlier)
    stack[slot, :, 0:channels] = first
    stack[slot, :, channels : 2 * channels] = row
    stack[slot, :, 2 * channels :] = last


def put_halo(stack, before, after, rows, peers, sign, pads):
    here = lax.axis_index("space")
    zero = jnp.zeros(before.shape, BF16)
    put_shifted(stack, 0, jnp.where(here > 0, before, zero), sign, pads.at[0])
    put_shifted(stack, rows + 1, jnp.where(here < peers - 1, after, zero), sign, pads.at[1])


def merge_kernel(*refs):
    far, (merged, merged_t, stack, feat, out_w), near, pads, sems = refs[:5], refs[5:10], refs[10:13], refs[13], refs[14]
    cot_far, lat_far, top_far, feat_far, taps_far = far
    cot, lat_w, top = near
    rows, cols, channels = cot.shape
    half, cells = cols // 2, rows * cols
    upper_cells, lower_cells = pl.ds(0, cells // 2), pl.ds(cells // 2, cells // 2)
    moves = [
        (cot_far, cot),
        (lat_far, lat_w),
        (feat_far.at[upper_cells, :], feat.at[upper_cells, :]),
        (top_far, top),
        (feat_far.at[lower_cells, :], feat.at[lower_cells, :]),
        (taps_far, out_w),
    ]
    copies = [pltpu.make_async_copy(a, b, sems.at[i]) for i, (a, b) in enumerate(moves)]
    for copy in copies:
        copy.start()
    upper = lax.broadcasted_iota(jnp.int32, (cols, half), 0)
    spread = jnp.where(upper // 2 == lax.broadcasted_iota(jnp.int32, (cols, half), 1), 1.0, 0.0).astype(BF16)
    copies[0].wait()
    for r in range(rows):
        put_shifted(stack, r, cot[r], 1, pads.at[r])
    for part, needed in ((0, copies[1:4]), (1, copies[4:5])):
        for copy in needed:
            copy.wait()
        start = part * cells // 2
        lateral = jnp.dot(feat[start : start + cells // 2, :], lat_w[...], preferred_element_type=F32)
        for q in range(rows // 4):
            lifted = jnp.dot(spread, top[part * rows // 4 + q], preferred_element_type=F32)
            for r in (2 * q, 2 * q + 1):
                merged[start + r * cols : start + (r + 1) * cols, :] = (
                    lateral[r * cols : (r + 1) * cols] + lifted
                ).astype(BF16)
        merged_t[:, start : start + cells // 2] = jnp.transpose(merged[start : start + cells // 2, :])
    copies[5].wait()


def strips_of(stack, halo):
    rows, cols, deep = stack.shape
    strips = [
        jnp.concatenate([stack[1:], halo[1:]], axis=0),
        stack[...],
        jnp.concatenate([halo[:1], stack[: rows - 1]], axis=0),
    ]
    return [strip.reshape(rows * cols, deep) for strip in strips]


def put_sums(outs, start, values):
    rows = slice(start, start + values.shape[0])
    if len(outs) == 1:
        outs[0][rows, :] = values
        return
    here = lax.axis_index("space")
    half = values.shape[1] // 2
    mine, theirs = outs
    mine[rows, :] = jnp.where(here == 0, values[:, :half], values[:, half:])
    theirs[rows, :] = jnp.where(here == 0, values[:, half:], values[:, :half]).astype(BF16)


def kernel_grad_kernel(stack, halo, merged_t, out):
    channels = merged_t.shape[0]
    for i, strip in enumerate(strips_of(stack, halo)):
        part = jnp.dot(merged_t[...], strip, preferred_element_type=F32)
        for j in range(3):
            start = (3 * i + j) * channels
            out[start : start + channels, :] = part[:, j * channels : (j + 1) * channels]


def pair_kernel_grad_kernel(stack, merged_t, cot, merged, out, image, pads):
    here = lax.axis_index("space")
    rows, cols, channels = cot.shape
    half = channels // 2
    zero = jnp.zeros((1, cols, 3 * half), BF16)
    image[0:1] = zero
    image[2 * rows + 1 :] = zero
    own, other = 1 + rows * here, 1 + rows * (1 - here)
    for r in range(rows):
        row = cot[r]
        put_shifted(image, other + r, jnp.where(here == 0, row[:, :half], row[:, half:]), 1, pads.at[r])
        for j in range(3):
            start = j * channels
            left, right = stack[r, :, start : start + half], stack[r, :, start + half : start + channels]
            image[own + r, :, j * half : (j + 1) * half] = jnp.where(here == 0, left, right)
    cells = []
    for first in (own, other):
        strips = [image[pl.ds(first + 1 - i, rows)].reshape(rows * cols, 3 * half) for i in range(3)]
        cells.append(jnp.concatenate(strips, axis=1))
    left = jnp.concatenate([merged_t[...], jnp.transpose(merged[...])], axis=1)
    part = jnp.dot(left, jnp.concatenate(cells, axis=0), preferred_element_type=F32)
    for tap in range(9):
        out[tap * channels : (tap + 1) * channels, :] = part[:, tap * half : (tap + 1) * half]


def data_grad_kernel(peers, stack, before, after, feat, out_w, grad, halo, *refs):
    outs, edge_pads = refs[:-1], refs[-1]
    put_halo(halo, before[before.shape[0] - 1], after[0], 0, peers, 1, edge_pads)
    cells = jnp.concatenate(strips_of(stack, halo), axis=1)
    taps = jnp.concatenate([out_w[tap] for tap in range(9)], axis=1)
    total = lax.dot_general(cells, taps, (((1,), (1,)), ((), ())), preferred_element_type=F32)
    grad[...] = total.astype(BF16)
    put_sums(outs, 0, jnp.dot(jnp.transpose(feat[...]), grad[...], preferred_element_type=F32))


def forward_kernel(peers, merged, out_w, grad, *refs):
    edges, (out, grad_top, stack, near, row_pads, sem) = refs[:-6], refs[-6:]
    rows, cols, channels = merged.shape
    half = cols // 2
    for r in range(rows):
        put_shifted(stack, r + 1, merged[r], -1, row_pads.at[r])
    put_halo(stack, edges[0][edges[0].shape[0] - 1], edges[1][0], rows, peers, -1, row_pads.at[pl.ds(rows, 2)])
    cells = jnp.concatenate([stack[i : i + rows].reshape(rows * cols, 3 * channels) for i in range(3)], axis=1)
    total = jnp.dot(cells, out_w[...].reshape(9 * channels, channels), preferred_element_type=F32)
    near[...] = total.astype(BF16).reshape(out.shape)
    copy = pltpu.make_async_copy(near, out, sem)
    copy.start()
    lower = lax.broadcasted_iota(jnp.int32, (half, 2 * cols), 1)
    lower = jnp.where(lower >= cols, lower - cols, lower)
    pool = jnp.where(lower // 2 == lax.broadcasted_iota(jnp.int32, (half, 2 * cols), 0), 1.0, 0.0).astype(BF16)
    for q in range(rows // 2):
        pair = grad[2 * q * cols : (2 * q + 2) * cols, :]
        grad_top[q] = jnp.dot(pool, pair, preferred_element_type=F32).astype(BF16)
    copy.wait()


def places():
    chip, core = lax.axis_index("dp"), lax.axis_index("space")
    plane, line = chip % 4, chip // 4
    return jnp.where(core == 0, plane, line), jnp.where(core == 0, line, plane)


def block(index, length):
    return pl.ds(pl.multiple_of(index * length, 16), length)


def cut_kernel(kernel_sums, mine, got, *refs):
    place, _ = places()
    edge, share = kernel_sums.shape[0] // 4, mine.shape[0] // 4
    for k, out in zip((0, 3, 2, 1), refs):
        out[:edge, :] = kernel_sums[block(place ^ k, edge), :].astype(out.dtype)
        rows = block(place ^ k, share)
        out[edge:, :] = (mine[rows, :] + got[rows, :].astype(F32)).astype(out.dtype)


def add_kernel(own, three, two, one, out):
    total = own[...] + one[...].astype(F32) + two[...].astype(F32) + three[...].astype(F32)
    out[...] = total.astype(BF16)


def finish_kernel(scale, own, three, two, one, _, out):
    near = own[...].astype(F32) + one[...].astype(F32)
    far = two[...].astype(F32) + three[...].astype(F32)
    out[...] = ((near + far) * scale).astype(BF16)


def place_kernel(pair, *refs):
    results, sems = refs[-3:-1], refs[-1]
    side = lax.axis_index("space")
    columns, place = (1 - side, places()[1]) if pair else (side, places()[0])
    lanes = pl.ds(pl.multiple_of(columns * 128, 128), 128)
    copies = []
    for k, quarter in zip((0, 3, 2, 1), refs):
        start = 0
        for result in results:
            share = result.shape[0] // 4
            to = result.at[block(place ^ k, share), lanes]
            copies.append(pltpu.make_async_copy(quarter.at[pl.ds(start, share), :], to, sems.at[len(copies)]))
            start += share
    for copy in copies:
        copy.start()
    for copy in copies:
        copy.wait()


def exchange(array, step, k):
    pairs = []
    for chip in range(16):
        for core in range(2):
            flip = k if core == step else 4 * k
            pairs.append((2 * chip + core, 2 * (chip ^ flip) + core))
    return lax.ppermute(array, ("dp", "space"), pairs)


def swap(array):
    return lax.ppermute(array, "space", [(0, 1), (1, 0)])


def call(kernel, *shapes, **more):
    return pl.pallas_call(
        kernel,
        out_shape=[jax.ShapeDtypeStruct(shape, kind) for shape, kind in shapes],
        compiler_params=pltpu.CompilerParams(vmem_limit_bytes=12 * 2**20),
        **more,
    )


def sum_everywhere(kernel_sums, lateral_part, scale, after):
    lengths, width = [kernel_sums.shape[0], lateral_part[0].shape[0]], kernel_sums.shape[1]
    vmem, far = pl.BlockSpec(memory_space=pltpu.VMEM), pl.BlockSpec(memory_space=pltpu.HBM)
    after = pltpu.with_memory_space_constraint(after, pltpu.HBM)
    quarter = (sum(lengths) // 4, width)
    own, *pieces = call(cut_kernel, (quarter, F32), *[(quarter, BF16)] * 3)(kernel_sums, *lateral_part)
    three, two, one = [exchange(piece, 0, k) for piece, k in zip(pieces, (3, 2, 1))]
    [total] = call(add_kernel, (quarter, BF16))(own, three, two, one)
    three, two, one = [exchange(total, 1, k) for k in (3, 2, 1)]
    finish = call(functools.partial(finish_kernel, scale), (quarter, BF16), in_specs=[vmem] * 4 + [far])
    [total] = finish(total, three, two, one, after)
    three, two, one = [exchange(total, 0, k) for k in (3, 2, 1)]
    quarters = [total, three, two, one]
    results = [((length, 2 * width), BF16) for length in lengths]
    place = dict(out_specs=[far] * 2, scratch_shapes=[pltpu.SemaphoreType.DMA((8,))])
    half = call(functools.partial(place_kernel, False), *results, **place)(*quarters)
    place.update(in_specs=[vmem] * 4 + [far] * 2, input_output_aliases={4: 0, 5: 1})
    return call(functools.partial(place_kernel, True), *results, **place)(*[swap(one) for one in quarters], *half)


def local(features, top_down, lateral_weight, out_kernel, cotangent):
    images, rows, cols, in_channels = features.shape
    channels = lateral_weight.shape[1]
    cells = rows * cols
    peers = lax.axis_size("space")
    taps = out_kernel.reshape(9, channels, channels)
    params = pltpu.CompilerParams(vmem_limit_bytes=32 * 2**20)
    halves = peers == 2 and lax.axis_size("dp") == 16 and images == 1 and (channels, in_channels) == (256, 512)

    def sums(length):
        if not halves:
            return [jax.ShapeDtypeStruct((length, channels), F32)]
        return [jax.ShapeDtypeStruct((length, channels // 2), kind) for kind in (F32, BF16)]

    def pads(count, width):
        return pltpu.VMEM((count, cols + 16, width), F32)

    outs, tops, parts = [], [], None
    for image in range(images):
        cot = cotangent[image]
        cot_before, cot_after = neighbour_rows(cot)
        arrays = (cot, lateral_weight, top_down[image], features[image].reshape(cells, in_channels), taps)
        arrays = [pltpu.with_memory_space_constraint(array, pltpu.HBM) for array in arrays]
        merged, merged_t, stack, near_feat, near_taps = pl.pallas_call(
            merge_kernel,
            out_shape=[
                jax.ShapeDtypeStruct(shape, BF16)
                for shape in (
                    (cells, channels),
                    (channels, cells),
                    (rows, cols, 3 * channels),
                    (cells, in_channels),
                    taps.shape,
                )
            ],
            in_specs=[pl.BlockSpec(memory_space=pltpu.HBM)] * 5,
            scratch_shapes=[*[pltpu.VMEM(array.shape, BF16) for array in arrays[:3]], pads(rows, channels), pltpu.SemaphoreType.DMA((6,))],
            compiler_params=params,
            cost_estimate=pl.CostEstimate(
                flops=2 * cells * channels * 4 * in_channels, bytes_accessed=4 * 2**20, transcendentals=0
            ),
        )(*arrays)
        merged = merged.reshape(rows, cols, channels)
        edges = neighbour_rows(merged)
        grad, halo, *lateral_part = pl.pallas_call(
            functools.partial(data_grad_kernel, peers),
            out_shape=[
                jax.ShapeDtypeStruct((cells, channels), BF16),
                jax.ShapeDtypeStruct((2, cols, 3 * channels), BF16),
                *sums(in_channels),
            ],
            scratch_shapes=[pads(2, channels)],
            compiler_params=params,
            cost_estimate=pl.CostEstimate(
                flops=2 * cells * channels * (9 * channels + in_channels), bytes_accessed=4 * 2**20, transcendentals=0
            ),
        )(stack, cot_before, cot_after, near_feat, near_taps)
        kernel_cost = pl.CostEstimate(
            flops=2 * cells * channels * 9 * channels, bytes_accessed=4 * 2**20, transcendentals=0
        )
        if halves:
            lateral_part[1] = swap(lateral_part[1])
            kernel_sums = pl.pallas_call(
                pair_kernel_grad_kernel,
                out_shape=jax.ShapeDtypeStruct((9 * channels, channels // 2), F32),
                scratch_shapes=[
                    pltpu.VMEM((2 * rows + 2, cols, 3 * channels // 2), BF16),
                    pads(rows, channels // 2),
                ],
                compiler_params=params,
                cost_estimate=kernel_cost,
            )(stack, merged_t, cot_after, edges[0].reshape(cells, channels))
        else:
            kernel_sums = pl.pallas_call(
                kernel_grad_kernel,
                out_shape=jax.ShapeDtypeStruct((9 * channels, channels), F32),
                compiler_params=params,
                cost_estimate=kernel_cost,
            )(stack, halo, merged_t)
        out, grad_top = pl.pallas_call(
            functools.partial(forward_kernel, peers),
            out_shape=[
                jax.ShapeDtypeStruct((rows, cols, channels), BF16),
                jax.ShapeDtypeStruct((rows // 2, cols // 2, channels), BF16),
            ],
            out_specs=[pl.BlockSpec(memory_space=pltpu.HBM), pl.BlockSpec(memory_space=pltpu.VMEM)],
            scratch_shapes=[
                pltpu.VMEM((rows + 2, cols, 3 * channels), BF16),
                pltpu.VMEM((rows, cols, channels), BF16),
                pads(rows + 2, channels),
                pltpu.SemaphoreType.DMA,
            ],
            compiler_params=params,
            cost_estimate=pl.CostEstimate(
                flops=2 * cells * channels * 9 * channels, bytes_accessed=2 * 2**20, transcendentals=0
            ),
        )(merged, near_taps, grad, *edges)
        outs.append(out)
        tops.append(grad_top)
        if not halves:
            part = [kernel_sums, lateral_part[0]]
            parts = part if parts is None else [a + b for a, b in zip(parts, part)]
    scale = 1.0 / (images * lax.axis_size("dp"))
    if halves:
        grad_kernel, grad_lateral = sum_everywhere(kernel_sums, lateral_part, scale, outs[0])
    else:
        grad_kernel, grad_lateral = [(total * scale).astype(BF16) for total in lax.psum(parts, ("dp", "space"))]
    return jnp.stack(outs), jnp.stack(tops), grad_kernel.reshape(out_kernel.shape), grad_lateral


def solution(mesh):
    return jax.shard_map(
        local,
        mesh=mesh,
        in_specs=(
            P("dp", "space", None, None),
            P("dp", "space", None, None),
            P(),
            P(),
            P("dp", "space", None, None),
        ),
        out_specs=(P("dp", "space", None, None), P("dp", "space", None, None), P(), P()),
        check_vma=False,
    )
```

```python
import functools

import jax
import jax.numpy as jnp
from jax import lax
from jax.experimental import pallas as pl
from jax.experimental.pallas import tpu as pltpu
from jax.sharding import PartitionSpec as P

F32 = jnp.float32
BF16 = jnp.bfloat16


def neighbour_rows(array):
    peers = lax.axis_size("space")
    if peers == 1:
        return array[-1:], array[:1]
    if peers == 2:
        got = lax.ppermute(array, "space", [(0, 1), (1, 0)])
        return got, got
    up = [(i, i + 1) for i in range(peers - 1)]
    down = [(j, i) for i, j in up]
    return lax.ppermute(array[-1:], "space", up), lax.ppermute(array[:1], "space", down)


def put_shifted(stack, slot, row, sign):
    cols, channels = row.shape
    wide = row.astype(F32)
    place = lax.broadcasted_iota(jnp.int32, (cols, channels), 0)
    later = jnp.where(place == cols - 1, 0.0, pltpu.roll(wide, cols - 1, 0)).astype(BF16)
    earlier = jnp.where(place == 0, 0.0, pltpu.roll(wide, 1, 0)).astype(BF16)
    first, last = (earlier, later) if sign < 0 else (later, earlier)
    stack[slot, :, 0:channels] = first
    stack[slot, :, channels : 2 * channels] = row
    stack[slot, :, 2 * channels :] = last


def put_halo(stack, before, after, rows, peers, sign):
    here = lax.axis_index("space")
    zero = jnp.zeros(before.shape, BF16)
    put_shifted(stack, 0, jnp.where(here > 0, before, zero), sign)
    put_shifted(stack, rows + 1, jnp.where(here < peers - 1, after, zero), sign)


def merge_kernel(*refs):
    far, (merged, merged_t, stack, feat, out_w), near, sems = refs[:5], refs[5:10], refs[10:13], refs[13]
    near = (*near, feat, out_w)
    copies = [pltpu.make_async_copy(a, b, sems.at[i]) for i, (a, b) in enumerate(zip(far, near))]
    for copy in copies:
        copy.start()
    cot, lat_w, top = near[:3]
    rows, cols, channels = cot.shape
    half = cols // 2
    copies[0].wait()
    for r in range(rows):
        put_shifted(stack, r, cot[r], 1)
    for copy in copies[1:4]:
        copy.wait()
    upper = lax.broadcasted_iota(jnp.int32, (cols, half), 0)
    spread = jnp.where(upper // 2 == lax.broadcasted_iota(jnp.int32, (cols, half), 1), 1.0, 0.0).astype(BF16)
    lateral = jnp.dot(feat[...], lat_w[...], preferred_element_type=F32)
    for q in range(rows // 2):
        lifted = jnp.dot(spread, top[q], preferred_element_type=F32)
        for r in (2 * q, 2 * q + 1):
            merged[r * cols : (r + 1) * cols, :] = (lateral[r * cols : (r + 1) * cols] + lifted).astype(BF16)
    merged_t[...] = jnp.transpose(merged[...])
    copies[4].wait()


def strips_of(stack, halo):
    rows, cols, deep = stack.shape
    strips = [
        jnp.concatenate([stack[1:], halo[1:]], axis=0),
        stack[...],
        jnp.concatenate([halo[:1], stack[: rows - 1]], axis=0),
    ]
    return [strip.reshape(rows * cols, deep) for strip in strips]


def put_sums(outs, start, values):
    rows = slice(start, start + values.shape[0])
    if len(outs) == 1:
        outs[0][rows, :] = values
        return
    here = lax.axis_index("space")
    half = values.shape[1] // 2
    mine, theirs = outs
    mine[rows, :] = jnp.where(here == 0, values[:, :half], values[:, half:])
    theirs[rows, :] = jnp.where(here == 0, values[:, half:], values[:, :half]).astype(BF16)


def kernel_grad_kernel(stack, halo, merged_t, out):
    channels = merged_t.shape[0]
    for i, strip in enumerate(strips_of(stack, halo)):
        part = jnp.dot(merged_t[...], strip, preferred_element_type=F32)
        for j in range(3):
            start = (3 * i + j) * channels
            out[start : start + channels, :] = part[:, j * channels : (j + 1) * channels]


def cells_of(image, first, rows):
    strips = [image[pl.ds(first + 1 - i, rows)] for i in range(3)]
    return jnp.concatenate([strip.reshape(-1, strip.shape[-1]) for strip in strips], axis=1)


def own_kernel_grad_kernel(stack, merged_t, cot, image, sums):
    here = lax.axis_index("space")
    rows, cols, channels = cot.shape
    half = channels // 2
    zero = jnp.zeros((1, cols, 3 * half), BF16)
    image[0:1] = zero
    image[2 * rows + 1 :] = zero
    own, other = 1 + rows * here, 1 + rows * (1 - here)
    for r in range(rows):
        row = cot[r]
        put_shifted(image, other + r, jnp.where(here == 0, row[:, :half], row[:, half:]), 1)
        for j in range(3):
            start = j * channels
            left, right = stack[r, :, start : start + half], stack[r, :, start + half : start + channels]
            image[own + r, :, j * half : (j + 1) * half] = jnp.where(here == 0, left, right)
    sums[...] = jnp.dot(merged_t[...], cells_of(image, own, rows), preferred_element_type=F32)


def rest_kernel_grad_kernel(image, sums, merged, *refs):
    outs, total = refs[:4], refs[4]
    here, (place, _) = lax.axis_index("space"), places()
    channels, half = merged.shape[1], total.shape[1]
    rows = (image.shape[0] - 2) // 2
    cells = cells_of(image, 1 + rows * (1 - here), rows)
    part = sums[...] + jnp.dot(jnp.transpose(merged[...]), cells, preferred_element_type=F32)
    for tap in range(9):
        total[tap * channels : (tap + 1) * channels, :] = part[:, tap * half : (tap + 1) * half]
    for k, out in zip((0, 3, 2, 1), outs):
        out[...] = total[block(place ^ k, out.shape[0]), :].astype(out.dtype)


def data_grad_kernel(peers, waits, stack, before, after, feat, out_w, *refs):
    grad, halo, *outs = refs[waits:]
    put_halo(halo, before[before.shape[0] - 1], after[0], 0, peers, 1)
    cells = jnp.concatenate(strips_of(stack, halo), axis=1)
    taps = jnp.concatenate([out_w[tap] for tap in range(9)], axis=1)
    total = lax.dot_general(cells, taps, (((1,), (1,)), ((), ())), preferred_element_type=F32)
    grad[...] = total.astype(BF16)
    put_sums(outs, 0, jnp.dot(jnp.transpose(feat[...]), grad[...], preferred_element_type=F32))


def forward_kernel(peers, merged, out_w, grad, *refs):
    edges, (out, grad_top, stack, near, sem) = refs[:-5], refs[-5:]
    rows, cols, channels = merged.shape
    half = cols // 2
    for r in range(rows):
        put_shifted(stack, r + 1, merged[r], -1)
    put_halo(stack, edges[0][edges[0].shape[0] - 1], edges[1][0], rows, peers, -1)
    cells = jnp.concatenate([stack[i : i + rows].reshape(rows * cols, 3 * channels) for i in range(3)], axis=1)
    total = jnp.dot(cells, out_w[...].reshape(9 * channels, channels), preferred_element_type=F32)
    near[...] = total.astype(BF16).reshape(out.shape)
    copy = pltpu.make_async_copy(near, out, sem)
    copy.start()
    lower = lax.broadcasted_iota(jnp.int32, (half, 2 * cols), 1)
    lower = jnp.where(lower >= cols, lower - cols, lower)
    pool = jnp.where(lower // 2 == lax.broadcasted_iota(jnp.int32, (half, 2 * cols), 0), 1.0, 0.0).astype(BF16)
    for q in range(rows // 2):
        pair = grad[2 * q * cols : (2 * q + 2) * cols, :]
        grad_top[q] = jnp.dot(pool, pair, preferred_element_type=F32).astype(BF16)
    copy.wait()


def places():
    chip, core = lax.axis_index("dp"), lax.axis_index("space")
    plane, line = chip % 4, chip // 4
    return jnp.where(core == 0, plane, line), jnp.where(core == 0, line, plane)


def block(index, length):
    return pl.ds(pl.multiple_of(index * length, 16), length)


def add_kernel(own, three, two, one, out):
    total = own[...] + one[...].astype(F32) + two[...].astype(F32) + three[...].astype(F32)
    out[...] = total.astype(BF16)


def finish_kernel(scale, own, three, two, one, _, out):
    near = own[...].astype(F32) + one[...].astype(F32)
    far = two[...].astype(F32) + three[...].astype(F32)
    out[...] = ((near + far) * scale).astype(BF16)


def place_kernel(pair, *refs):
    result, sems = refs[-2:]
    side = lax.axis_index("space")
    columns, place = (1 - side, places()[1]) if pair else (side, places()[0])
    lanes = pl.ds(pl.multiple_of(columns * 128, 128), 128)
    share = result.shape[0] // 8
    copies = []
    for k, quarter in zip((0, 3, 2, 1), refs):
        for part in range(2):
            to = result.at[block(2 * (place ^ k) + part, share), lanes]
            copies.append(pltpu.make_async_copy(quarter.at[pl.ds(part * share, share), :], to, sems.at[len(copies)]))
    for copy in copies:
        copy.start()
    for copy in copies:
        copy.wait()


def place_lateral_kernel(mine, other, result, sems):
    side = lax.axis_index("space")
    copies = []
    for columns, half in ((side, mine), (1 - side, other)):
        lanes = pl.ds(pl.multiple_of(columns * 128, 128), 128)
        copies.append(pltpu.make_async_copy(half, result.at[:, lanes], sems.at[len(copies)]))
    for copy in copies:
        copy.start()
    for copy in copies:
        copy.wait()


def exchange(array, step, k):
    pairs = []
    for chip in range(16):
        for core in range(2):
            flip = k if core == step else 4 * k
            pairs.append((2 * chip + core, 2 * (chip ^ flip) + core))
    return lax.ppermute(array, ("dp", "space"), pairs)


def swap(array):
    return lax.ppermute(array, "space", [(0, 1), (1, 0)])


def call(kernel, *shapes, **more):
    return pl.pallas_call(
        kernel,
        out_shape=[jax.ShapeDtypeStruct(shape, kind) for shape, kind in shapes],
        compiler_params=pltpu.CompilerParams(vmem_limit_bytes=12 * 2**20),
        **more,
    )


def sum_lateral(mine, got, scale):
    length, width = mine.shape
    plane = [[2 * (4 * z + q) + core for q in range(4)] for z in range(4) for core in range(2)]
    line = [[2 * (4 * z + q) + core for z in range(4)] for q in range(4) for core in range(2)]
    total = mine + got.astype(F32)
    for groups in (plane, line):
        total = lax.psum(total, ("dp", "space"), axis_index_groups=groups)
    total = (total * scale).astype(BF16)
    [result] = call(
        place_lateral_kernel,
        ((length, 2 * width), BF16),
        out_specs=[pl.BlockSpec(memory_space=pltpu.HBM)],
        scratch_shapes=[pltpu.SemaphoreType.DMA((2,))],
    )(total, swap(total))
    return result


def sum_kernel(pieces, scale, after):
    own, *pieces = pieces
    quarter = own.shape
    vmem, far = pl.BlockSpec(memory_space=pltpu.VMEM), pl.BlockSpec(memory_space=pltpu.HBM)
    after = pltpu.with_memory_space_constraint(after, pltpu.HBM)
    three, two, one = [exchange(piece, 0, k) for piece, k in zip(pieces, (3, 2, 1))]
    slow = pl.CostEstimate(flops=2**32, bytes_accessed=2**10, transcendentals=0)
    [total] = call(add_kernel, (quarter, BF16), cost_estimate=slow)(own, three, two, one)
    three, two, one = [exchange(total, 1, k) for k in (3, 2, 1)]
    finish = call(functools.partial(finish_kernel, scale), (quarter, BF16), in_specs=[vmem] * 4 + [far])
    [total] = finish(total, three, two, one, after)
    three, two, one = [exchange(total, 0, k) for k in (3, 2, 1)]
    quarters = [total, three, two, one]
    result = ((4 * quarter[0], 2 * quarter[1]), BF16)
    place = dict(out_specs=[far], scratch_shapes=[pltpu.SemaphoreType.DMA((8,))])
    [half] = call(functools.partial(place_kernel, False), result, **place)(*quarters)
    place.update(in_specs=[vmem] * 4 + [far], input_output_aliases={4: 0})
    [whole] = call(functools.partial(place_kernel, True), result, **place)(*[swap(one) for one in quarters], half)
    return whole


def local(features, top_down, lateral_weight, out_kernel, cotangent):
    images, rows, cols, in_channels = features.shape
    channels = lateral_weight.shape[1]
    cells = rows * cols
    peers = lax.axis_size("space")
    taps = out_kernel.reshape(9, channels, channels)
    params = pltpu.CompilerParams(vmem_limit_bytes=32 * 2**20)
    halves = peers == 2 and lax.axis_size("dp") == 16 and images == 1 and (channels, in_channels) == (256, 512)

    def sums(length):
        if not halves:
            return [jax.ShapeDtypeStruct((length, channels), F32)]
        return [jax.ShapeDtypeStruct((length, channels // 2), kind) for kind in (F32, BF16)]

    outs, tops, parts = [], [], None
    for image in range(images):
        cot = cotangent[image]
        cot_before, cot_after = neighbour_rows(cot)
        arrays = (cot, lateral_weight, top_down[image], features[image].reshape(cells, in_channels), taps)
        arrays = [pltpu.with_memory_space_constraint(array, pltpu.HBM) for array in arrays]
        merged, merged_t, stack, near_feat, near_taps = pl.pallas_call(
            merge_kernel,
            out_shape=[
                jax.ShapeDtypeStruct(shape, BF16)
                for shape in (
                    (cells, channels),
                    (channels, cells),
                    (rows, cols, 3 * channels),
                    (cells, in_channels),
                    taps.shape,
                )
            ],
            in_specs=[pl.BlockSpec(memory_space=pltpu.HBM)] * 5,
            scratch_shapes=[*[pltpu.VMEM(array.shape, BF16) for array in arrays[:3]], pltpu.SemaphoreType.DMA((5,))],
            compiler_params=params,
            cost_estimate=pl.CostEstimate(
                flops=2 * cells * channels * 4 * in_channels, bytes_accessed=4 * 2**20, transcendentals=0
            ),
        )(*arrays)
        merged = merged.reshape(rows, cols, channels)
        edges = neighbour_rows(merged)
        kernel_flops = 2 * cells * channels * 9 * channels
        waited = []
        if halves:
            half, quarter = channels // 2, (9 * channels // 4, channels // 2)
            image_shape = (2 * rows + 2, cols, 3 * half)
            cost = pl.CostEstimate(flops=kernel_flops // 2, bytes_accessed=2**20, transcendentals=0)
            image, first_sums = pl.pallas_call(
                own_kernel_grad_kernel,
                out_shape=[
                    jax.ShapeDtypeStruct(image_shape, BF16),
                    jax.ShapeDtypeStruct((channels, 9 * half), F32),
                ],
                compiler_params=params,
                cost_estimate=cost,
            )(stack, merged_t, cot_after)
            pieces = pl.pallas_call(
                rest_kernel_grad_kernel,
                out_shape=[jax.ShapeDtypeStruct(quarter, F32), *[jax.ShapeDtypeStruct(quarter, BF16)] * 3],
                scratch_shapes=[pltpu.VMEM((9 * channels, half), F32)],
                compiler_params=params,
                cost_estimate=cost,
            )(image, first_sums, edges[0].reshape(cells, channels))
            waited = [pieces[0]]
        grad, halo, *lateral_part = pl.pallas_call(
            functools.partial(data_grad_kernel, peers, len(waited)),
            out_shape=[
                jax.ShapeDtypeStruct((cells, channels), BF16),
                jax.ShapeDtypeStruct((2, cols, 3 * channels), BF16),
                *sums(in_channels),
            ],
            compiler_params=params,
            cost_estimate=pl.CostEstimate(
                flops=2 * cells * channels * (9 * channels + in_channels), bytes_accessed=4 * 2**20, transcendentals=0
            ),
        )(stack, cot_before, cot_after, near_feat, near_taps, *waited)
        if halves:
            lateral_part[1] = swap(lateral_part[1])
        else:
            kernel_sums = pl.pallas_call(
                kernel_grad_kernel,
                out_shape=jax.ShapeDtypeStruct((9 * channels, channels), F32),
                compiler_params=params,
                cost_estimate=pl.CostEstimate(flops=kernel_flops, bytes_accessed=4 * 2**20, transcendentals=0),
            )(stack, halo, merged_t)
        out, grad_top = pl.pallas_call(
            functools.partial(forward_kernel, peers),
            out_shape=[
                jax.ShapeDtypeStruct((rows, cols, channels), BF16),
                jax.ShapeDtypeStruct((rows // 2, cols // 2, channels), BF16),
            ],
            out_specs=[pl.BlockSpec(memory_space=pltpu.HBM), pl.BlockSpec(memory_space=pltpu.VMEM)],
            scratch_shapes=[
                pltpu.VMEM((rows + 2, cols, 3 * channels), BF16),
                pltpu.VMEM((rows, cols, channels), BF16),
                pltpu.SemaphoreType.DMA,
            ],
            compiler_params=params,
            cost_estimate=pl.CostEstimate(
                flops=2 * cells * channels * 9 * channels, bytes_accessed=2 * 2**20, transcendentals=0
            ),
        )(merged, near_taps, grad, *edges)
        outs.append(out)
        tops.append(grad_top)
        if not halves:
            part = [kernel_sums, lateral_part[0]]
            parts = part if parts is None else [a + b for a, b in zip(parts, part)]
    scale = 1.0 / (images * lax.axis_size("dp"))
    if halves:
        grad_kernel = sum_kernel(pieces, scale, outs[0])
        grad_lateral = sum_lateral(*lateral_part, scale)
    else:
        grad_kernel, grad_lateral = [(total * scale).astype(BF16) for total in lax.psum(parts, ("dp", "space"))]
    return jnp.stack(outs), jnp.stack(tops), grad_kernel.reshape(out_kernel.shape), grad_lateral


def solution(mesh):
    return jax.shard_map(
        local,
        mesh=mesh,
        in_specs=(
            P("dp", "space", None, None),
            P("dp", "space", None, None),
            P(),
            P(),
            P("dp", "space", None, None),
        ),
        out_specs=(P("dp", "space", None, None), P("dp", "space", None, None), P(), P()),
        check_vma=False,
    )
```

```python
import functools

import jax
import jax.numpy as jnp
from jax import lax
from jax.experimental import pallas as pl
from jax.experimental.pallas import tpu as pltpu
from jax.sharding import PartitionSpec as P

F32 = jnp.float32
BF16 = jnp.bfloat16


def neighbour_rows(array):
    peers = lax.axis_size("space")
    if peers == 1:
        return array[-1:], array[:1]
    if peers == 2:
        got = lax.ppermute(array, "space", [(0, 1), (1, 0)])
        return got, got
    up = [(i, i + 1) for i in range(peers - 1)]
    down = [(j, i) for i, j in up]
    return lax.ppermute(array[-1:], "space", up), lax.ppermute(array[:1], "space", down)


def put_shifted(stack, slot, row, sign):
    cols, channels = row.shape
    wide = row.astype(F32)
    place = lax.broadcasted_iota(jnp.int32, (cols, channels), 0)
    later = jnp.where(place == cols - 1, 0.0, pltpu.roll(wide, cols - 1, 0)).astype(BF16)
    earlier = jnp.where(place == 0, 0.0, pltpu.roll(wide, 1, 0)).astype(BF16)
    first, last = (earlier, later) if sign < 0 else (later, earlier)
    stack[slot, :, 0:channels] = first
    stack[slot, :, channels : 2 * channels] = row
    stack[slot, :, 2 * channels :] = last


def put_halo(stack, before, after, rows, peers, sign):
    here = lax.axis_index("space")
    zero = jnp.zeros(before.shape, BF16)
    put_shifted(stack, 0, jnp.where(here > 0, before, zero), sign)
    put_shifted(stack, rows + 1, jnp.where(here < peers - 1, after, zero), sign)


def merge_kernel(*refs):
    far, (merged, merged_t, stack, feat, out_w), near, sems = refs[:5], refs[5:10], refs[10:13], refs[13]
    near = (*near, feat, out_w)
    copies = [pltpu.make_async_copy(a, b, sems.at[i]) for i, (a, b) in enumerate(zip(far, near))]
    for copy in copies:
        copy.start()
    cot, lat_w, top = near[:3]
    rows, cols, channels = cot.shape
    half = cols // 2
    copies[0].wait()
    for r in range(rows):
        put_shifted(stack, r, cot[r], 1)
    for copy in copies[1:4]:
        copy.wait()
    upper = lax.broadcasted_iota(jnp.int32, (cols, half), 0)
    spread = jnp.where(upper // 2 == lax.broadcasted_iota(jnp.int32, (cols, half), 1), 1.0, 0.0).astype(BF16)
    lateral = jnp.dot(feat[...], lat_w[...], preferred_element_type=F32)
    for q in range(rows // 2):
        lifted = jnp.dot(spread, top[q], preferred_element_type=F32)
        for r in (2 * q, 2 * q + 1):
            merged[r * cols : (r + 1) * cols, :] = (lateral[r * cols : (r + 1) * cols] + lifted).astype(BF16)
    merged_t[...] = jnp.transpose(merged[...])
    copies[4].wait()


def strips_of(stack, halo):
    rows, cols, deep = stack.shape
    strips = [
        jnp.concatenate([stack[1:], halo[1:]], axis=0),
        stack[...],
        jnp.concatenate([halo[:1], stack[: rows - 1]], axis=0),
    ]
    return [strip.reshape(rows * cols, deep) for strip in strips]


def put_sums(outs, start, values):
    rows = slice(start, start + values.shape[0])
    if len(outs) == 1:
        outs[0][rows, :] = values
        return
    here = lax.axis_index("space")
    half = values.shape[1] // 2
    mine, theirs = outs
    mine[rows, :] = jnp.where(here == 0, values[:, :half], values[:, half:])
    theirs[rows, :] = jnp.where(here == 0, values[:, half:], values[:, :half]).astype(BF16)


def kernel_grad_kernel(stack, halo, merged_t, out):
    channels = merged_t.shape[0]
    for i, strip in enumerate(strips_of(stack, halo)):
        part = jnp.dot(merged_t[...], strip, preferred_element_type=F32)
        for j in range(3):
            start = (3 * i + j) * channels
            out[start : start + channels, :] = part[:, j * channels : (j + 1) * channels]


def cells_of(image, first, rows):
    strips = [image[pl.ds(first + 1 - i, rows)] for i in range(3)]
    return jnp.concatenate([strip.reshape(-1, strip.shape[-1]) for strip in strips], axis=1)


def own_kernel_grad_kernel(stack, merged_t, cot, image, sums):
    here = lax.axis_index("space")
    rows, cols, channels = cot.shape
    half = channels // 2
    zero = jnp.zeros((1, cols, 3 * half), BF16)
    image[0:1] = zero
    image[2 * rows + 1 :] = zero
    own, other = 1 + rows * here, 1 + rows * (1 - here)
    for r in range(rows):
        row = cot[r]
        put_shifted(image, other + r, jnp.where(here == 0, row[:, :half], row[:, half:]), 1)
        for j in range(3):
            start = j * channels
            left, right = stack[r, :, start : start + half], stack[r, :, start + half : start + channels]
            image[own + r, :, j * half : (j + 1) * half] = jnp.where(here == 0, left, right)
    sums[...] = jnp.dot(merged_t[...], cells_of(image, own, rows), preferred_element_type=F32)


def rest_kernel_grad_kernel(image, sums, merged, *refs):
    outs, total = refs[:4], refs[4]
    here, (place, _) = lax.axis_index("space"), places()
    channels, half = merged.shape[1], total.shape[1]
    rows = (image.shape[0] - 2) // 2
    cells = cells_of(image, 1 + rows * (1 - here), rows)
    part = sums[...] + jnp.dot(jnp.transpose(merged[...]), cells, preferred_element_type=F32)
    for tap in range(9):
        total[tap * channels : (tap + 1) * channels, :] = part[:, tap * half : (tap + 1) * half]
    for k, out in zip((0, 3, 2, 1), outs):
        out[...] = total[block(place ^ k, out.shape[0]), :].astype(out.dtype)


def data_grad_kernel(peers, waits, stack, before, after, feat, out_w, *refs):
    grad, halo, *outs = refs[waits:]
    put_halo(halo, before[before.shape[0] - 1], after[0], 0, peers, 1)
    cells = jnp.concatenate(strips_of(stack, halo), axis=1)
    taps = jnp.concatenate([out_w[tap] for tap in range(9)], axis=1)
    total = lax.dot_general(cells, taps, (((1,), (1,)), ((), ())), preferred_element_type=F32)
    grad[...] = total.astype(BF16)
    put_sums(outs, 0, jnp.dot(jnp.transpose(feat[...]), grad[...], preferred_element_type=F32))


def forward_kernel(peers, merged, out_w, grad, *refs):
    edges, (out, grad_top, stack, near, sem) = refs[:-5], refs[-5:]
    rows, cols, channels = merged.shape
    half = cols // 2
    for r in range(rows):
        put_shifted(stack, r + 1, merged[r], -1)
    put_halo(stack, edges[0][edges[0].shape[0] - 1], edges[1][0], rows, peers, -1)
    cells = jnp.concatenate([stack[i : i + rows].reshape(rows * cols, 3 * channels) for i in range(3)], axis=1)
    total = jnp.dot(cells, out_w[...].reshape(9 * channels, channels), preferred_element_type=F32)
    near[...] = total.astype(BF16).reshape(out.shape)
    copy = pltpu.make_async_copy(near, out, sem)
    copy.start()
    lower = lax.broadcasted_iota(jnp.int32, (half, 2 * cols), 1)
    lower = jnp.where(lower >= cols, lower - cols, lower)
    pool = jnp.where(lower // 2 == lax.broadcasted_iota(jnp.int32, (half, 2 * cols), 0), 1.0, 0.0).astype(BF16)
    for q in range(rows // 2):
        pair = grad[2 * q * cols : (2 * q + 2) * cols, :]
        grad_top[q] = jnp.dot(pool, pair, preferred_element_type=F32).astype(BF16)
    copy.wait()


def places():
    chip, core = lax.axis_index("dp"), lax.axis_index("space")
    plane, line = chip % 4, chip // 4
    return jnp.where(core == 0, plane, line), jnp.where(core == 0, line, plane)


def block(index, length):
    return pl.ds(pl.multiple_of(index * length, 16), length)


def cut_kernel(mine, got, *refs):
    place, _ = places()
    for k, out in zip((0, 3, 2, 1), refs):
        rows = block(place ^ k, out.shape[0])
        out[...] = (mine[rows, :] + got[rows, :].astype(F32)).astype(out.dtype)


def add_kernel(own, three, two, one, out):
    total = own[...] + one[...].astype(F32) + two[...].astype(F32) + three[...].astype(F32)
    out[...] = total.astype(BF16)


def finish_kernel(scale, own, one, two, three, *refs):
    near = own[...].astype(F32) + one[...].astype(F32)
    far = two[...].astype(F32) + three[...].astype(F32)
    out = refs[-1]
    start = out.shape[0] - own.shape[0]
    if start:
        out[:start, :] = refs[0][...]
    out[start:, :] = ((near + far) * scale).astype(BF16)


def copy_kernel(array, _, out):
    out[...] = array[...]


def place_kernel(pair, *refs):
    results, sems = refs[-3:-1], refs[-1]
    side = lax.axis_index("space")
    columns, place = (1 - side, places()[1]) if pair else (side, places()[0])
    lanes = pl.ds(pl.multiple_of(columns * 128, 128), 128)
    copies = []
    for k, quarter in enumerate(refs[:4]):
        start = 0
        for result in results:
            share = result.shape[0] // 4
            to = result.at[block(place ^ k, share), lanes]
            copies.append(pltpu.make_async_copy(quarter.at[pl.ds(start, share), :], to, sems.at[len(copies)]))
            start += share
    for copy in copies:
        copy.start()
    for copy in copies:
        copy.wait()


def exchange(array, step, k):
    pairs = []
    for chip in range(16):
        for core in range(2):
            flip = k if core == step else 4 * k
            pairs.append((2 * chip + core, 2 * (chip ^ flip) + core))
    return lax.ppermute(array, ("dp", "space"), pairs)


def swap(array):
    return lax.ppermute(array, "space", [(0, 1), (1, 0)])


def call(kernel, *shapes, **more):
    return pl.pallas_call(
        kernel,
        out_shape=[jax.ShapeDtypeStruct(shape, kind) for shape, kind in shapes],
        compiler_params=pltpu.CompilerParams(vmem_limit_bytes=12 * 2**20),
        **more,
    )


def sum_everywhere(pieces, lateral_part, scale, after):
    vmem, far = pl.BlockSpec(memory_space=pltpu.VMEM), pl.BlockSpec(memory_space=pltpu.HBM)
    after = pltpu.with_memory_space_constraint(after, pltpu.HBM)
    slow = [pl.CostEstimate(flops=flops, bytes_accessed=2**10, transcendentals=0) for flops in (2**30, 2**31)]
    lateral = lateral_part[0].shape
    share = (lateral[0] // 4, lateral[1])
    lateral_pieces = call(cut_kernel, (share, F32), *[(share, BF16)] * 3)(*lateral_part)
    sums = []
    for (own, *others), cost in zip((pieces, lateral_pieces), slow):
        came = [exchange(piece, 0, k) for piece, k in zip(others, (3, 2, 1))]
        [total] = call(add_kernel, (own.shape, BF16), cost_estimate=cost)(own, *came)
        sums.append([total] + [exchange(total, 1, k) for k in (3, 2, 1)][::-1])
    finish = functools.partial(finish_kernel, scale)
    [first] = call(finish, (pieces[0].shape, BF16), cost_estimate=slow[0])(*sums[0])
    joint = (first.shape[0] + share[0], share[1])
    [total] = call(finish, (joint, BF16))(*sums[1], first)
    three, two, one = [exchange(total, 0, k) for k in (3, 2, 1)]
    quarters = [total, one, two, three]
    [ready] = call(copy_kernel, (joint, BF16), in_specs=[vmem, far])(total, after)
    results = [((4 * rows, 2 * share[1]), BF16) for rows in (first.shape[0], share[0])]
    place = dict(out_specs=[far] * 2, scratch_shapes=[pltpu.SemaphoreType.DMA((8,))])
    half = call(functools.partial(place_kernel, False), *results, **place)(*quarters)
    place.update(in_specs=[vmem] * 4 + [far] * 2, input_output_aliases={4: 0, 5: 1})
    return call(functools.partial(place_kernel, True), *results, **place)(*[swap(one) for one in (ready, *quarters[1:])], *half)


def local(features, top_down, lateral_weight, out_kernel, cotangent):
    images, rows, cols, in_channels = features.shape
    channels = lateral_weight.shape[1]
    cells = rows * cols
    peers = lax.axis_size("space")
    taps = out_kernel.reshape(9, channels, channels)
    params = pltpu.CompilerParams(vmem_limit_bytes=32 * 2**20)
    halves = peers == 2 and lax.axis_size("dp") == 16 and images == 1 and (channels, in_channels) == (256, 512)

    def sums(length):
        if not halves:
            return [jax.ShapeDtypeStruct((length, channels), F32)]
        return [jax.ShapeDtypeStruct((length, channels // 2), kind) for kind in (F32, BF16)]

    outs, tops, parts = [], [], None
    for image in range(images):
        cot = cotangent[image]
        cot_before, cot_after = neighbour_rows(cot)
        arrays = (cot, lateral_weight, top_down[image], features[image].reshape(cells, in_channels), taps)
        arrays = [pltpu.with_memory_space_constraint(array, pltpu.HBM) for array in arrays]
        merged, merged_t, stack, near_feat, near_taps = pl.pallas_call(
            merge_kernel,
            out_shape=[
                jax.ShapeDtypeStruct(shape, BF16)
                for shape in (
                    (cells, channels),
                    (channels, cells),
                    (rows, cols, 3 * channels),
                    (cells, in_channels),
                    taps.shape,
                )
            ],
            in_specs=[pl.BlockSpec(memory_space=pltpu.HBM)] * 5,
            scratch_shapes=[*[pltpu.VMEM(array.shape, BF16) for array in arrays[:3]], pltpu.SemaphoreType.DMA((5,))],
            compiler_params=params,
            cost_estimate=pl.CostEstimate(
                flops=2 * cells * channels * 4 * in_channels, bytes_accessed=4 * 2**20, transcendentals=0
            ),
        )(*arrays)
        merged = merged.reshape(rows, cols, channels)
        edges = neighbour_rows(merged)
        kernel_flops = 2 * cells * channels * 9 * channels
        waited = []
        if halves:
            half, quarter = channels // 2, (9 * channels // 4, channels // 2)
            image_shape = (2 * rows + 2, cols, 3 * half)
            cost = pl.CostEstimate(flops=kernel_flops // 2, bytes_accessed=2**20, transcendentals=0)
            image, first_sums = pl.pallas_call(
                own_kernel_grad_kernel,
                out_shape=[
                    jax.ShapeDtypeStruct(image_shape, BF16),
                    jax.ShapeDtypeStruct((channels, 9 * half), F32),
                ],
                compiler_params=params,
                cost_estimate=cost,
            )(stack, merged_t, cot_after)
            pieces = pl.pallas_call(
                rest_kernel_grad_kernel,
                out_shape=[jax.ShapeDtypeStruct(quarter, F32), *[jax.ShapeDtypeStruct(quarter, BF16)] * 3],
                scratch_shapes=[pltpu.VMEM((9 * channels, half), F32)],
                compiler_params=params,
                cost_estimate=cost,
            )(image, first_sums, edges[0].reshape(cells, channels))
            waited = [pieces[0]]
        grad, halo, *lateral_part = pl.pallas_call(
            functools.partial(data_grad_kernel, peers, len(waited)),
            out_shape=[
                jax.ShapeDtypeStruct((cells, channels), BF16),
                jax.ShapeDtypeStruct((2, cols, 3 * channels), BF16),
                *sums(in_channels),
            ],
            compiler_params=params,
            cost_estimate=pl.CostEstimate(
                flops=2 * cells * channels * (9 * channels + in_channels), bytes_accessed=4 * 2**20, transcendentals=0
            ),
        )(stack, cot_before, cot_after, near_feat, near_taps, *waited)
        if halves:
            lateral_part[1] = swap(lateral_part[1])
        else:
            kernel_sums = pl.pallas_call(
                kernel_grad_kernel,
                out_shape=jax.ShapeDtypeStruct((9 * channels, channels), F32),
                compiler_params=params,
                cost_estimate=pl.CostEstimate(flops=kernel_flops, bytes_accessed=4 * 2**20, transcendentals=0),
            )(stack, halo, merged_t)
        out, grad_top = pl.pallas_call(
            functools.partial(forward_kernel, peers),
            out_shape=[
                jax.ShapeDtypeStruct((rows, cols, channels), BF16),
                jax.ShapeDtypeStruct((rows // 2, cols // 2, channels), BF16),
            ],
            out_specs=[pl.BlockSpec(memory_space=pltpu.HBM), pl.BlockSpec(memory_space=pltpu.VMEM)],
            scratch_shapes=[
                pltpu.VMEM((rows + 2, cols, 3 * channels), BF16),
                pltpu.VMEM((rows, cols, channels), BF16),
                pltpu.SemaphoreType.DMA,
            ],
            compiler_params=params,
            cost_estimate=pl.CostEstimate(
                flops=2 * cells * channels * 9 * channels, bytes_accessed=2 * 2**20, transcendentals=0
            ),
        )(merged, near_taps, grad, *edges)
        outs.append(out)
        tops.append(grad_top)
        if not halves:
            part = [kernel_sums, lateral_part[0]]
            parts = part if parts is None else [a + b for a, b in zip(parts, part)]
    scale = 1.0 / (images * lax.axis_size("dp"))
    if halves:
        grad_kernel, grad_lateral = sum_everywhere(pieces, lateral_part, scale, outs[0])
    else:
        grad_kernel, grad_lateral = [(total * scale).astype(BF16) for total in lax.psum(parts, ("dp", "space"))]
    return jnp.stack(outs), jnp.stack(tops), grad_kernel.reshape(out_kernel.shape), grad_lateral


def solution(mesh):
    return jax.shard_map(
        local,
        mesh=mesh,
        in_specs=(
            P("dp", "space", None, None),
            P("dp", "space", None, None),
            P(),
            P(),
            P("dp", "space", None, None),
        ),
        out_specs=(P("dp", "space", None, None), P("dp", "space", None, None), P(), P()),
        check_vma=False,
    )
```

```python
import functools

import jax
import jax.numpy as jnp
from jax import lax
from jax.experimental import pallas as pl
from jax.experimental.pallas import tpu as pltpu
from jax.sharding import PartitionSpec as P

F32 = jnp.float32
BF16 = jnp.bfloat16


def neighbour_rows(array):
    peers = lax.axis_size("space")
    if peers == 1:
        return array[-1:], array[:1]
    if peers == 2:
        got = lax.ppermute(array, "space", [(0, 1), (1, 0)])
        return got, got
    up = [(i, i + 1) for i in range(peers - 1)]
    down = [(j, i) for i, j in up]
    return lax.ppermute(array[-1:], "space", up), lax.ppermute(array[:1], "space", down)


def put_shifted(stack, slot, row, sign):
    cols, channels = row.shape
    wide = row.astype(F32)
    place = lax.broadcasted_iota(jnp.int32, (cols, channels), 0)
    later = jnp.where(place == cols - 1, 0.0, pltpu.roll(wide, cols - 1, 0)).astype(BF16)
    earlier = jnp.where(place == 0, 0.0, pltpu.roll(wide, 1, 0)).astype(BF16)
    first, last = (earlier, later) if sign < 0 else (later, earlier)
    stack[slot, :, 0:channels] = first
    stack[slot, :, channels : 2 * channels] = row
    stack[slot, :, 2 * channels :] = last


def put_halo(stack, before, after, rows, peers, sign):
    here = lax.axis_index("space")
    zero = jnp.zeros(before.shape, BF16)
    put_shifted(stack, 0, jnp.where(here > 0, before, zero), sign)
    put_shifted(stack, rows + 1, jnp.where(here < peers - 1, after, zero), sign)


def merge_kernel(*refs):
    far, (merged, merged_t, stack, feat, out_w), near, sems = refs[:5], refs[5:10], refs[10:13], refs[13]
    near = (*near, feat, out_w)
    copies = [pltpu.make_async_copy(a, b, sems.at[i]) for i, (a, b) in enumerate(zip(far, near))]
    for copy in copies:
        copy.start()
    cot, lat_w, top = near[:3]
    rows, cols, channels = cot.shape
    half = cols // 2
    for copy in copies[:4]:
        copy.wait()
    for r in range(rows):
        put_shifted(stack, r, cot[r], 1)
    upper = lax.broadcasted_iota(jnp.int32, (cols, half), 0)
    spread = jnp.where(upper // 2 == lax.broadcasted_iota(jnp.int32, (cols, half), 1), 1.0, 0.0).astype(BF16)
    lateral = jnp.dot(feat[...], lat_w[...], preferred_element_type=F32)
    for q in range(rows // 2):
        lifted = jnp.dot(spread, top[q], preferred_element_type=F32)
        for r in (2 * q, 2 * q + 1):
            merged[r * cols : (r + 1) * cols, :] = (lateral[r * cols : (r + 1) * cols] + lifted).astype(BF16)
    merged_t[...] = jnp.transpose(merged[...])
    copies[4].wait()


def strips_of(stack, halo):
    rows, cols, deep = stack.shape
    strips = [
        jnp.concatenate([stack[1:], halo[1:]], axis=0),
        stack[...],
        jnp.concatenate([halo[:1], stack[: rows - 1]], axis=0),
    ]
    return [strip.reshape(rows * cols, deep) for strip in strips]


def put_sums(outs, start, values):
    rows = slice(start, start + values.shape[0])
    if len(outs) == 1:
        outs[0][rows, :] = values
        return
    here = lax.axis_index("space")
    half = values.shape[1] // 2
    mine, theirs = outs
    mine[rows, :] = jnp.where(here == 0, values[:, :half], values[:, half:])
    theirs[rows, :] = jnp.where(here == 0, values[:, half:], values[:, :half]).astype(BF16)


def kernel_grad_kernel(stack, halo, merged_t, out):
    channels = merged_t.shape[0]
    for i, strip in enumerate(strips_of(stack, halo)):
        part = jnp.dot(merged_t[...], strip, preferred_element_type=F32)
        for j in range(3):
            start = (3 * i + j) * channels
            out[start : start + channels, :] = part[:, j * channels : (j + 1) * channels]


def pair_kernel_grad_kernel(stack, merged_t, cot, merged, out, image):
    here = lax.axis_index("space")
    rows, cols, channels = cot.shape
    half = channels // 2
    zero = jnp.zeros((1, cols, 3 * half), BF16)
    image[0:1] = zero
    image[2 * rows + 1 :] = zero
    own, other = 1 + rows * here, 1 + rows * (1 - here)
    for r in range(rows):
        row = cot[r]
        put_shifted(image, other + r, jnp.where(here == 0, row[:, :half], row[:, half:]), 1)
        for j in range(3):
            start = j * channels
            left, right = stack[r, :, start : start + half], stack[r, :, start + half : start + channels]
            image[own + r, :, j * half : (j + 1) * half] = jnp.where(here == 0, left, right)
    cells = []
    for first in (own, other):
        strips = [image[pl.ds(first + 1 - i, rows)].reshape(rows * cols, 3 * half) for i in range(3)]
        cells.append(jnp.concatenate(strips, axis=1))
    left = jnp.concatenate([merged_t[...], jnp.transpose(merged[...])], axis=1)
    part = jnp.dot(left, jnp.concatenate(cells, axis=0), preferred_element_type=F32)
    for tap in range(9):
        out[tap * channels : (tap + 1) * channels, :] = part[:, tap * half : (tap + 1) * half]


def data_grad_kernel(peers, stack, before, after, feat, out_w, grad, halo, *outs):
    put_halo(halo, before[before.shape[0] - 1], after[0], 0, peers, 1)
    cells = jnp.concatenate(strips_of(stack, halo), axis=1)
    taps = jnp.concatenate([out_w[tap] for tap in range(9)], axis=1)
    total = lax.dot_general(cells, taps, (((1,), (1,)), ((), ())), preferred_element_type=F32)
    grad[...] = total.astype(BF16)
    put_sums(outs, 0, jnp.dot(jnp.transpose(feat[...]), grad[...], preferred_element_type=F32))


def forward_kernel(peers, merged, out_w, grad, *refs):
    edges, (out, grad_top, stack, near, sem) = refs[:-5], refs[-5:]
    rows, cols, channels = merged.shape
    half = cols // 2
    for r in range(rows):
        put_shifted(stack, r + 1, merged[r], -1)
    put_halo(stack, edges[0][edges[0].shape[0] - 1], edges[1][0], rows, peers, -1)
    cells = jnp.concatenate([stack[i : i + rows].reshape(rows * cols, 3 * channels) for i in range(3)], axis=1)
    total = jnp.dot(cells, out_w[...].reshape(9 * channels, channels), preferred_element_type=F32)
    near[...] = total.astype(BF16).reshape(out.shape)
    copy = pltpu.make_async_copy(near, out, sem)
    copy.start()
    lower = lax.broadcasted_iota(jnp.int32, (half, 2 * cols), 1)
    lower = jnp.where(lower >= cols, lower - cols, lower)
    pool = jnp.where(lower // 2 == lax.broadcasted_iota(jnp.int32, (half, 2 * cols), 0), 1.0, 0.0).astype(BF16)
    for q in range(rows // 2):
        pair = grad[2 * q * cols : (2 * q + 2) * cols, :]
        grad_top[q] = jnp.dot(pool, pair, preferred_element_type=F32).astype(BF16)
    copy.wait()


def places():
    chip, core = lax.axis_index("dp"), lax.axis_index("space")
    plane, line = chip % 4, chip // 4
    return jnp.where(core == 0, plane, line), jnp.where(core == 0, line, plane)


def block(index, length):
    return pl.ds(pl.multiple_of(index * length, 16), length)


def cut_kernel(kernel_sums, mine, got, *refs):
    place, _ = places()
    edge, share = kernel_sums.shape[0] // 4, mine.shape[0] // 4
    for k, out in zip((0, 3, 2, 1), refs):
        out[:edge, :] = kernel_sums[block(place ^ k, edge), :].astype(out.dtype)
        rows = block(place ^ k, share)
        out[edge:, :] = (mine[rows, :] + got[rows, :].astype(F32)).astype(out.dtype)


def add_kernel(own, three, two, one, out):
    total = own[...] + one[...].astype(F32) + two[...].astype(F32) + three[...].astype(F32)
    out[...] = total.astype(BF16)


def finish_kernel(scale, own, three, two, one, _, out):
    near = own[...].astype(F32) + one[...].astype(F32)
    far = two[...].astype(F32) + three[...].astype(F32)
    out[...] = ((near + far) * scale).astype(BF16)


def place_kernel(plan, *refs):
    results, sems = refs[-3:-1], refs[-1]
    side, (own, other) = lax.axis_index("space"), places()
    copies = []
    for quarter, (pair, k) in zip(refs, plan):
        columns, place = (1 - side, other) if pair else (side, own)
        lanes = pl.ds(pl.multiple_of(columns * 128, 128), 128)
        start = 0
        for result in results:
            share = result.shape[0] // 4
            to = result.at[block(place ^ k, share), lanes]
            copies.append(pltpu.make_async_copy(quarter.at[pl.ds(start, share), :], to, sems.at[len(copies)]))
            start += share
    for copy in copies:
        copy.start()
    for copy in copies:
        copy.wait()


def exchange(array, step, k):
    pairs = []
    for chip in range(16):
        for core in range(2):
            flip = k if core == step else 4 * k
            pairs.append((2 * chip + core, 2 * (chip ^ flip) + core))
    return lax.ppermute(array, ("dp", "space"), pairs)


def swap(array):
    return lax.ppermute(array, "space", [(0, 1), (1, 0)])


def call(kernel, *shapes, **more):
    return pl.pallas_call(
        kernel,
        out_shape=[jax.ShapeDtypeStruct(shape, kind) for shape, kind in shapes],
        compiler_params=pltpu.CompilerParams(vmem_limit_bytes=12 * 2**20),
        **more,
    )


def sum_everywhere(kernel_sums, lateral_part, scale, after):
    lengths, width = [kernel_sums.shape[0], lateral_part[0].shape[0]], kernel_sums.shape[1]
    vmem, far = pl.BlockSpec(memory_space=pltpu.VMEM), pl.BlockSpec(memory_space=pltpu.HBM)
    after = pltpu.with_memory_space_constraint(after, pltpu.HBM)
    quarter = (sum(lengths) // 4, width)
    own, *pieces = call(cut_kernel, (quarter, F32), *[(quarter, BF16)] * 3)(kernel_sums, *lateral_part)
    three, two, one = [exchange(piece, 0, k) for piece, k in zip(pieces, (3, 2, 1))]
    [total] = call(add_kernel, (quarter, BF16))(own, three, two, one)
    three, two, one = [exchange(total, 1, k) for k in (3, 2, 1)]
    finish = call(functools.partial(finish_kernel, scale), (quarter, BF16), in_specs=[vmem] * 4 + [far])
    [total] = finish(total, three, two, one, after)
    three, two, one = [exchange(total, 0, k) for k in (3, 2, 1)]
    quarters = [total, three, two, one]
    results = [((length, 2 * width), BF16) for length in lengths]
    others = [swap(one) for one in quarters]
    place = dict(out_specs=[far] * 2, scratch_shapes=[pltpu.SemaphoreType.DMA((10,))])
    plan = (False, 0), (False, 3), (False, 2), (False, 1), (True, 0)
    most = call(functools.partial(place_kernel, plan), *results, **place)(*quarters, others[0])
    plan = (True, 3), (True, 2), (True, 1)
    place.update(in_specs=[vmem] * 3 + [far] * 2, input_output_aliases={3: 0, 4: 1})
    return call(functools.partial(place_kernel, plan), *results, **place)(*others[1:], *most)


def local(features, top_down, lateral_weight, out_kernel, cotangent):
    images, rows, cols, in_channels = features.shape
    channels = lateral_weight.shape[1]
    cells = rows * cols
    peers = lax.axis_size("space")
    taps = out_kernel.reshape(9, channels, channels)
    params = pltpu.CompilerParams(vmem_limit_bytes=32 * 2**20)
    halves = peers == 2 and lax.axis_size("dp") == 16 and images == 1 and (channels, in_channels) == (256, 512)

    def sums(length):
        if not halves:
            return [jax.ShapeDtypeStruct((length, channels), F32)]
        return [jax.ShapeDtypeStruct((length, channels // 2), kind) for kind in (F32, BF16)]

    outs, tops, parts = [], [], None
    for image in range(images):
        cot = cotangent[image]
        cot_before, cot_after = neighbour_rows(cot)
        arrays = (cot, lateral_weight, top_down[image], features[image].reshape(cells, in_channels), taps)
        arrays = [pltpu.with_memory_space_constraint(array, pltpu.HBM) for array in arrays]
        merged, merged_t, stack, near_feat, near_taps = pl.pallas_call(
            merge_kernel,
            out_shape=[
                jax.ShapeDtypeStruct(shape, BF16)
                for shape in (
                    (cells, channels),
                    (channels, cells),
                    (rows, cols, 3 * channels),
                    (cells, in_channels),
                    taps.shape,
                )
            ],
            in_specs=[pl.BlockSpec(memory_space=pltpu.HBM)] * 5,
            scratch_shapes=[*[pltpu.VMEM(array.shape, BF16) for array in arrays[:3]], pltpu.SemaphoreType.DMA((5,))],
            compiler_params=params,
            cost_estimate=pl.CostEstimate(
                flops=2 * cells * channels * 4 * in_channels, bytes_accessed=4 * 2**20, transcendentals=0
            ),
        )(*arrays)
        merged = merged.reshape(rows, cols, channels)
        edges = neighbour_rows(merged)
        grad, halo, *lateral_part = pl.pallas_call(
            functools.partial(data_grad_kernel, peers),
            out_shape=[
                jax.ShapeDtypeStruct((cells, channels), BF16),
                jax.ShapeDtypeStruct((2, cols, 3 * channels), BF16),
                *sums(in_channels),
            ],
            compiler_params=params,
            cost_estimate=pl.CostEstimate(
                flops=2 * cells * channels * (9 * channels + in_channels), bytes_accessed=4 * 2**20, transcendentals=0
            ),
        )(stack, cot_before, cot_after, near_feat, near_taps)
        kernel_cost = pl.CostEstimate(
            flops=2 * cells * channels * 9 * channels, bytes_accessed=4 * 2**20, transcendentals=0
        )
        if halves:
            lateral_part[1] = swap(lateral_part[1])
            kernel_sums = pl.pallas_call(
                pair_kernel_grad_kernel,
                out_shape=jax.ShapeDtypeStruct((9 * channels, channels // 2), F32),
                scratch_shapes=[pltpu.VMEM((2 * rows + 2, cols, 3 * channels // 2), BF16)],
                compiler_params=params,
                cost_estimate=kernel_cost,
            )(stack, merged_t, cot_after, edges[0].reshape(cells, channels))
        else:
            kernel_sums = pl.pallas_call(
                kernel_grad_kernel,
                out_shape=jax.ShapeDtypeStruct((9 * channels, channels), F32),
                compiler_params=params,
                cost_estimate=kernel_cost,
            )(stack, halo, merged_t)
        out, grad_top = pl.pallas_call(
            functools.partial(forward_kernel, peers),
            out_shape=[
                jax.ShapeDtypeStruct((rows, cols, channels), BF16),
                jax.ShapeDtypeStruct((rows // 2, cols // 2, channels), BF16),
            ],
            out_specs=[pl.BlockSpec(memory_space=pltpu.HBM), pl.BlockSpec(memory_space=pltpu.VMEM)],
            scratch_shapes=[
                pltpu.VMEM((rows + 2, cols, 3 * channels), BF16),
                pltpu.VMEM((rows, cols, channels), BF16),
                pltpu.SemaphoreType.DMA,
            ],
            compiler_params=params,
            cost_estimate=pl.CostEstimate(
                flops=2 * cells * channels * 9 * channels, bytes_accessed=2 * 2**20, transcendentals=0
            ),
        )(merged, near_taps, grad, *edges)
        outs.append(out)
        tops.append(grad_top)
        if not halves:
            part = [kernel_sums, lateral_part[0]]
            parts = part if parts is None else [a + b for a, b in zip(parts, part)]
    scale = 1.0 / (images * lax.axis_size("dp"))
    if halves:
        grad_kernel, grad_lateral = sum_everywhere(kernel_sums, lateral_part, scale, outs[0])
    else:
        grad_kernel, grad_lateral = [(total * scale).astype(BF16) for total in lax.psum(parts, ("dp", "space"))]
    return jnp.stack(outs), jnp.stack(tops), grad_kernel.reshape(out_kernel.shape), grad_lateral


def solution(mesh):
    return jax.shard_map(
        local,
        mesh=mesh,
        in_specs=(
            P("dp", "space", None, None),
            P("dp", "space", None, None),
            P(),
            P(),
            P("dp", "space", None, None),
        ),
        out_specs=(P("dp", "space", None, None), P("dp", "space", None, None), P(), P()),
        check_vma=False,
    )
```

```python
import functools

import jax
import jax.numpy as jnp
from jax import lax
from jax.experimental import pallas as pl
from jax.experimental.pallas import tpu as pltpu
from jax.sharding import PartitionSpec as P

F32 = jnp.float32
BF16 = jnp.bfloat16


def neighbour_rows(array):
    peers = lax.axis_size("space")
    if peers == 1:
        return array[-1:], array[:1]
    if peers == 2:
        got = lax.ppermute(array, "space", [(0, 1), (1, 0)])
        return got, got
    up = [(i, i + 1) for i in range(peers - 1)]
    down = [(j, i) for i, j in up]
    return lax.ppermute(array[-1:], "space", up), lax.ppermute(array[:1], "space", down)


def put_shifted(stack, slot, row, sign):
    cols, channels = row.shape
    wide = row.astype(F32)
    place = lax.broadcasted_iota(jnp.int32, (cols, channels), 0)
    later = jnp.where(place == cols - 1, 0.0, pltpu.roll(wide, cols - 1, 0)).astype(BF16)
    earlier = jnp.where(place == 0, 0.0, pltpu.roll(wide, 1, 0)).astype(BF16)
    first, last = (earlier, later) if sign < 0 else (later, earlier)
    stack[slot, :, 0:channels] = first
    stack[slot, :, channels : 2 * channels] = row
    stack[slot, :, 2 * channels :] = last


def put_halo(stack, before, after, rows, peers, sign):
    here = lax.axis_index("space")
    zero = jnp.zeros(before.shape, BF16)
    put_shifted(stack, 0, jnp.where(here > 0, before, zero), sign)
    put_shifted(stack, rows + 1, jnp.where(here < peers - 1, after, zero), sign)


def merge_kernel(*refs):
    far, (merged, merged_t, stack, feat, out_w), near, sems = refs[:5], refs[5:10], refs[10:13], refs[13]
    near = (*near, feat, out_w)
    copies = [pltpu.make_async_copy(a, b, sems.at[i]) for i, (a, b) in enumerate(zip(far, near))]
    for copy in copies:
        copy.start()
    cot, lat_w, top = near[:3]
    rows, cols, channels = cot.shape
    half = cols // 2
    upper = lax.broadcasted_iota(jnp.int32, (cols, half), 0)
    spread = jnp.where(upper // 2 == lax.broadcasted_iota(jnp.int32, (cols, half), 1), 1.0, 0.0).astype(BF16)
    copies[0].wait()
    for r in range(rows):
        put_shifted(stack, r, cot[r], 1)
    for copy in copies[1:4]:
        copy.wait()
    lateral = jnp.dot(feat[...], lat_w[...], preferred_element_type=F32)
    for q in range(rows // 2):
        lifted = jnp.dot(spread, top[q], preferred_element_type=F32)
        for r in (2 * q, 2 * q + 1):
            merged[r * cols : (r + 1) * cols, :] = (lateral[r * cols : (r + 1) * cols] + lifted).astype(BF16)
    merged_t[...] = jnp.transpose(merged[...])
    copies[4].wait()


def strips_of(stack, halo):
    rows, cols, deep = stack.shape
    strips = [
        jnp.concatenate([stack[1:], halo[1:]], axis=0),
        stack[...],
        jnp.concatenate([halo[:1], stack[: rows - 1]], axis=0),
    ]
    return [strip.reshape(rows * cols, deep) for strip in strips]


def put_sums(outs, start, values):
    rows = slice(start, start + values.shape[0])
    if len(outs) == 1:
        outs[0][rows, :] = values
        return
    here = lax.axis_index("space")
    half = values.shape[1] // 2
    mine, theirs = outs
    mine[rows, :] = jnp.where(here == 0, values[:, :half], values[:, half:])
    theirs[rows, :] = jnp.where(here == 0, values[:, half:], values[:, :half]).astype(BF16)


def kernel_grad_kernel(stack, halo, merged_t, out):
    channels = merged_t.shape[0]
    for i, strip in enumerate(strips_of(stack, halo)):
        part = jnp.dot(merged_t[...], strip, preferred_element_type=F32)
        for j in range(3):
            start = (3 * i + j) * channels
            out[start : start + channels, :] = part[:, j * channels : (j + 1) * channels]


def pair_kernel_grad_kernel(stack, merged_t, cot, merged, out, image):
    here = lax.axis_index("space")
    rows, cols, channels = cot.shape
    half = channels // 2
    zero = jnp.zeros((1, cols, 3 * half), BF16)
    image[0:1] = zero
    image[2 * rows + 1 :] = zero
    own, other = 1 + rows * here, 1 + rows * (1 - here)
    for r in range(rows):
        row = cot[r]
        put_shifted(image, other + r, jnp.where(here == 0, row[:, :half], row[:, half:]), 1)
        for j in range(3):
            start = j * channels
            left, right = stack[r, :, start : start + half], stack[r, :, start + half : start + channels]
            image[own + r, :, j * half : (j + 1) * half] = jnp.where(here == 0, left, right)
    cells = []
    for first in (own, other):
        strips = [image[pl.ds(first + 1 - i, rows)].reshape(rows * cols, 3 * half) for i in range(3)]
        cells.append(jnp.concatenate(strips, axis=1))
    left = jnp.concatenate([merged_t[...], jnp.transpose(merged[...])], axis=1)
    part = jnp.dot(left, jnp.concatenate(cells, axis=0), preferred_element_type=F32)
    for tap in range(9):
        out[tap * channels : (tap + 1) * channels, :] = part[:, tap * half : (tap + 1) * half]


def data_grad_kernel(peers, stack, before, after, feat, out_w, grad, halo, *outs):
    put_halo(halo, before[before.shape[0] - 1], after[0], 0, peers, 1)
    cells = jnp.concatenate(strips_of(stack, halo), axis=1)
    taps = jnp.concatenate([out_w[tap] for tap in range(9)], axis=1)
    total = lax.dot_general(cells, taps, (((1,), (1,)), ((), ())), preferred_element_type=F32)
    grad[...] = total.astype(BF16)
    put_sums(outs, 0, jnp.dot(jnp.transpose(feat[...]), grad[...], preferred_element_type=F32))


def forward_kernel(peers, merged, out_w, grad, *refs):
    edges, (out, grad_top, stack, near, sem) = refs[:-5], refs[-5:]
    rows, cols, channels = merged.shape
    half = cols // 2
    for r in range(rows):
        put_shifted(stack, r + 1, merged[r], -1)
    put_halo(stack, edges[0][edges[0].shape[0] - 1], edges[1][0], rows, peers, -1)
    cells = jnp.concatenate([stack[i : i + rows].reshape(rows * cols, 3 * channels) for i in range(3)], axis=1)
    total = jnp.dot(cells, out_w[...].reshape(9 * channels, channels), preferred_element_type=F32)
    near[...] = total.astype(BF16).reshape(out.shape)
    copy = pltpu.make_async_copy(near, out, sem)
    copy.start()
    lower = lax.broadcasted_iota(jnp.int32, (half, 2 * cols), 1)
    lower = jnp.where(lower >= cols, lower - cols, lower)
    pool = jnp.where(lower // 2 == lax.broadcasted_iota(jnp.int32, (half, 2 * cols), 0), 1.0, 0.0).astype(BF16)
    for q in range(rows // 2):
        pair = grad[2 * q * cols : (2 * q + 2) * cols, :]
        grad_top[q] = jnp.dot(pool, pair, preferred_element_type=F32).astype(BF16)
    copy.wait()


def places():
    chip, core = lax.axis_index("dp"), lax.axis_index("space")
    plane, line = chip % 4, chip // 4
    return jnp.where(core == 0, plane, line), jnp.where(core == 0, line, plane)


def block(index, length):
    return pl.ds(pl.multiple_of(index * length, 16), length)


def cut_kernel(kernel_sums, mine, got, *refs):
    place, _ = places()
    edge, share = kernel_sums.shape[0] // 4, mine.shape[0] // 4
    for k, out in zip((0, 3, 2, 1), refs):
        out[:edge, :] = kernel_sums[block(place ^ k, edge), :].astype(out.dtype)
        rows = block(place ^ k, share)
        out[edge:, :] = (mine[rows, :] + got[rows, :].astype(F32)).astype(out.dtype)


def add_kernel(own, three, two, one, out):
    total = own[...] + one[...].astype(F32) + two[...].astype(F32) + three[...].astype(F32)
    out[...] = total.astype(BF16)


def finish_kernel(scale, own, three, two, one, _, out):
    near = own[...].astype(F32) + one[...].astype(F32)
    far = two[...].astype(F32) + three[...].astype(F32)
    out[...] = ((near + far) * scale).astype(BF16)


def place_kernel(plan, *refs):
    results, sems = refs[-3:-1], refs[-1]
    side, (own, other) = lax.axis_index("space"), places()
    copies = []
    for quarter, (pair, k) in zip(refs, plan):
        columns, place = (1 - side, other) if pair else (side, own)
        lanes = pl.ds(pl.multiple_of(columns * 128, 128), 128)
        start = 0
        for result in results:
            share = result.shape[0] // 4
            to = result.at[block(place ^ k, share), lanes]
            copies.append(pltpu.make_async_copy(quarter.at[pl.ds(start, share), :], to, sems.at[len(copies)]))
            start += share
    for copy in copies:
        copy.start()
    for copy in copies:
        copy.wait()


def exchange(array, step, k):
    pairs = []
    for chip in range(16):
        for core in range(2):
            flip = k if core == step else 4 * k
            pairs.append((2 * chip + core, 2 * (chip ^ flip) + core))
    return lax.ppermute(array, ("dp", "space"), pairs)


def swap(array):
    return lax.ppermute(array, "space", [(0, 1), (1, 0)])


def call(kernel, *shapes, **more):
    return pl.pallas_call(
        kernel,
        out_shape=[jax.ShapeDtypeStruct(shape, kind) for shape, kind in shapes],
        compiler_params=pltpu.CompilerParams(vmem_limit_bytes=12 * 2**20),
        **more,
    )


def sum_everywhere(kernel_sums, lateral_part, scale, after):
    lengths, width = [kernel_sums.shape[0], lateral_part[0].shape[0]], kernel_sums.shape[1]
    vmem, far = pl.BlockSpec(memory_space=pltpu.VMEM), pl.BlockSpec(memory_space=pltpu.HBM)
    after = pltpu.with_memory_space_constraint(after, pltpu.HBM)
    quarter = (sum(lengths) // 4, width)
    own, *pieces = call(cut_kernel, (quarter, F32), *[(quarter, BF16)] * 3)(kernel_sums, *lateral_part)
    three, two, one = [exchange(piece, 0, k) for piece, k in zip(pieces, (3, 2, 1))]
    [total] = call(add_kernel, (quarter, BF16))(own, three, two, one)
    three, two, one = [exchange(total, 1, k) for k in (3, 2, 1)]
    finish = call(functools.partial(finish_kernel, scale), (quarter, BF16), in_specs=[vmem] * 4 + [far])
    [total] = finish(total, three, two, one, after)
    three, two, one = [exchange(total, 0, k) for k in (3, 2, 1)]
    quarters = [total, three, two, one]
    results = [((length, 2 * width), BF16) for length in lengths]
    others = [swap(one) for one in quarters]
    place = dict(out_specs=[far] * 2, scratch_shapes=[pltpu.SemaphoreType.DMA((10,))])
    plan = (False, 0), (False, 3), (False, 2), (False, 1), (True, 0)
    most = call(functools.partial(place_kernel, plan), *results, **place)(*quarters, others[0])
    plan = (True, 3), (True, 2), (True, 1)
    place.update(in_specs=[vmem] * 3 + [far] * 2, input_output_aliases={3: 0, 4: 1})
    return call(functools.partial(place_kernel, plan), *results, **place)(*others[1:], *most)


def local(features, top_down, lateral_weight, out_kernel, cotangent):
    images, rows, cols, in_channels = features.shape
    channels = lateral_weight.shape[1]
    cells = rows * cols
    peers = lax.axis_size("space")
    taps = out_kernel.reshape(9, channels, channels)
    params = pltpu.CompilerParams(vmem_limit_bytes=32 * 2**20)
    halves = peers == 2 and lax.axis_size("dp") == 16 and images == 1 and (channels, in_channels) == (256, 512)

    def sums(length):
        if not halves:
            return [jax.ShapeDtypeStruct((length, channels), F32)]
        return [jax.ShapeDtypeStruct((length, channels // 2), kind) for kind in (F32, BF16)]

    outs, tops, parts = [], [], None
    for image in range(images):
        cot = cotangent[image]
        cot_before, cot_after = neighbour_rows(cot)
        arrays = (cot, lateral_weight, top_down[image], features[image].reshape(cells, in_channels), taps)
        arrays = [pltpu.with_memory_space_constraint(array, pltpu.HBM) for array in arrays]
        merged, merged_t, stack, near_feat, near_taps = pl.pallas_call(
            merge_kernel,
            out_shape=[
                jax.ShapeDtypeStruct(shape, BF16)
                for shape in (
                    (cells, channels),
                    (channels, cells),
                    (rows, cols, 3 * channels),
                    (cells, in_channels),
                    taps.shape,
                )
            ],
            in_specs=[pl.BlockSpec(memory_space=pltpu.HBM)] * 5,
            scratch_shapes=[*[pltpu.VMEM(array.shape, BF16) for array in arrays[:3]], pltpu.SemaphoreType.DMA((5,))],
            compiler_params=params,
            cost_estimate=pl.CostEstimate(
                flops=2 * cells * channels * 4 * in_channels, bytes_accessed=4 * 2**20, transcendentals=0
            ),
        )(*arrays)
        merged = merged.reshape(rows, cols, channels)
        edges = neighbour_rows(merged)
        grad, halo, *lateral_part = pl.pallas_call(
            functools.partial(data_grad_kernel, peers),
            out_shape=[
                jax.ShapeDtypeStruct((cells, channels), BF16),
                jax.ShapeDtypeStruct((2, cols, 3 * channels), BF16),
                *sums(in_channels),
            ],
            compiler_params=params,
            cost_estimate=pl.CostEstimate(
                flops=2 * cells * channels * (9 * channels + in_channels), bytes_accessed=4 * 2**20, transcendentals=0
            ),
        )(stack, cot_before, cot_after, near_feat, near_taps)
        kernel_cost = pl.CostEstimate(
            flops=2 * cells * channels * 9 * channels, bytes_accessed=4 * 2**20, transcendentals=0
        )
        if halves:
            lateral_part[1] = swap(lateral_part[1])
            kernel_sums = pl.pallas_call(
                pair_kernel_grad_kernel,
                out_shape=jax.ShapeDtypeStruct((9 * channels, channels // 2), F32),
                scratch_shapes=[pltpu.VMEM((2 * rows + 2, cols, 3 * channels // 2), BF16)],
                compiler_params=params,
                cost_estimate=kernel_cost,
            )(stack, merged_t, cot_after, edges[0].reshape(cells, channels))
        else:
            kernel_sums = pl.pallas_call(
                kernel_grad_kernel,
                out_shape=jax.ShapeDtypeStruct((9 * channels, channels), F32),
                compiler_params=params,
                cost_estimate=kernel_cost,
            )(stack, halo, merged_t)
        out, grad_top = pl.pallas_call(
            functools.partial(forward_kernel, peers),
            out_shape=[
                jax.ShapeDtypeStruct((rows, cols, channels), BF16),
                jax.ShapeDtypeStruct((rows // 2, cols // 2, channels), BF16),
            ],
            out_specs=[pl.BlockSpec(memory_space=pltpu.HBM), pl.BlockSpec(memory_space=pltpu.VMEM)],
            scratch_shapes=[
                pltpu.VMEM((rows + 2, cols, 3 * channels), BF16),
                pltpu.VMEM((rows, cols, channels), BF16),
                pltpu.SemaphoreType.DMA,
            ],
            compiler_params=params,
            cost_estimate=pl.CostEstimate(
                flops=2 * cells * channels * 9 * channels, bytes_accessed=2 * 2**20, transcendentals=0
            ),
        )(merged, near_taps, grad, *edges)
        outs.append(out)
        tops.append(grad_top)
        if not halves:
            part = [kernel_sums, lateral_part[0]]
            parts = part if parts is None else [a + b for a, b in zip(parts, part)]
    scale = 1.0 / (images * lax.axis_size("dp"))
    if halves:
        grad_kernel, grad_lateral = sum_everywhere(kernel_sums, lateral_part, scale, outs[0])
    else:
        grad_kernel, grad_lateral = [(total * scale).astype(BF16) for total in lax.psum(parts, ("dp", "space"))]
    return jnp.stack(outs), jnp.stack(tops), grad_kernel.reshape(out_kernel.shape), grad_lateral


def solution(mesh):
    return jax.shard_map(
        local,
        mesh=mesh,
        in_specs=(
            P("dp", "space", None, None),
            P("dp", "space", None, None),
            P(),
            P(),
            P("dp", "space", None, None),
        ),
        out_specs=(P("dp", "space", None, None), P("dp", "space", None, None), P(), P()),
        check_vma=False,
    )
```

```python
import functools

import jax
import jax.numpy as jnp
from jax import lax
from jax.experimental import pallas as pl
from jax.experimental.pallas import tpu as pltpu
from jax.sharding import PartitionSpec as P

F32 = jnp.float32
BF16 = jnp.bfloat16


def neighbour_rows(array):
    peers = lax.axis_size("space")
    if peers == 1:
        return array[-1:], array[:1]
    if peers == 2:
        got = lax.ppermute(array, "space", [(0, 1), (1, 0)])
        return got, got
    up = [(i, i + 1) for i in range(peers - 1)]
    down = [(j, i) for i, j in up]
    return lax.ppermute(array[-1:], "space", up), lax.ppermute(array[:1], "space", down)


def put_shifted(stack, slot, row, sign):
    cols, channels = row.shape
    wide = row.astype(F32)
    place = lax.broadcasted_iota(jnp.int32, (cols, channels), 0)
    later = jnp.where(place == cols - 1, 0.0, pltpu.roll(wide, cols - 1, 0)).astype(BF16)
    earlier = jnp.where(place == 0, 0.0, pltpu.roll(wide, 1, 0)).astype(BF16)
    first, last = (earlier, later) if sign < 0 else (later, earlier)
    stack[slot, :, 0:channels] = first
    stack[slot, :, channels : 2 * channels] = row
    stack[slot, :, 2 * channels :] = last


def put_halo(stack, before, after, rows, peers, sign):
    here = lax.axis_index("space")
    zero = jnp.zeros(before.shape, BF16)
    put_shifted(stack, 0, jnp.where(here > 0, before, zero), sign)
    put_shifted(stack, rows + 1, jnp.where(here < peers - 1, after, zero), sign)


def merge_kernel(*refs):
    far, (merged, merged_t, stack, feat, out_w), near, sems = refs[:5], refs[5:10], refs[10:13], refs[13]
    near = (*near, feat, out_w)
    copies = [pltpu.make_async_copy(a, b, sems.at[i]) for i, (a, b) in enumerate(zip(far, near))]
    for copy in copies:
        copy.start()
    cot, lat_w, top = near[:3]
    rows, cols, channels = cot.shape
    half = cols // 2
    upper = lax.broadcasted_iota(jnp.int32, (cols, half), 0)
    spread = jnp.where(upper // 2 == lax.broadcasted_iota(jnp.int32, (cols, half), 1), 1.0, 0.0).astype(BF16)
    copies[0].wait()
    for r in range(rows):
        put_shifted(stack, r, cot[r], 1)
    for copy in copies[1:4]:
        copy.wait()
    lateral = jnp.dot(feat[...], lat_w[...], preferred_element_type=F32)
    for q in range(rows // 2):
        lifted = jnp.dot(spread, top[q], preferred_element_type=F32)
        for r in (2 * q, 2 * q + 1):
            merged[r * cols : (r + 1) * cols, :] = (lateral[r * cols : (r + 1) * cols] + lifted).astype(BF16)
    merged_t[...] = jnp.transpose(merged[...])
    copies[4].wait()


def strips_of(stack, halo):
    rows, cols, deep = stack.shape
    strips = [
        jnp.concatenate([stack[1:], halo[1:]], axis=0),
        stack[...],
        jnp.concatenate([halo[:1], stack[: rows - 1]], axis=0),
    ]
    return [strip.reshape(rows * cols, deep) for strip in strips]


def put_sums(outs, start, values):
    rows = slice(start, start + values.shape[0])
    if len(outs) == 1:
        outs[0][rows, :] = values
        return
    here = lax.axis_index("space")
    half = values.shape[1] // 2
    mine, theirs = outs
    mine[rows, :] = jnp.where(here == 0, values[:, :half], values[:, half:])
    theirs[rows, :] = jnp.where(here == 0, values[:, half:], values[:, :half]).astype(BF16)


def kernel_grad_kernel(stack, halo, merged_t, out):
    channels = merged_t.shape[0]
    for i, strip in enumerate(strips_of(stack, halo)):
        part = jnp.dot(merged_t[...], strip, preferred_element_type=F32)
        for j in range(3):
            start = (3 * i + j) * channels
            out[start : start + channels, :] = part[:, j * channels : (j + 1) * channels]


def pair_kernel_grad_kernel(stack, merged_t, cot, merged, out, image):
    here = lax.axis_index("space")
    rows, cols, channels = cot.shape
    half = channels // 2
    zero = jnp.zeros((1, cols, 3 * half), BF16)
    image[0:1] = zero
    image[2 * rows + 1 :] = zero
    own, other = 1 + rows * here, 1 + rows * (1 - here)
    for r in range(rows):
        row = cot[r]
        put_shifted(image, other + r, jnp.where(here == 0, row[:, :half], row[:, half:]), 1)
        for j in range(3):
            start = j * channels
            left, right = stack[r, :, start : start + half], stack[r, :, start + half : start + channels]
            image[own + r, :, j * half : (j + 1) * half] = jnp.where(here == 0, left, right)
    cells = []
    for first in (own, other):
        strips = [image[pl.ds(first + 1 - i, rows)].reshape(rows * cols, 3 * half) for i in range(3)]
        cells.append(jnp.concatenate(strips, axis=1))
    left = jnp.concatenate([merged_t[...], jnp.transpose(merged[...])], axis=1)
    part = jnp.dot(left, jnp.concatenate(cells, axis=0), preferred_element_type=F32)
    for tap in range(9):
        out[tap * channels : (tap + 1) * channels, :] = part[:, tap * half : (tap + 1) * half]


def data_grad_kernel(peers, stack, before, after, feat, out_w, grad, halo, *outs):
    put_halo(halo, before[before.shape[0] - 1], after[0], 0, peers, 1)
    cells = jnp.concatenate(strips_of(stack, halo), axis=1)
    taps = jnp.concatenate([out_w[tap] for tap in range(9)], axis=1)
    total = lax.dot_general(cells, taps, (((1,), (1,)), ((), ())), preferred_element_type=F32)
    grad[...] = total.astype(BF16)
    put_sums(outs, 0, jnp.dot(jnp.transpose(feat[...]), grad[...], preferred_element_type=F32))


def forward_kernel(peers, merged, out_w, grad, *refs):
    edges, (out, grad_top, stack, near, sem) = refs[:-5], refs[-5:]
    rows, cols, channels = merged.shape
    half = cols // 2
    for r in range(rows):
        put_shifted(stack, r + 1, merged[r], -1)
    put_halo(stack, edges[0][edges[0].shape[0] - 1], edges[1][0], rows, peers, -1)
    cells = jnp.concatenate([stack[i : i + rows].reshape(rows * cols, 3 * channels) for i in range(3)], axis=1)
    total = jnp.dot(cells, out_w[...].reshape(9 * channels, channels), preferred_element_type=F32)
    near[...] = total.astype(BF16).reshape(out.shape)
    copy = pltpu.make_async_copy(near, out, sem)
    copy.start()
    lower = lax.broadcasted_iota(jnp.int32, (half, 2 * cols), 1)
    lower = jnp.where(lower >= cols, lower - cols, lower)
    pool = jnp.where(lower // 2 == lax.broadcasted_iota(jnp.int32, (half, 2 * cols), 0), 1.0, 0.0).astype(BF16)
    for q in range(rows // 2):
        pair = grad[2 * q * cols : (2 * q + 2) * cols, :]
        grad_top[q] = jnp.dot(pool, pair, preferred_element_type=F32).astype(BF16)
    copy.wait()


def places():
    chip, core = lax.axis_index("dp"), lax.axis_index("space")
    plane, line = chip % 4, chip // 4
    return jnp.where(core == 0, plane, line), jnp.where(core == 0, line, plane)


def block(index, length):
    return pl.ds(pl.multiple_of(index * length, 16), length)


def cut_kernel(kernel_sums, mine, got, *refs):
    place, _ = places()
    edge, share = kernel_sums.shape[0] // 4, mine.shape[0] // 4
    for k, out in zip((0, 3, 2, 1), refs):
        out[:edge, :] = kernel_sums[block(place ^ k, edge), :].astype(out.dtype)
        rows = block(place ^ k, share)
        out[edge:, :] = (mine[rows, :] + got[rows, :].astype(F32)).astype(out.dtype)


def add_kernel(own, three, two, one, out):
    total = own[...] + one[...].astype(F32) + two[...].astype(F32) + three[...].astype(F32)
    out[...] = total.astype(BF16)


def finish_kernel(scale, own, three, two, one, _, out):
    near = own[...].astype(F32) + one[...].astype(F32)
    far = two[...].astype(F32) + three[...].astype(F32)
    out[...] = ((near + far) * scale).astype(BF16)


def place_kernel(plan, *refs):
    results, sems = refs[-3:-1], refs[-1]
    side, (own, other) = lax.axis_index("space"), places()
    copies = []
    for quarter, (pair, k) in zip(refs, plan):
        columns, place = (1 - side, other) if pair else (side, own)
        lanes = pl.ds(pl.multiple_of(columns * 128, 128), 128)
        start = 0
        for result in results:
            share = result.shape[0] // 4
            to = result.at[block(place ^ k, share), lanes]
            copies.append(pltpu.make_async_copy(quarter.at[pl.ds(start, share), :], to, sems.at[len(copies)]))
            start += share
    for copy in copies:
        copy.start()
    for copy in copies:
        copy.wait()


def exchange(array, step, k):
    pairs = []
    for chip in range(16):
        for core in range(2):
            flip = (k if step == 0 else 4 - k) if core == step else 4 * k
            pairs.append((2 * chip + core, 2 * (chip ^ flip) + core))
    return lax.ppermute(array, ("dp", "space"), pairs)


def swap(array):
    return lax.ppermute(array, "space", [(0, 1), (1, 0)])


def call(kernel, *shapes, **more):
    return pl.pallas_call(
        kernel,
        out_shape=[jax.ShapeDtypeStruct(shape, kind) for shape, kind in shapes],
        compiler_params=pltpu.CompilerParams(vmem_limit_bytes=12 * 2**20),
        **more,
    )


def sum_everywhere(kernel_sums, lateral_part, scale, after):
    lengths, width = [kernel_sums.shape[0], lateral_part[0].shape[0]], kernel_sums.shape[1]
    vmem, far = pl.BlockSpec(memory_space=pltpu.VMEM), pl.BlockSpec(memory_space=pltpu.HBM)
    after = pltpu.with_memory_space_constraint(after, pltpu.HBM)
    quarter = (sum(lengths) // 4, width)
    own, *pieces = call(cut_kernel, (quarter, F32), *[(quarter, BF16)] * 3)(kernel_sums, *lateral_part)
    three, two, one = [exchange(piece, 0, k) for piece, k in zip(pieces, (3, 2, 1))]
    [total] = call(add_kernel, (quarter, BF16))(own, three, two, one)
    three, two, one = [exchange(total, 1, k) for k in (3, 2, 1)]
    finish = call(functools.partial(finish_kernel, scale), (quarter, BF16), in_specs=[vmem] * 4 + [far])
    [total] = finish(total, three, two, one, after)
    three, two, one = [exchange(total, 0, k) for k in (3, 2, 1)]
    quarters = [total, three, two, one]
    results = [((length, 2 * width), BF16) for length in lengths]
    others = [swap(one) for one in quarters]
    place = dict(out_specs=[far] * 2, scratch_shapes=[pltpu.SemaphoreType.DMA((10,))])
    plan = (False, 0), (False, 3), (False, 2), (False, 1), (True, 0)
    most = call(functools.partial(place_kernel, plan), *results, **place)(*quarters, others[0])
    plan = (True, 3), (True, 2), (True, 1)
    place.update(in_specs=[vmem] * 3 + [far] * 2, input_output_aliases={3: 0, 4: 1})
    return call(functools.partial(place_kernel, plan), *results, **place)(*others[1:], *most)


def local(features, top_down, lateral_weight, out_kernel, cotangent):
    images, rows, cols, in_channels = features.shape
    channels = lateral_weight.shape[1]
    cells = rows * cols
    peers = lax.axis_size("space")
    taps = out_kernel.reshape(9, channels, channels)
    params = pltpu.CompilerParams(vmem_limit_bytes=32 * 2**20)
    halves = peers == 2 and lax.axis_size("dp") == 16 and images == 1 and (channels, in_channels) == (256, 512)

    def sums(length):
        if not halves:
            return [jax.ShapeDtypeStruct((length, channels), F32)]
        return [jax.ShapeDtypeStruct((length, channels // 2), kind) for kind in (F32, BF16)]

    outs, tops, parts = [], [], None
    for image in range(images):
        cot = cotangent[image]
        cot_before, cot_after = neighbour_rows(cot)
        arrays = (cot, lateral_weight, top_down[image], features[image].reshape(cells, in_channels), taps)
        arrays = [pltpu.with_memory_space_constraint(array, pltpu.HBM) for array in arrays]
        merged, merged_t, stack, near_feat, near_taps = pl.pallas_call(
            merge_kernel,
            out_shape=[
                jax.ShapeDtypeStruct(shape, BF16)
                for shape in (
                    (cells, channels),
                    (channels, cells),
                    (rows, cols, 3 * channels),
                    (cells, in_channels),
                    taps.shape,
                )
            ],
            in_specs=[pl.BlockSpec(memory_space=pltpu.HBM)] * 5,
            scratch_shapes=[*[pltpu.VMEM(array.shape, BF16) for array in arrays[:3]], pltpu.SemaphoreType.DMA((5,))],
            compiler_params=params,
            cost_estimate=pl.CostEstimate(
                flops=2 * cells * channels * 4 * in_channels, bytes_accessed=4 * 2**20, transcendentals=0
            ),
        )(*arrays)
        merged = merged.reshape(rows, cols, channels)
        edges = neighbour_rows(merged)
        grad, halo, *lateral_part = pl.pallas_call(
            functools.partial(data_grad_kernel, peers),
            out_shape=[
                jax.ShapeDtypeStruct((cells, channels), BF16),
                jax.ShapeDtypeStruct((2, cols, 3 * channels), BF16),
                *sums(in_channels),
            ],
            compiler_params=params,
            cost_estimate=pl.CostEstimate(
                flops=2 * cells * channels * (9 * channels + in_channels), bytes_accessed=4 * 2**20, transcendentals=0
            ),
        )(stack, cot_before, cot_after, near_feat, near_taps)
        kernel_cost = pl.CostEstimate(
            flops=2 * cells * channels * 9 * channels, bytes_accessed=4 * 2**20, transcendentals=0
        )
        if halves:
            lateral_part[1] = swap(lateral_part[1])
            kernel_sums = pl.pallas_call(
                pair_kernel_grad_kernel,
                out_shape=jax.ShapeDtypeStruct((9 * channels, channels // 2), F32),
                scratch_shapes=[pltpu.VMEM((2 * rows + 2, cols, 3 * channels // 2), BF16)],
                compiler_params=params,
                cost_estimate=kernel_cost,
            )(stack, merged_t, cot_after, edges[0].reshape(cells, channels))
        else:
            kernel_sums = pl.pallas_call(
                kernel_grad_kernel,
                out_shape=jax.ShapeDtypeStruct((9 * channels, channels), F32),
                compiler_params=params,
                cost_estimate=kernel_cost,
            )(stack, halo, merged_t)
        out, grad_top = pl.pallas_call(
            functools.partial(forward_kernel, peers),
            out_shape=[
                jax.ShapeDtypeStruct((rows, cols, channels), BF16),
                jax.ShapeDtypeStruct((rows // 2, cols // 2, channels), BF16),
            ],
            out_specs=[pl.BlockSpec(memory_space=pltpu.HBM), pl.BlockSpec(memory_space=pltpu.VMEM)],
            scratch_shapes=[
                pltpu.VMEM((rows + 2, cols, 3 * channels), BF16),
                pltpu.VMEM((rows, cols, channels), BF16),
                pltpu.SemaphoreType.DMA,
            ],
            compiler_params=params,
            cost_estimate=pl.CostEstimate(
                flops=2 * cells * channels * 9 * channels, bytes_accessed=2 * 2**20, transcendentals=0
            ),
        )(merged, near_taps, grad, *edges)
        outs.append(out)
        tops.append(grad_top)
        if not halves:
            part = [kernel_sums, lateral_part[0]]
            parts = part if parts is None else [a + b for a, b in zip(parts, part)]
    scale = 1.0 / (images * lax.axis_size("dp"))
    if halves:
        grad_kernel, grad_lateral = sum_everywhere(kernel_sums, lateral_part, scale, outs[0])
    else:
        grad_kernel, grad_lateral = [(total * scale).astype(BF16) for total in lax.psum(parts, ("dp", "space"))]
    return jnp.stack(outs), jnp.stack(tops), grad_kernel.reshape(out_kernel.shape), grad_lateral


def solution(mesh):
    return jax.shard_map(
        local,
        mesh=mesh,
        in_specs=(
            P("dp", "space", None, None),
            P("dp", "space", None, None),
            P(),
            P(),
            P("dp", "space", None, None),
        ),
        out_specs=(P("dp", "space", None, None), P("dp", "space", None, None), P(), P()),
        check_vma=False,
    )
```

```python
import functools

import jax
import jax.numpy as jnp
from jax import lax
from jax.experimental import pallas as pl
from jax.experimental.pallas import tpu as pltpu
from jax.sharding import PartitionSpec as P

F32 = jnp.float32
BF16 = jnp.bfloat16


def neighbour_rows(array):
    peers = lax.axis_size("space")
    if peers == 1:
        return array[-1:], array[:1]
    if peers == 2:
        got = lax.ppermute(array, "space", [(0, 1), (1, 0)])
        return got, got
    up = [(i, i + 1) for i in range(peers - 1)]
    down = [(j, i) for i, j in up]
    return lax.ppermute(array[-1:], "space", up), lax.ppermute(array[:1], "space", down)


def put_shifted(stack, slot, row, sign):
    cols, channels = row.shape
    wide = row.astype(F32)
    place = lax.broadcasted_iota(jnp.int32, (cols, channels), 0)
    later = jnp.where(place == cols - 1, 0.0, pltpu.roll(wide, cols - 1, 0)).astype(BF16)
    earlier = jnp.where(place == 0, 0.0, pltpu.roll(wide, 1, 0)).astype(BF16)
    first, last = (earlier, later) if sign < 0 else (later, earlier)
    stack[slot, :, 0:channels] = first
    stack[slot, :, channels : 2 * channels] = row
    stack[slot, :, 2 * channels :] = last


def put_halo(stack, before, after, rows, peers, sign):
    here = lax.axis_index("space")
    zero = jnp.zeros(before.shape, BF16)
    put_shifted(stack, 0, jnp.where(here > 0, before, zero), sign)
    put_shifted(stack, rows + 1, jnp.where(here < peers - 1, after, zero), sign)


def merge_kernel(*refs):
    far, (merged, stack, feat, out_w), near, sems = refs[:5], refs[5:9], refs[9:12], refs[12]
    near = (*near, feat, out_w)
    copies = [pltpu.make_async_copy(a, b, sems.at[i]) for i, (a, b) in enumerate(zip(far, near))]
    for copy in copies:
        copy.start()
    cot, lat_w, top = near[:3]
    rows, cols, channels = cot.shape
    half = cols // 2
    upper = lax.broadcasted_iota(jnp.int32, (cols, half), 0)
    spread = jnp.where(upper // 2 == lax.broadcasted_iota(jnp.int32, (cols, half), 1), 1.0, 0.0).astype(BF16)
    copies[0].wait()
    for r in range(rows):
        put_shifted(stack, r, cot[r], 1)
    for copy in copies[1:4]:
        copy.wait()
    lateral = jnp.dot(feat[...], lat_w[...], preferred_element_type=F32)
    for q in range(rows // 2):
        lifted = jnp.dot(spread, top[q], preferred_element_type=F32)
        for r in (2 * q, 2 * q + 1):
            merged[r * cols : (r + 1) * cols, :] = (lateral[r * cols : (r + 1) * cols] + lifted).astype(BF16)
    copies[4].wait()


def over_cells(left, right):
    return lax.dot_general(left, right, (((0,), (0,)), ((), ())), preferred_element_type=F32)


def strips_of(stack, halo):
    rows, cols, deep = stack.shape
    strips = [
        jnp.concatenate([stack[1:], halo[1:]], axis=0),
        stack[...],
        jnp.concatenate([halo[:1], stack[: rows - 1]], axis=0),
    ]
    return [strip.reshape(rows * cols, deep) for strip in strips]


def put_sums(outs, start, values):
    rows = slice(start, start + values.shape[0])
    if len(outs) == 1:
        outs[0][rows, :] = values
        return
    here = lax.axis_index("space")
    half = values.shape[1] // 2
    mine, theirs = outs
    mine[rows, :] = jnp.where(here == 0, values[:, :half], values[:, half:])
    theirs[rows, :] = jnp.where(here == 0, values[:, half:], values[:, :half]).astype(BF16)


def kernel_grad_kernel(stack, halo, merged, out):
    channels = merged.shape[1]
    for i, strip in enumerate(strips_of(stack, halo)):
        part = over_cells(merged[...], strip)
        for j in range(3):
            start = (3 * i + j) * channels
            out[start : start + channels, :] = part[:, j * channels : (j + 1) * channels]


def pair_kernel_grad_kernel(stack, merged, cot, other_merged, out, image):
    here = lax.axis_index("space")
    rows, cols, channels = cot.shape
    half = channels // 2
    zero = jnp.zeros((1, cols, 3 * half), BF16)
    image[0:1] = zero
    image[2 * rows + 1 :] = zero
    own, other = 1 + rows * here, 1 + rows * (1 - here)
    for r in range(rows):
        row = cot[r]
        put_shifted(image, other + r, jnp.where(here == 0, row[:, :half], row[:, half:]), 1)
        for j in range(3):
            start = j * channels
            left, right = stack[r, :, start : start + half], stack[r, :, start + half : start + channels]
            image[own + r, :, j * half : (j + 1) * half] = jnp.where(here == 0, left, right)
    cells = []
    for first in (own, other):
        strips = [image[pl.ds(first + 1 - i, rows)].reshape(rows * cols, 3 * half) for i in range(3)]
        cells.append(jnp.concatenate(strips, axis=1))
    left = jnp.concatenate([merged[...], other_merged[...]], axis=0)
    part = over_cells(left, jnp.concatenate(cells, axis=0))
    for tap in range(9):
        out[tap * channels : (tap + 1) * channels, :] = part[:, tap * half : (tap + 1) * half]


def data_grad_kernel(peers, stack, before, after, feat, out_w, grad, halo, *outs):
    put_halo(halo, before[before.shape[0] - 1], after[0], 0, peers, 1)
    cells = jnp.concatenate(strips_of(stack, halo), axis=1)
    taps = jnp.concatenate([out_w[tap] for tap in range(9)], axis=1)
    total = lax.dot_general(cells, taps, (((1,), (1,)), ((), ())), preferred_element_type=F32)
    grad[...] = total.astype(BF16)
    put_sums(outs, 0, over_cells(feat[...], grad[...]))


def forward_kernel(peers, merged, out_w, grad, *refs):
    edges, (out, grad_top, stack, near, sem) = refs[:-5], refs[-5:]
    rows, cols, channels = merged.shape
    half = cols // 2
    for r in range(rows):
        put_shifted(stack, r + 1, merged[r], -1)
    put_halo(stack, edges[0][edges[0].shape[0] - 1], edges[1][0], rows, peers, -1)
    cells = jnp.concatenate([stack[i : i + rows].reshape(rows * cols, 3 * channels) for i in range(3)], axis=1)
    total = jnp.dot(cells, out_w[...].reshape(9 * channels, channels), preferred_element_type=F32)
    near[...] = total.astype(BF16).reshape(out.shape)
    copy = pltpu.make_async_copy(near, out, sem)
    copy.start()
    lower = lax.broadcasted_iota(jnp.int32, (half, 2 * cols), 1)
    lower = jnp.where(lower >= cols, lower - cols, lower)
    pool = jnp.where(lower // 2 == lax.broadcasted_iota(jnp.int32, (half, 2 * cols), 0), 1.0, 0.0).astype(BF16)
    for q in range(rows // 2):
        pair = grad[2 * q * cols : (2 * q + 2) * cols, :]
        grad_top[q] = jnp.dot(pool, pair, preferred_element_type=F32).astype(BF16)
    copy.wait()


def places():
    chip, core = lax.axis_index("dp"), lax.axis_index("space")
    plane, line = chip % 4, chip // 4
    return jnp.where(core == 0, plane, line), jnp.where(core == 0, line, plane)


def block(index, length):
    return pl.ds(pl.multiple_of(index * length, 16), length)


def cut_kernel(kernel_sums, mine, got, *refs):
    place, _ = places()
    edge, share = kernel_sums.shape[0] // 4, mine.shape[0] // 4
    for k, out in zip((0, 3, 2, 1), refs):
        out[:edge, :] = kernel_sums[block(place ^ k, edge), :].astype(out.dtype)
        rows = block(place ^ k, share)
        out[edge:, :] = (mine[rows, :] + got[rows, :].astype(F32)).astype(out.dtype)


def add_kernel(own, three, two, one, out):
    total = own[...] + one[...].astype(F32) + two[...].astype(F32) + three[...].astype(F32)
    out[...] = total.astype(BF16)


def finish_kernel(scale, own, three, two, one, _, out):
    near = own[...].astype(F32) + one[...].astype(F32)
    far = two[...].astype(F32) + three[...].astype(F32)
    out[...] = ((near + far) * scale).astype(BF16)


def place_kernel(plan, *refs):
    results, sems = refs[-3:-1], refs[-1]
    side, (own, other) = lax.axis_index("space"), places()
    copies = []
    for quarter, (pair, k) in zip(refs, plan):
        columns, place = (1 - side, other) if pair else (side, own)
        lanes = pl.ds(pl.multiple_of(columns * 128, 128), 128)
        start = 0
        for result in results:
            share = result.shape[0] // 4
            to = result.at[block(place ^ k, share), lanes]
            copies.append(pltpu.make_async_copy(quarter.at[pl.ds(start, share), :], to, sems.at[len(copies)]))
            start += share
    for copy in copies:
        copy.start()
    for copy in copies:
        copy.wait()


def exchange(array, step, k):
    pairs = []
    for chip in range(16):
        for core in range(2):
            flip = k if core == step else 4 * k
            pairs.append((2 * chip + core, 2 * (chip ^ flip) + core))
    return lax.ppermute(array, ("dp", "space"), pairs)


def swap(array):
    return lax.ppermute(array, "space", [(0, 1), (1, 0)])


def call(kernel, *shapes, **more):
    return pl.pallas_call(
        kernel,
        out_shape=[jax.ShapeDtypeStruct(shape, kind) for shape, kind in shapes],
        compiler_params=pltpu.CompilerParams(vmem_limit_bytes=12 * 2**20),
        **more,
    )


def sum_everywhere(kernel_sums, lateral_part, scale, after):
    lengths, width = [kernel_sums.shape[0], lateral_part[0].shape[0]], kernel_sums.shape[1]
    vmem, far = pl.BlockSpec(memory_space=pltpu.VMEM), pl.BlockSpec(memory_space=pltpu.HBM)
    after = pltpu.with_memory_space_constraint(after, pltpu.HBM)
    quarter = (sum(lengths) // 4, width)
    own, *pieces = call(cut_kernel, (quarter, F32), *[(quarter, BF16)] * 3)(kernel_sums, *lateral_part)
    three, two, one = [exchange(piece, 0, k) for piece, k in zip(pieces, (3, 2, 1))]
    [total] = call(add_kernel, (quarter, BF16))(own, three, two, one)
    three, two, one = [exchange(total, 1, k) for k in (3, 2, 1)]
    finish = call(functools.partial(finish_kernel, scale), (quarter, BF16), in_specs=[vmem] * 4 + [far])
    [total] = finish(total, three, two, one, after)
    three, two, one = [exchange(total, 0, k) for k in (3, 2, 1)]
    quarters = [total, three, two, one]
    results = [((length, 2 * width), BF16) for length in lengths]
    others = [swap(one) for one in quarters]
    place = dict(out_specs=[far] * 2, scratch_shapes=[pltpu.SemaphoreType.DMA((10,))])
    plan = (False, 0), (False, 3), (False, 2), (False, 1), (True, 0)
    most = call(functools.partial(place_kernel, plan), *results, **place)(*quarters, others[0])
    plan = (True, 3), (True, 2), (True, 1)
    place.update(in_specs=[vmem] * 3 + [far] * 2, input_output_aliases={3: 0, 4: 1})
    return call(functools.partial(place_kernel, plan), *results, **place)(*others[1:], *most)


def local(features, top_down, lateral_weight, out_kernel, cotangent):
    images, rows, cols, in_channels = features.shape
    channels = lateral_weight.shape[1]
    cells = rows * cols
    peers = lax.axis_size("space")
    taps = out_kernel.reshape(9, channels, channels)
    params = pltpu.CompilerParams(vmem_limit_bytes=32 * 2**20)
    halves = peers == 2 and lax.axis_size("dp") == 16 and images == 1 and (channels, in_channels) == (256, 512)

    def sums(length):
        if not halves:
            return [jax.ShapeDtypeStruct((length, channels), F32)]
        return [jax.ShapeDtypeStruct((length, channels // 2), kind) for kind in (F32, BF16)]

    outs, tops, parts = [], [], None
    for image in range(images):
        cot = cotangent[image]
        cot_before, cot_after = neighbour_rows(cot)
        arrays = (cot, lateral_weight, top_down[image], features[image].reshape(cells, in_channels), taps)
        arrays = [pltpu.with_memory_space_constraint(array, pltpu.HBM) for array in arrays]
        merged, stack, near_feat, near_taps = pl.pallas_call(
            merge_kernel,
            out_shape=[
                jax.ShapeDtypeStruct(shape, BF16)
                for shape in (
                    (cells, channels),
                    (rows, cols, 3 * channels),
                    (cells, in_channels),
                    taps.shape,
                )
            ],
            in_specs=[pl.BlockSpec(memory_space=pltpu.HBM)] * 5,
            scratch_shapes=[*[pltpu.VMEM(array.shape, BF16) for array in arrays[:3]], pltpu.SemaphoreType.DMA((5,))],
            compiler_params=params,
            cost_estimate=pl.CostEstimate(
                flops=2 * cells * channels * 4 * in_channels, bytes_accessed=4 * 2**20, transcendentals=0
            ),
        )(*arrays)
        merged = merged.reshape(rows, cols, channels)
        edges = neighbour_rows(merged)
        grad, halo, *lateral_part = pl.pallas_call(
            functools.partial(data_grad_kernel, peers),
            out_shape=[
                jax.ShapeDtypeStruct((cells, channels), BF16),
                jax.ShapeDtypeStruct((2, cols, 3 * channels), BF16),
                *sums(in_channels),
            ],
            compiler_params=params,
            cost_estimate=pl.CostEstimate(
                flops=2 * cells * channels * (9 * channels + in_channels), bytes_accessed=4 * 2**20, transcendentals=0
            ),
        )(stack, cot_before, cot_after, near_feat, near_taps)
        kernel_cost = pl.CostEstimate(
            flops=2 * cells * channels * 9 * channels, bytes_accessed=4 * 2**20, transcendentals=0
        )
        if halves:
            lateral_part[1] = swap(lateral_part[1])
            kernel_sums = pl.pallas_call(
                pair_kernel_grad_kernel,
                out_shape=jax.ShapeDtypeStruct((9 * channels, channels // 2), F32),
                scratch_shapes=[pltpu.VMEM((2 * rows + 2, cols, 3 * channels // 2), BF16)],
                compiler_params=params,
                cost_estimate=kernel_cost,
            )(stack, merged.reshape(cells, channels), cot_after, edges[0].reshape(cells, channels))
        else:
            kernel_sums = pl.pallas_call(
                kernel_grad_kernel,
                out_shape=jax.ShapeDtypeStruct((9 * channels, channels), F32),
                compiler_params=params,
                cost_estimate=kernel_cost,
            )(stack, halo, merged.reshape(cells, channels))
        out, grad_top = pl.pallas_call(
            functools.partial(forward_kernel, peers),
            out_shape=[
                jax.ShapeDtypeStruct((rows, cols, channels), BF16),
                jax.ShapeDtypeStruct((rows // 2, cols // 2, channels), BF16),
            ],
            out_specs=[pl.BlockSpec(memory_space=pltpu.HBM), pl.BlockSpec(memory_space=pltpu.VMEM)],
            scratch_shapes=[
                pltpu.VMEM((rows + 2, cols, 3 * channels), BF16),
                pltpu.VMEM((rows, cols, channels), BF16),
                pltpu.SemaphoreType.DMA,
            ],
            compiler_params=params,
            cost_estimate=pl.CostEstimate(
                flops=2 * cells * channels * 9 * channels, bytes_accessed=2 * 2**20, transcendentals=0
            ),
        )(merged, near_taps, grad, *edges)
        outs.append(out)
        tops.append(grad_top)
        if not halves:
            part = [kernel_sums, lateral_part[0]]
            parts = part if parts is None else [a + b for a, b in zip(parts, part)]
    scale = 1.0 / (images * lax.axis_size("dp"))
    if halves:
        grad_kernel, grad_lateral = sum_everywhere(kernel_sums, lateral_part, scale, outs[0])
    else:
        grad_kernel, grad_lateral = [(total * scale).astype(BF16) for total in lax.psum(parts, ("dp", "space"))]
    return jnp.stack(outs), jnp.stack(tops), grad_kernel.reshape(out_kernel.shape), grad_lateral


def solution(mesh):
    return jax.shard_map(
        local,
        mesh=mesh,
        in_specs=(
            P("dp", "space", None, None),
            P("dp", "space", None, None),
            P(),
            P(),
            P("dp", "space", None, None),
        ),
        out_specs=(P("dp", "space", None, None), P("dp", "space", None, None), P(), P()),
        check_vma=False,
    )
```

```python
import functools

import jax
import jax.numpy as jnp
from jax import lax
from jax.experimental import pallas as pl
from jax.experimental.pallas import tpu as pltpu
from jax.sharding import PartitionSpec as P

F32 = jnp.float32
BF16 = jnp.bfloat16


def neighbour_rows(array):
    peers = lax.axis_size("space")
    if peers == 1:
        return array[-1:], array[:1]
    if peers == 2:
        got = lax.ppermute(array, "space", [(0, 1), (1, 0)])
        return got, got
    up = [(i, i + 1) for i in range(peers - 1)]
    down = [(j, i) for i, j in up]
    return lax.ppermute(array[-1:], "space", up), lax.ppermute(array[:1], "space", down)


def put_shifted(stack, slot, row, sign):
    cols, channels = row.shape
    wide = row.astype(F32)
    place = lax.broadcasted_iota(jnp.int32, (cols, channels), 0)
    later = jnp.where(place == cols - 1, 0.0, pltpu.roll(wide, cols - 1, 0)).astype(BF16)
    earlier = jnp.where(place == 0, 0.0, pltpu.roll(wide, 1, 0)).astype(BF16)
    first, last = (earlier, later) if sign < 0 else (later, earlier)
    stack[slot, :, 0:channels] = first
    stack[slot, :, channels : 2 * channels] = row
    stack[slot, :, 2 * channels :] = last


def put_halo(stack, before, after, rows, peers, sign):
    here = lax.axis_index("space")
    zero = jnp.zeros(before.shape, BF16)
    put_shifted(stack, 0, jnp.where(here > 0, before, zero), sign)
    put_shifted(stack, rows + 1, jnp.where(here < peers - 1, after, zero), sign)


def merge_kernel(*refs):
    far, (merged, stack, feat, out_w), near, sems = refs[:5], refs[5:9], refs[9:12], refs[12]
    near = (*near, feat, out_w)
    copies = [pltpu.make_async_copy(a, b, sems.at[i]) for i, (a, b) in enumerate(zip(far, near))]
    for copy in copies:
        copy.start()
    cot, lat_w, top = near[:3]
    rows, cols, channels = cot.shape
    half = cols // 2
    upper = lax.broadcasted_iota(jnp.int32, (cols, half), 0)
    spread = jnp.where(upper // 2 == lax.broadcasted_iota(jnp.int32, (cols, half), 1), 1.0, 0.0).astype(BF16)
    copies[0].wait()
    for r in range(rows):
        put_shifted(stack, r, cot[r], 1)
    for copy in copies[1:4]:
        copy.wait()
    lateral = jnp.dot(feat[...], lat_w[...], preferred_element_type=F32)
    for q in range(rows // 2):
        lifted = jnp.dot(spread, top[q], preferred_element_type=F32)
        for r in (2 * q, 2 * q + 1):
            merged[r * cols : (r + 1) * cols, :] = (lateral[r * cols : (r + 1) * cols] + lifted).astype(BF16)
    copies[4].wait()


def over_cells(left, right):
    return lax.dot_general(left, right, (((0,), (0,)), ((), ())), preferred_element_type=F32)


def strips_of(stack, halo):
    rows, cols, deep = stack.shape
    strips = [
        jnp.concatenate([stack[1:], halo[1:]], axis=0),
        stack[...],
        jnp.concatenate([halo[:1], stack[: rows - 1]], axis=0),
    ]
    return [strip.reshape(rows * cols, deep) for strip in strips]


def put_sums(outs, start, values):
    rows = slice(start, start + values.shape[0])
    if len(outs) == 1:
        outs[0][rows, :] = values
        return
    here = lax.axis_index("space")
    half = values.shape[1] // 2
    mine, theirs = outs
    mine[rows, :] = jnp.where(here == 0, values[:, :half], values[:, half:])
    theirs[rows, :] = jnp.where(here == 0, values[:, half:], values[:, :half]).astype(BF16)


def kernel_grad_kernel(stack, halo, merged, out):
    channels = merged.shape[1]
    for i, strip in enumerate(strips_of(stack, halo)):
        part = over_cells(merged[...], strip)
        for j in range(3):
            start = (3 * i + j) * channels
            out[start : start + channels, :] = part[:, j * channels : (j + 1) * channels]


def pair_kernel_grad_kernel(stack, merged, cot, other_merged, out, image):
    here = lax.axis_index("space")
    rows, cols, channels = cot.shape
    half = channels // 2
    zero = jnp.zeros((1, cols, 3 * half), BF16)
    image[0:1] = zero
    image[2 * rows + 1 :] = zero
    own, other = 1 + rows * here, 1 + rows * (1 - here)
    for r in range(rows):
        row = cot[r]
        put_shifted(image, other + r, jnp.where(here == 0, row[:, :half], row[:, half:]), 1)
        for j in range(3):
            start = j * channels
            left, right = stack[r, :, start : start + half], stack[r, :, start + half : start + channels]
            image[own + r, :, j * half : (j + 1) * half] = jnp.where(here == 0, left, right)
    cells = []
    for first in (own, other):
        strips = [image[pl.ds(first + 1 - i, rows)].reshape(rows * cols, 3 * half) for i in range(3)]
        cells.append(jnp.concatenate(strips, axis=1))
    left = jnp.concatenate([merged[...], other_merged[...]], axis=0)
    part = over_cells(left, jnp.concatenate(cells, axis=0))
    for tap in range(9):
        out[tap * channels : (tap + 1) * channels, :] = part[:, tap * half : (tap + 1) * half]


def data_grad_kernel(peers, stack, before, after, feat, out_w, grad, halo, *outs):
    put_halo(halo, before[before.shape[0] - 1], after[0], 0, peers, 1)
    cells = jnp.concatenate(strips_of(stack, halo), axis=1)
    taps = jnp.concatenate([out_w[tap] for tap in range(9)], axis=1)
    total = lax.dot_general(cells, taps, (((1,), (1,)), ((), ())), preferred_element_type=F32)
    grad[...] = total.astype(BF16)
    put_sums(outs, 0, over_cells(feat[...], grad[...]))


def forward_kernel(peers, merged, out_w, grad, *refs):
    edges, (out, grad_top, stack, near, sem) = refs[:-5], refs[-5:]
    rows, cols, channels = merged.shape
    half = cols // 2
    for r in range(rows):
        put_shifted(stack, r + 1, merged[r], -1)
    put_halo(stack, edges[0][edges[0].shape[0] - 1], edges[1][0], rows, peers, -1)
    cells = jnp.concatenate([stack[i : i + rows].reshape(rows * cols, 3 * channels) for i in range(3)], axis=1)
    total = jnp.dot(cells, out_w[...].reshape(9 * channels, channels), preferred_element_type=F32)
    near[...] = total.astype(BF16).reshape(out.shape)
    copy = pltpu.make_async_copy(near, out, sem)
    copy.start()
    lower = lax.broadcasted_iota(jnp.int32, (half, 2 * cols), 1)
    lower = jnp.where(lower >= cols, lower - cols, lower)
    pool = jnp.where(lower // 2 == lax.broadcasted_iota(jnp.int32, (half, 2 * cols), 0), 1.0, 0.0).astype(BF16)
    for q in range(rows // 2):
        pair = grad[2 * q * cols : (2 * q + 2) * cols, :]
        grad_top[q] = jnp.dot(pool, pair, preferred_element_type=F32).astype(BF16)
    copy.wait()


def places():
    chip, core = lax.axis_index("dp"), lax.axis_index("space")
    plane, line = chip % 4, chip // 4
    return jnp.where(core == 0, plane, line), jnp.where(core == 0, line, plane)


def block(index, length):
    return pl.ds(pl.multiple_of(index * length, 16), length)


def cut_kernel(kernel_sums, mine, got, *refs):
    place, _ = places()
    edge, share = kernel_sums.shape[0] // 4, mine.shape[0] // 4
    for k, out in zip((0, 3, 2, 1), refs):
        out[:edge, :] = kernel_sums[block(place ^ k, edge), :].astype(out.dtype)
        rows = block(place ^ k, share)
        out[edge:, :] = (mine[rows, :] + got[rows, :].astype(F32)).astype(out.dtype)


def add_kernel(own, three, two, one, out):
    total = own[...] + one[...].astype(F32) + two[...].astype(F32) + three[...].astype(F32)
    out[...] = total.astype(BF16)


def finish_kernel(scale, own, one, two, three, _, out):
    near = own[...].astype(F32) + one[...].astype(F32)
    far = two[...].astype(F32) + three[...].astype(F32)
    out[...] = ((near + far) * scale).astype(BF16)


def place_kernel(plan, *refs):
    results, sems = refs[-3:-1], refs[-1]
    side, (own, other) = lax.axis_index("space"), places()
    copies = []
    for quarter, (pair, k) in zip(refs, plan):
        columns, place = (1 - side, other) if pair else (side, own)
        lanes = pl.ds(pl.multiple_of(columns * 128, 128), 128)
        start = 0
        for result in results:
            share = result.shape[0] // 4
            to = result.at[block(place ^ k, share), lanes]
            copies.append(pltpu.make_async_copy(quarter.at[pl.ds(start, share), :], to, sems.at[len(copies)]))
            start += share
    for copy in copies:
        copy.start()
    for copy in copies:
        copy.wait()


def exchange(array, step, k):
    pairs = []
    for chip in range(16):
        for core in range(2):
            flip = k if core == step else 4 * k
            pairs.append((2 * chip + core, 2 * (chip ^ flip) + core))
    return lax.ppermute(array, ("dp", "space"), pairs)


def swap(array):
    return lax.ppermute(array, "space", [(0, 1), (1, 0)])


def call(kernel, *shapes, **more):
    return pl.pallas_call(
        kernel,
        out_shape=[jax.ShapeDtypeStruct(shape, kind) for shape, kind in shapes],
        compiler_params=pltpu.CompilerParams(vmem_limit_bytes=12 * 2**20),
        **more,
    )


def sum_everywhere(kernel_sums, lateral_part, scale, after):
    lengths, width = [kernel_sums.shape[0], lateral_part[0].shape[0]], kernel_sums.shape[1]
    vmem, far = pl.BlockSpec(memory_space=pltpu.VMEM), pl.BlockSpec(memory_space=pltpu.HBM)
    after = pltpu.with_memory_space_constraint(after, pltpu.HBM)
    quarter = (sum(lengths) // 4, width)
    own, *pieces = call(cut_kernel, (quarter, F32), *[(quarter, BF16)] * 3)(kernel_sums, *lateral_part)
    three, two, one = [exchange(piece, 0, k) for piece, k in zip(pieces, (3, 2, 1))]
    [total] = call(add_kernel, (quarter, BF16))(own, three, two, one)
    three, two, one = [exchange(total, 1, k) for k in (3, 2, 1)]
    finish = call(functools.partial(finish_kernel, scale), (quarter, BF16), in_specs=[vmem] * 4 + [far])
    [total] = finish(total, one, two, three, after)
    three, two, one = [exchange(total, 0, k) for k in (3, 2, 1)]
    quarters = [total, one, two, three]
    results = [((length, 2 * width), BF16) for length in lengths]
    others = [swap(one) for one in quarters]
    place = dict(out_specs=[far] * 2, scratch_shapes=[pltpu.SemaphoreType.DMA((10,))])
    plan = (False, 0), (False, 1), (False, 2), (False, 3), (True, 0)
    most = call(functools.partial(place_kernel, plan), *results, **place)(*quarters, others[0])
    plan = (True, 1), (True, 2), (True, 3)
    place.update(in_specs=[vmem] * 3 + [far] * 2, input_output_aliases={3: 0, 4: 1})
    return call(functools.partial(place_kernel, plan), *results, **place)(*others[1:], *most)


def local(features, top_down, lateral_weight, out_kernel, cotangent):
    images, rows, cols, in_channels = features.shape
    channels = lateral_weight.shape[1]
    cells = rows * cols
    peers = lax.axis_size("space")
    taps = out_kernel.reshape(9, channels, channels)
    params = pltpu.CompilerParams(vmem_limit_bytes=32 * 2**20)
    halves = peers == 2 and lax.axis_size("dp") == 16 and images == 1 and (channels, in_channels) == (256, 512)

    def sums(length):
        if not halves:
            return [jax.ShapeDtypeStruct((length, channels), F32)]
        return [jax.ShapeDtypeStruct((length, channels // 2), kind) for kind in (F32, BF16)]

    outs, tops, parts = [], [], None
    for image in range(images):
        cot = cotangent[image]
        cot_before, cot_after = neighbour_rows(cot)
        arrays = (cot, lateral_weight, top_down[image], features[image].reshape(cells, in_channels), taps)
        arrays = [pltpu.with_memory_space_constraint(array, pltpu.HBM) for array in arrays]
        merged, stack, near_feat, near_taps = pl.pallas_call(
            merge_kernel,
            out_shape=[
                jax.ShapeDtypeStruct(shape, BF16)
                for shape in (
                    (cells, channels),
                    (rows, cols, 3 * channels),
                    (cells, in_channels),
                    taps.shape,
                )
            ],
            in_specs=[pl.BlockSpec(memory_space=pltpu.HBM)] * 5,
            scratch_shapes=[*[pltpu.VMEM(array.shape, BF16) for array in arrays[:3]], pltpu.SemaphoreType.DMA((5,))],
            compiler_params=params,
            cost_estimate=pl.CostEstimate(
                flops=2 * cells * channels * 4 * in_channels, bytes_accessed=4 * 2**20, transcendentals=0
            ),
        )(*arrays)
        merged = merged.reshape(rows, cols, channels)
        edges = neighbour_rows(merged)
        grad, halo, *lateral_part = pl.pallas_call(
            functools.partial(data_grad_kernel, peers),
            out_shape=[
                jax.ShapeDtypeStruct((cells, channels), BF16),
                jax.ShapeDtypeStruct((2, cols, 3 * channels), BF16),
                *sums(in_channels),
            ],
            compiler_params=params,
            cost_estimate=pl.CostEstimate(
                flops=2 * cells * channels * (9 * channels + in_channels), bytes_accessed=4 * 2**20, transcendentals=0
            ),
        )(stack, cot_before, cot_after, near_feat, near_taps)
        kernel_cost = pl.CostEstimate(
            flops=2 * cells * channels * 9 * channels, bytes_accessed=4 * 2**20, transcendentals=0
        )
        if halves:
            lateral_part[1] = swap(lateral_part[1])
            kernel_sums = pl.pallas_call(
                pair_kernel_grad_kernel,
                out_shape=jax.ShapeDtypeStruct((9 * channels, channels // 2), F32),
                scratch_shapes=[pltpu.VMEM((2 * rows + 2, cols, 3 * channels // 2), BF16)],
                compiler_params=params,
                cost_estimate=kernel_cost,
            )(stack, merged.reshape(cells, channels), cot_after, edges[0].reshape(cells, channels))
        else:
            kernel_sums = pl.pallas_call(
                kernel_grad_kernel,
                out_shape=jax.ShapeDtypeStruct((9 * channels, channels), F32),
                compiler_params=params,
                cost_estimate=kernel_cost,
            )(stack, halo, merged.reshape(cells, channels))
        out, grad_top = pl.pallas_call(
            functools.partial(forward_kernel, peers),
            out_shape=[
                jax.ShapeDtypeStruct((rows, cols, channels), BF16),
                jax.ShapeDtypeStruct((rows // 2, cols // 2, channels), BF16),
            ],
            out_specs=[pl.BlockSpec(memory_space=pltpu.HBM), pl.BlockSpec(memory_space=pltpu.VMEM)],
            scratch_shapes=[
                pltpu.VMEM((rows + 2, cols, 3 * channels), BF16),
                pltpu.VMEM((rows, cols, channels), BF16),
                pltpu.SemaphoreType.DMA,
            ],
            compiler_params=params,
            cost_estimate=pl.CostEstimate(
                flops=2 * cells * channels * 9 * channels, bytes_accessed=2 * 2**20, transcendentals=0
            ),
        )(merged, near_taps, grad, *edges)
        outs.append(out)
        tops.append(grad_top)
        if not halves:
            part = [kernel_sums, lateral_part[0]]
            parts = part if parts is None else [a + b for a, b in zip(parts, part)]
    scale = 1.0 / (images * lax.axis_size("dp"))
    if halves:
        grad_kernel, grad_lateral = sum_everywhere(kernel_sums, lateral_part, scale, outs[0])
    else:
        grad_kernel, grad_lateral = [(total * scale).astype(BF16) for total in lax.psum(parts, ("dp", "space"))]
    return jnp.stack(outs), jnp.stack(tops), grad_kernel.reshape(out_kernel.shape), grad_lateral


def solution(mesh):
    return jax.shard_map(
        local,
        mesh=mesh,
        in_specs=(
            P("dp", "space", None, None),
            P("dp", "space", None, None),
            P(),
            P(),
            P("dp", "space", None, None),
        ),
        out_specs=(P("dp", "space", None, None), P("dp", "space", None, None), P(), P()),
        check_vma=False,
    )
```

```python
import functools

import jax
import jax.numpy as jnp
from jax import lax
from jax.experimental import pallas as pl
from jax.experimental.pallas import tpu as pltpu
from jax.sharding import PartitionSpec as P

F32 = jnp.float32
BF16 = jnp.bfloat16


def neighbour_rows(array):
    peers = lax.axis_size("space")
    if peers == 1:
        return array[-1:], array[:1]
    if peers == 2:
        got = lax.ppermute(array, "space", [(0, 1), (1, 0)])
        return got, got
    up = [(i, i + 1) for i in range(peers - 1)]
    down = [(j, i) for i, j in up]
    return lax.ppermute(array[-1:], "space", up), lax.ppermute(array[:1], "space", down)


def put_shifted(stack, slot, row, sign):
    cols, channels = row.shape
    wide = row.astype(F32)
    place = lax.broadcasted_iota(jnp.int32, (cols, channels), 0)
    later = jnp.where(place == cols - 1, 0.0, pltpu.roll(wide, cols - 1, 0)).astype(BF16)
    earlier = jnp.where(place == 0, 0.0, pltpu.roll(wide, 1, 0)).astype(BF16)
    first, last = (earlier, later) if sign < 0 else (later, earlier)
    stack[slot, :, 0:channels] = first
    stack[slot, :, channels : 2 * channels] = row
    stack[slot, :, 2 * channels :] = last


def put_halo(stack, before, after, rows, peers, sign):
    here = lax.axis_index("space")
    zero = jnp.zeros(before.shape, BF16)
    put_shifted(stack, 0, jnp.where(here > 0, before, zero), sign)
    put_shifted(stack, rows + 1, jnp.where(here < peers - 1, after, zero), sign)


def merge_kernel(*refs):
    far, (merged, stack, feat, out_w), near, sems = refs[:5], refs[5:9], refs[9:12], refs[12]
    near = (*near, feat, out_w)
    copies = [pltpu.make_async_copy(a, b, sems.at[i]) for i, (a, b) in enumerate(zip(far, near))]
    for copy in copies:
        copy.start()
    cot, lat_w, top = near[:3]
    rows, cols, channels = cot.shape
    half = cols // 2
    upper = lax.broadcasted_iota(jnp.int32, (cols, half), 0)
    spread = jnp.where(upper // 2 == lax.broadcasted_iota(jnp.int32, (cols, half), 1), 1.0, 0.0).astype(BF16)
    copies[0].wait()
    for r in range(rows):
        put_shifted(stack, r, cot[r], 1)
    for copy in copies[1:4]:
        copy.wait()
    lateral = jnp.dot(feat[...], lat_w[...], preferred_element_type=F32)
    for q in range(rows // 2):
        lifted = jnp.dot(spread, top[q], preferred_element_type=F32)
        for r in (2 * q, 2 * q + 1):
            merged[r * cols : (r + 1) * cols, :] = (lateral[r * cols : (r + 1) * cols] + lifted).astype(BF16)
    copies[4].wait()


def over_cells(left, right):
    return lax.dot_general(left, right, (((0,), (0,)), ((), ())), preferred_element_type=F32)


def strips_of(stack, halo):
    rows, cols, deep = stack.shape
    strips = [
        jnp.concatenate([stack[1:], halo[1:]], axis=0),
        stack[...],
        jnp.concatenate([halo[:1], stack[: rows - 1]], axis=0),
    ]
    return [strip.reshape(rows * cols, deep) for strip in strips]


def put_sums(outs, start, values):
    rows = slice(start, start + values.shape[0])
    if len(outs) == 1:
        outs[0][rows, :] = values
        return
    here = lax.axis_index("space")
    half = values.shape[1] // 2
    mine, theirs = outs
    mine[rows, :] = jnp.where(here == 0, values[:, :half], values[:, half:])
    theirs[rows, :] = jnp.where(here == 0, values[:, half:], values[:, :half]).astype(BF16)


def kernel_grad_kernel(stack, halo, merged, out):
    channels = merged.shape[1]
    for i, strip in enumerate(strips_of(stack, halo)):
        part = over_cells(merged[...], strip)
        for j in range(3):
            start = (3 * i + j) * channels
            out[start : start + channels, :] = part[:, j * channels : (j + 1) * channels]


def pair_kernel_grad_kernel(stack, merged, cot, other_merged, out, image):
    here = lax.axis_index("space")
    rows, cols, channels = cot.shape
    half = channels // 2
    zero = jnp.zeros((1, cols, 3 * half), BF16)
    image[0:1] = zero
    image[2 * rows + 1 :] = zero
    own, other = 1 + rows * here, 1 + rows * (1 - here)
    for r in range(rows):
        row = cot[r]
        put_shifted(image, other + r, jnp.where(here == 0, row[:, :half], row[:, half:]), 1)
        for j in range(3):
            start = j * channels
            left, right = stack[r, :, start : start + half], stack[r, :, start + half : start + channels]
            image[own + r, :, j * half : (j + 1) * half] = jnp.where(here == 0, left, right)
    cells = []
    for first in (own, other):
        strips = [image[pl.ds(first + 1 - i, rows)].reshape(rows * cols, 3 * half) for i in range(3)]
        cells.append(jnp.concatenate(strips, axis=1))
    left = jnp.concatenate([merged[...], other_merged[...]], axis=0)
    part = over_cells(left, jnp.concatenate(cells, axis=0))
    for tap in range(9):
        out[tap * channels : (tap + 1) * channels, :] = part[:, tap * half : (tap + 1) * half]


def data_grad_kernel(peers, stack, before, after, feat, out_w, grad, halo, *outs):
    put_halo(halo, before[before.shape[0] - 1], after[0], 0, peers, 1)
    cells = jnp.concatenate(strips_of(stack, halo), axis=1)
    taps = jnp.concatenate([out_w[tap] for tap in range(9)], axis=1)
    total = lax.dot_general(cells, taps, (((1,), (1,)), ((), ())), preferred_element_type=F32)
    grad[...] = total.astype(BF16)
    put_sums(outs, 0, over_cells(feat[...], grad[...]))


def forward_kernel(peers, merged, out_w, grad, *refs):
    edges, (out, grad_top, stack, near, sem) = refs[:-5], refs[-5:]
    rows, cols, channels = merged.shape
    half = cols // 2
    for r in range(rows):
        put_shifted(stack, r + 1, merged[r], -1)
    put_halo(stack, edges[0][edges[0].shape[0] - 1], edges[1][0], rows, peers, -1)
    cells = jnp.concatenate([stack[i : i + rows].reshape(rows * cols, 3 * channels) for i in range(3)], axis=1)
    total = jnp.dot(cells, out_w[...].reshape(9 * channels, channels), preferred_element_type=F32)
    near[...] = total.astype(BF16).reshape(out.shape)
    copy = pltpu.make_async_copy(near, out, sem)
    copy.start()
    lower = lax.broadcasted_iota(jnp.int32, (half, 2 * cols), 1)
    lower = jnp.where(lower >= cols, lower - cols, lower)
    pool = jnp.where(lower // 2 == lax.broadcasted_iota(jnp.int32, (half, 2 * cols), 0), 1.0, 0.0).astype(BF16)
    for q in range(rows // 2):
        pair = grad[2 * q * cols : (2 * q + 2) * cols, :]
        grad_top[q] = jnp.dot(pool, pair, preferred_element_type=F32).astype(BF16)
    copy.wait()


def places():
    chip, core = lax.axis_index("dp"), lax.axis_index("space")
    plane, line = chip % 4, chip // 4
    return jnp.where(core == 0, plane, line), jnp.where(core == 0, line, plane)


def block(index, length):
    return pl.ds(pl.multiple_of(index * length, 16), length)


def cut_kernel(kernel_sums, mine, got, *refs):
    place, _ = places()
    edge, share = kernel_sums.shape[0] // 4, mine.shape[0] // 4
    for k, out in zip((0, 3, 2, 1), refs):
        out[:edge, :] = kernel_sums[block(place ^ k, edge), :].astype(out.dtype)
        rows = block(place ^ k, share)
        out[edge:, :] = (mine[rows, :] + got[rows, :].astype(F32)).astype(out.dtype)


def add_kernel(own, three, two, one, out):
    total = own[...] + one[...].astype(F32) + two[...].astype(F32) + three[...].astype(F32)
    out[...] = total.astype(BF16)


def finish_kernel(scale, own, one, two, three, _, out):
    near = own[...].astype(F32) + one[...].astype(F32)
    far = two[...].astype(F32) + three[...].astype(F32)
    out[...] = ((near + far) * scale).astype(BF16)


def place_kernel(plan, *refs):
    results, sems = refs[-3:-1], refs[-1]
    side, (own, other) = lax.axis_index("space"), places()
    copies = []
    for quarter, (pair, k) in zip(refs, plan):
        columns, place = (1 - side, other) if pair else (side, own)
        lanes = pl.ds(pl.multiple_of(columns * 128, 128), 128)
        start = 0
        for result in results:
            share = result.shape[0] // 4
            to = result.at[block(place ^ k, share), lanes]
            copies.append(pltpu.make_async_copy(quarter.at[pl.ds(start, share), :], to, sems.at[len(copies)]))
            start += share
    for copy in copies:
        copy.start()
    for copy in copies:
        copy.wait()


def exchange(array, step, k):
    pairs = []
    for chip in range(16):
        for core in range(2):
            flip = k if core == step else 4 * k
            pairs.append((2 * chip + core, 2 * (chip ^ flip) + core))
    return lax.ppermute(array, ("dp", "space"), pairs)


def swap(array):
    return lax.ppermute(array, "space", [(0, 1), (1, 0)])


def call(kernel, *shapes, **more):
    return pl.pallas_call(
        kernel,
        out_shape=[jax.ShapeDtypeStruct(shape, kind) for shape, kind in shapes],
        compiler_params=pltpu.CompilerParams(vmem_limit_bytes=12 * 2**20),
        **more,
    )


def sum_everywhere(kernel_sums, lateral_part, scale, after):
    lengths, width = [kernel_sums.shape[0], lateral_part[0].shape[0]], kernel_sums.shape[1]
    vmem, far = pl.BlockSpec(memory_space=pltpu.VMEM), pl.BlockSpec(memory_space=pltpu.HBM)
    after = pltpu.with_memory_space_constraint(after, pltpu.HBM)
    quarter = (sum(lengths) // 4, width)
    own, *pieces = call(cut_kernel, (quarter, F32), *[(quarter, BF16)] * 3)(kernel_sums, *lateral_part)
    three, two, one = [exchange(piece, 0, k) for piece, k in zip(pieces, (3, 2, 1))]
    [total] = call(add_kernel, (quarter, BF16))(own, three, two, one)
    three, two, one = [exchange(total, 1, k) for k in (3, 2, 1)]
    finish = call(functools.partial(finish_kernel, scale), (quarter, BF16), in_specs=[vmem] * 4 + [far])
    [total] = finish(total, one, two, three, after)
    three, two, one = [exchange(total, 0, k) for k in (3, 2, 1)]
    quarters = [total, three, two, one]
    results = [((length, 2 * width), BF16) for length in lengths]
    others = [swap(one) for one in quarters]
    place = dict(out_specs=[far] * 2, scratch_shapes=[pltpu.SemaphoreType.DMA((10,))])
    plan = (False, 0), (False, 3), (False, 2), (False, 1), (True, 0)
    most = call(functools.partial(place_kernel, plan), *results, **place)(*quarters, others[0])
    plan = (True, 3), (True, 2), (True, 1)
    place.update(in_specs=[vmem] * 3 + [far] * 2, input_output_aliases={3: 0, 4: 1})
    return call(functools.partial(place_kernel, plan), *results, **place)(*others[1:], *most)


def local(features, top_down, lateral_weight, out_kernel, cotangent):
    images, rows, cols, in_channels = features.shape
    channels = lateral_weight.shape[1]
    cells = rows * cols
    peers = lax.axis_size("space")
    taps = out_kernel.reshape(9, channels, channels)
    params = pltpu.CompilerParams(vmem_limit_bytes=32 * 2**20)
    halves = peers == 2 and lax.axis_size("dp") == 16 and images == 1 and (channels, in_channels) == (256, 512)

    def sums(length):
        if not halves:
            return [jax.ShapeDtypeStruct((length, channels), F32)]
        return [jax.ShapeDtypeStruct((length, channels // 2), kind) for kind in (F32, BF16)]

    outs, tops, parts = [], [], None
    for image in range(images):
        cot = cotangent[image]
        cot_before, cot_after = neighbour_rows(cot)
        arrays = (cot, lateral_weight, top_down[image], features[image].reshape(cells, in_channels), taps)
        arrays = [pltpu.with_memory_space_constraint(array, pltpu.HBM) for array in arrays]
        merged, stack, near_feat, near_taps = pl.pallas_call(
            merge_kernel,
            out_shape=[
                jax.ShapeDtypeStruct(shape, BF16)
                for shape in (
                    (cells, channels),
                    (rows, cols, 3 * channels),
                    (cells, in_channels),
                    taps.shape,
                )
            ],
            in_specs=[pl.BlockSpec(memory_space=pltpu.HBM)] * 5,
            scratch_shapes=[*[pltpu.VMEM(array.shape, BF16) for array in arrays[:3]], pltpu.SemaphoreType.DMA((5,))],
            compiler_params=params,
            cost_estimate=pl.CostEstimate(
                flops=2 * cells * channels * 4 * in_channels, bytes_accessed=4 * 2**20, transcendentals=0
            ),
        )(*arrays)
        merged = merged.reshape(rows, cols, channels)
        edges = neighbour_rows(merged)
        grad, halo, *lateral_part = pl.pallas_call(
            functools.partial(data_grad_kernel, peers),
            out_shape=[
                jax.ShapeDtypeStruct((cells, channels), BF16),
                jax.ShapeDtypeStruct((2, cols, 3 * channels), BF16),
                *sums(in_channels),
            ],
            compiler_params=params,
            cost_estimate=pl.CostEstimate(
                flops=2 * cells * channels * (9 * channels + in_channels), bytes_accessed=4 * 2**20, transcendentals=0
            ),
        )(stack, cot_before, cot_after, near_feat, near_taps)
        kernel_cost = pl.CostEstimate(
            flops=2 * cells * channels * 9 * channels, bytes_accessed=4 * 2**20, transcendentals=0
        )
        if halves:
            lateral_part[1] = swap(lateral_part[1])
            kernel_sums = pl.pallas_call(
                pair_kernel_grad_kernel,
                out_shape=jax.ShapeDtypeStruct((9 * channels, channels // 2), F32),
                scratch_shapes=[pltpu.VMEM((2 * rows + 2, cols, 3 * channels // 2), BF16)],
                compiler_params=params,
                cost_estimate=kernel_cost,
            )(stack, merged.reshape(cells, channels), cot_after, edges[0].reshape(cells, channels))
        else:
            kernel_sums = pl.pallas_call(
                kernel_grad_kernel,
                out_shape=jax.ShapeDtypeStruct((9 * channels, channels), F32),
                compiler_params=params,
                cost_estimate=kernel_cost,
            )(stack, halo, merged.reshape(cells, channels))
        out, grad_top = pl.pallas_call(
            functools.partial(forward_kernel, peers),
            out_shape=[
                jax.ShapeDtypeStruct((rows, cols, channels), BF16),
                jax.ShapeDtypeStruct((rows // 2, cols // 2, channels), BF16),
            ],
            out_specs=[pl.BlockSpec(memory_space=pltpu.HBM), pl.BlockSpec(memory_space=pltpu.VMEM)],
            scratch_shapes=[
                pltpu.VMEM((rows + 2, cols, 3 * channels), BF16),
                pltpu.VMEM((rows, cols, channels), BF16),
                pltpu.SemaphoreType.DMA,
            ],
            compiler_params=params,
            cost_estimate=pl.CostEstimate(
                flops=2 * cells * channels * 9 * channels, bytes_accessed=2 * 2**20, transcendentals=0
            ),
        )(merged, near_taps, grad, *edges)
        outs.append(out)
        tops.append(grad_top)
        if not halves:
            part = [kernel_sums, lateral_part[0]]
            parts = part if parts is None else [a + b for a, b in zip(parts, part)]
    scale = 1.0 / (images * lax.axis_size("dp"))
    if halves:
        grad_kernel, grad_lateral = sum_everywhere(kernel_sums, lateral_part, scale, outs[0])
    else:
        grad_kernel, grad_lateral = [(total * scale).astype(BF16) for total in lax.psum(parts, ("dp", "space"))]
    return jnp.stack(outs), jnp.stack(tops), grad_kernel.reshape(out_kernel.shape), grad_lateral


def solution(mesh):
    return jax.shard_map(
        local,
        mesh=mesh,
        in_specs=(
            P("dp", "space", None, None),
            P("dp", "space", None, None),
            P(),
            P(),
            P("dp", "space", None, None),
        ),
        out_specs=(P("dp", "space", None, None), P("dp", "space", None, None), P(), P()),
        check_vma=False,
    )
```

```python
import functools

import jax
import jax.numpy as jnp
from jax import lax
from jax.experimental import pallas as pl
from jax.experimental.pallas import tpu as pltpu
from jax.sharding import PartitionSpec as P

F32 = jnp.float32
BF16 = jnp.bfloat16


def neighbour_rows(array):
    peers = lax.axis_size("space")
    if peers == 1:
        return array[-1:], array[:1]
    if peers == 2:
        got = lax.ppermute(array, "space", [(0, 1), (1, 0)])
        return got, got
    up = [(i, i + 1) for i in range(peers - 1)]
    down = [(j, i) for i, j in up]
    return lax.ppermute(array[-1:], "space", up), lax.ppermute(array[:1], "space", down)


def put_shifted(stack, slot, row, sign):
    cols, channels = row.shape
    wide = row.astype(F32)
    place = lax.broadcasted_iota(jnp.int32, (cols, channels), 0)
    later = jnp.where(place == cols - 1, 0.0, pltpu.roll(wide, cols - 1, 0)).astype(BF16)
    earlier = jnp.where(place == 0, 0.0, pltpu.roll(wide, 1, 0)).astype(BF16)
    first, last = (earlier, later) if sign < 0 else (later, earlier)
    stack[slot, :, 0:channels] = first
    stack[slot, :, channels : 2 * channels] = row
    stack[slot, :, 2 * channels :] = last


def put_halo(stack, before, after, rows, peers, sign):
    here = lax.axis_index("space")
    zero = jnp.zeros(before.shape, BF16)
    put_shifted(stack, 0, jnp.where(here > 0, before, zero), sign)
    put_shifted(stack, rows + 1, jnp.where(here < peers - 1, after, zero), sign)


def merge_kernel(*refs):
    far, (merged, stack, feat, out_w), near, sems = refs[:5], refs[5:9], refs[9:12], refs[12]
    near = (*near, feat, out_w)
    copies = [pltpu.make_async_copy(a, b, sems.at[i]) for i, (a, b) in enumerate(zip(far, near))]
    for copy in copies:
        copy.start()
    cot, lat_w, top = near[:3]
    rows, cols, channels = cot.shape
    half = cols // 2
    upper = lax.broadcasted_iota(jnp.int32, (cols, half), 0)
    spread = jnp.where(upper // 2 == lax.broadcasted_iota(jnp.int32, (cols, half), 1), 1.0, 0.0).astype(BF16)
    copies[0].wait()
    for r in range(rows):
        put_shifted(stack, r, cot[r], 1)
    for copy in copies[1:4]:
        copy.wait()
    lateral = jnp.dot(feat[...], lat_w[...], preferred_element_type=F32)
    for q in range(rows // 2):
        lifted = jnp.dot(spread, top[q], preferred_element_type=F32)
        for r in (2 * q, 2 * q + 1):
            merged[r * cols : (r + 1) * cols, :] = (lateral[r * cols : (r + 1) * cols] + lifted).astype(BF16)
    copies[4].wait()


def over_cells(left, right):
    return lax.dot_general(left, right, (((0,), (0,)), ((), ())), preferred_element_type=F32)


def strips_of(stack, halo):
    rows, cols, deep = stack.shape
    strips = [
        jnp.concatenate([stack[1:], halo[1:]], axis=0),
        stack[...],
        jnp.concatenate([halo[:1], stack[: rows - 1]], axis=0),
    ]
    return [strip.reshape(rows * cols, deep) for strip in strips]


def put_sums(outs, start, values):
    rows = slice(start, start + values.shape[0])
    if len(outs) == 1:
        outs[0][rows, :] = values
        return
    here = lax.axis_index("space")
    half = values.shape[1] // 2
    mine, theirs = outs
    mine[rows, :] = jnp.where(here == 0, values[:, :half], values[:, half:])
    theirs[rows, :] = jnp.where(here == 0, values[:, half:], values[:, :half]).astype(BF16)


def kernel_grad_kernel(stack, halo, merged, out):
    channels = merged.shape[1]
    for i, strip in enumerate(strips_of(stack, halo)):
        part = over_cells(merged[...], strip)
        for j in range(3):
            start = (3 * i + j) * channels
            out[start : start + channels, :] = part[:, j * channels : (j + 1) * channels]


def pair_kernel_grad_kernel(stack, merged, cot, other_merged, out, image):
    here = lax.axis_index("space")
    rows, cols, channels = cot.shape
    half = channels // 2
    zero = jnp.zeros((1, cols, 3 * half), BF16)
    image[0:1] = zero
    image[2 * rows + 1 :] = zero
    own, other = 1 + rows * here, 1 + rows * (1 - here)
    for r in range(rows):
        row = cot[r]
        put_shifted(image, other + r, jnp.where(here == 0, row[:, :half], row[:, half:]), 1)
        for j in range(3):
            start = j * channels
            left, right = stack[r, :, start : start + half], stack[r, :, start + half : start + channels]
            image[own + r, :, j * half : (j + 1) * half] = jnp.where(here == 0, left, right)
    cells = []
    for first in (own, other):
        strips = [image[pl.ds(first + 1 - i, rows)].reshape(rows * cols, 3 * half) for i in range(3)]
        cells.append(jnp.concatenate(strips, axis=1))
    left = jnp.concatenate([merged[...], other_merged[...]], axis=0)
    part = over_cells(left, jnp.concatenate(cells, axis=0))
    for tap in range(9):
        out[tap * channels : (tap + 1) * channels, :] = part[:, tap * half : (tap + 1) * half]


def data_grad_kernel(peers, stack, before, after, feat, out_w, grad, halo, *outs):
    put_halo(halo, before[before.shape[0] - 1], after[0], 0, peers, 1)
    cells = jnp.concatenate(strips_of(stack, halo), axis=1)
    taps = jnp.concatenate([out_w[tap] for tap in range(9)], axis=1)
    total = lax.dot_general(cells, taps, (((1,), (1,)), ((), ())), preferred_element_type=F32)
    grad[...] = total.astype(BF16)
    put_sums(outs, 0, over_cells(feat[...], grad[...]))


def forward_kernel(peers, merged, out_w, grad, *refs):
    edges, (out, grad_top, stack, near, sem) = refs[:-5], refs[-5:]
    rows, cols, channels = merged.shape
    half = cols // 2
    for r in range(rows):
        put_shifted(stack, r + 1, merged[r], -1)
    put_halo(stack, edges[0][edges[0].shape[0] - 1], edges[1][0], rows, peers, -1)
    cells = jnp.concatenate([stack[i : i + rows].reshape(rows * cols, 3 * channels) for i in range(3)], axis=1)
    total = jnp.dot(cells, out_w[...].reshape(9 * channels, channels), preferred_element_type=F32)
    near[...] = total.astype(BF16).reshape(out.shape)
    copy = pltpu.make_async_copy(near, out, sem)
    copy.start()
    lower = lax.broadcasted_iota(jnp.int32, (half, 2 * cols), 1)
    lower = jnp.where(lower >= cols, lower - cols, lower)
    pool = jnp.where(lower // 2 == lax.broadcasted_iota(jnp.int32, (half, 2 * cols), 0), 1.0, 0.0).astype(BF16)
    for q in range(rows // 2):
        pair = grad[2 * q * cols : (2 * q + 2) * cols, :]
        grad_top[q] = jnp.dot(pool, pair, preferred_element_type=F32).astype(BF16)
    copy.wait()


def places():
    chip, core = lax.axis_index("dp"), lax.axis_index("space")
    plane, line = chip % 4, chip // 4
    return jnp.where(core == 0, plane, line), jnp.where(core == 0, line, plane)


def block(index, length):
    return pl.ds(pl.multiple_of(index * length, 16), length)


def cut_kernel(kernel_sums, mine, got, *refs):
    place, _ = places()
    edge, share = kernel_sums.shape[0] // 4, mine.shape[0] // 4
    for k, out in zip((0, 3, 2, 1), refs):
        out[:edge, :] = kernel_sums[block(place ^ k, edge), :].astype(out.dtype)
        rows = block(place ^ k, share)
        out[edge:, :] = (mine[rows, :] + got[rows, :].astype(F32)).astype(out.dtype)


def add_kernel(own, three, two, one, out):
    total = own[...] + one[...].astype(F32) + two[...].astype(F32) + three[...].astype(F32)
    out[...] = total.astype(BF16)


def finish_kernel(scale, own, three, two, one, _, out):
    near = own[...].astype(F32) + one[...].astype(F32)
    far = two[...].astype(F32) + three[...].astype(F32)
    out[...] = ((near + far) * scale).astype(BF16)


def place_kernel(plan, *refs):
    results, sems = refs[-3:-1], refs[-1]
    side, (own, other) = lax.axis_index("space"), places()
    copies = []
    for quarter, (pair, k) in zip(refs, plan):
        columns, place = (1 - side, other) if pair else (side, own)
        lanes = pl.ds(pl.multiple_of(columns * 128, 128), 128)
        start = 0
        for result in results:
            share = result.shape[0] // 4
            to = result.at[block(place ^ k, share), lanes]
            copies.append(pltpu.make_async_copy(quarter.at[pl.ds(start, share), :], to, sems.at[len(copies)]))
            start += share
    for copy in copies:
        copy.start()
    for copy in copies:
        copy.wait()


def exchange(array, step, k):
    pairs = []
    for chip in range(16):
        for core in range(2):
            flip = k if core == step else 4 * k
            pairs.append((2 * chip + core, 2 * (chip ^ flip) + core))
    return lax.ppermute(array, ("dp", "space"), pairs)


def swap(array):
    return lax.ppermute(array, "space", [(0, 1), (1, 0)])


def call(kernel, *shapes, **more):
    return pl.pallas_call(
        kernel,
        out_shape=[jax.ShapeDtypeStruct(shape, kind) for shape, kind in shapes],
        compiler_params=pltpu.CompilerParams(vmem_limit_bytes=12 * 2**20),
        **more,
    )


def sum_everywhere(kernel_sums, lateral_part, scale, after):
    lengths, width = [kernel_sums.shape[0], lateral_part[0].shape[0]], kernel_sums.shape[1]
    vmem, far = pl.BlockSpec(memory_space=pltpu.VMEM), pl.BlockSpec(memory_space=pltpu.HBM)
    after = pltpu.with_memory_space_constraint(after, pltpu.HBM)
    quarter = (sum(lengths) // 4, width)
    own, *pieces = call(cut_kernel, (quarter, F32), *[(quarter, BF16)] * 3)(kernel_sums, *lateral_part)
    three, two, one = [exchange(piece, 0, k) for piece, k in zip(pieces, (3, 2, 1))]
    [total] = call(add_kernel, (quarter, BF16))(own, three, two, one)
    three, two, one = [exchange(total, 1, k) for k in (3, 2, 1)]
    finish = call(functools.partial(finish_kernel, scale), (quarter, BF16), in_specs=[vmem] * 4 + [far])
    [total] = finish(total, three, two, one, after)
    three, two, one = [exchange(total, 0, k) for k in (3, 2, 1)]
    quarters = [total, one, two, three]
    results = [((length, 2 * width), BF16) for length in lengths]
    others = [swap(one) for one in quarters]
    place = dict(out_specs=[far] * 2, scratch_shapes=[pltpu.SemaphoreType.DMA((10,))])
    plan = (False, 0), (False, 1), (False, 2), (False, 3), (True, 0)
    most = call(functools.partial(place_kernel, plan), *results, **place)(*quarters, others[0])
    plan = (True, 1), (True, 2), (True, 3)
    place.update(in_specs=[vmem] * 3 + [far] * 2, input_output_aliases={3: 0, 4: 1})
    return call(functools.partial(place_kernel, plan), *results, **place)(*others[1:], *most)


def local(features, top_down, lateral_weight, out_kernel, cotangent):
    images, rows, cols, in_channels = features.shape
    channels = lateral_weight.shape[1]
    cells = rows * cols
    peers = lax.axis_size("space")
    taps = out_kernel.reshape(9, channels, channels)
    params = pltpu.CompilerParams(vmem_limit_bytes=32 * 2**20)
    halves = peers == 2 and lax.axis_size("dp") == 16 and images == 1 and (channels, in_channels) == (256, 512)

    def sums(length):
        if not halves:
            return [jax.ShapeDtypeStruct((length, channels), F32)]
        return [jax.ShapeDtypeStruct((length, channels // 2), kind) for kind in (F32, BF16)]

    outs, tops, parts = [], [], None
    for image in range(images):
        cot = cotangent[image]
        cot_before, cot_after = neighbour_rows(cot)
        arrays = (cot, lateral_weight, top_down[image], features[image].reshape(cells, in_channels), taps)
        arrays = [pltpu.with_memory_space_constraint(array, pltpu.HBM) for array in arrays]
        merged, stack, near_feat, near_taps = pl.pallas_call(
            merge_kernel,
            out_shape=[
                jax.ShapeDtypeStruct(shape, BF16)
                for shape in (
                    (cells, channels),
                    (rows, cols, 3 * channels),
                    (cells, in_channels),
                    taps.shape,
                )
            ],
            in_specs=[pl.BlockSpec(memory_space=pltpu.HBM)] * 5,
            scratch_shapes=[*[pltpu.VMEM(array.shape, BF16) for array in arrays[:3]], pltpu.SemaphoreType.DMA((5,))],
            compiler_params=params,
            cost_estimate=pl.CostEstimate(
                flops=2 * cells * channels * 4 * in_channels, bytes_accessed=4 * 2**20, transcendentals=0
            ),
        )(*arrays)
        merged = merged.reshape(rows, cols, channels)
        edges = neighbour_rows(merged)
        grad, halo, *lateral_part = pl.pallas_call(
            functools.partial(data_grad_kernel, peers),
            out_shape=[
                jax.ShapeDtypeStruct((cells, channels), BF16),
                jax.ShapeDtypeStruct((2, cols, 3 * channels), BF16),
                *sums(in_channels),
            ],
            compiler_params=params,
            cost_estimate=pl.CostEstimate(
                flops=2 * cells * channels * (9 * channels + in_channels), bytes_accessed=4 * 2**20, transcendentals=0
            ),
        )(stack, cot_before, cot_after, near_feat, near_taps)
        kernel_cost = pl.CostEstimate(
            flops=2 * cells * channels * 9 * channels, bytes_accessed=4 * 2**20, transcendentals=0
        )
        if halves:
            lateral_part[1] = swap(lateral_part[1])
            kernel_sums = pl.pallas_call(
                pair_kernel_grad_kernel,
                out_shape=jax.ShapeDtypeStruct((9 * channels, channels // 2), F32),
                scratch_shapes=[pltpu.VMEM((2 * rows + 2, cols, 3 * channels // 2), BF16)],
                compiler_params=params,
                cost_estimate=kernel_cost,
            )(stack, merged.reshape(cells, channels), cot_after, edges[0].reshape(cells, channels))
        else:
            kernel_sums = pl.pallas_call(
                kernel_grad_kernel,
                out_shape=jax.ShapeDtypeStruct((9 * channels, channels), F32),
                compiler_params=params,
                cost_estimate=kernel_cost,
            )(stack, halo, merged.reshape(cells, channels))
        out, grad_top = pl.pallas_call(
            functools.partial(forward_kernel, peers),
            out_shape=[
                jax.ShapeDtypeStruct((rows, cols, channels), BF16),
                jax.ShapeDtypeStruct((rows // 2, cols // 2, channels), BF16),
            ],
            out_specs=[pl.BlockSpec(memory_space=pltpu.HBM), pl.BlockSpec(memory_space=pltpu.VMEM)],
            scratch_shapes=[
                pltpu.VMEM((rows + 2, cols, 3 * channels), BF16),
                pltpu.VMEM((rows, cols, channels), BF16),
                pltpu.SemaphoreType.DMA,
            ],
            compiler_params=params,
            cost_estimate=pl.CostEstimate(
                flops=2 * cells * channels * 9 * channels, bytes_accessed=2 * 2**20, transcendentals=0
            ),
        )(merged, near_taps, grad, *edges)
        outs.append(out)
        tops.append(grad_top)
        if not halves:
            part = [kernel_sums, lateral_part[0]]
            parts = part if parts is None else [a + b for a, b in zip(parts, part)]
    scale = 1.0 / (images * lax.axis_size("dp"))
    if halves:
        grad_kernel, grad_lateral = sum_everywhere(kernel_sums, lateral_part, scale, outs[0])
    else:
        grad_kernel, grad_lateral = [(total * scale).astype(BF16) for total in lax.psum(parts, ("dp", "space"))]
    return jnp.stack(outs), jnp.stack(tops), grad_kernel.reshape(out_kernel.shape), grad_lateral


def solution(mesh):
    return jax.shard_map(
        local,
        mesh=mesh,
        in_specs=(
            P("dp", "space", None, None),
            P("dp", "space", None, None),
            P(),
            P(),
            P("dp", "space", None, None),
        ),
        out_specs=(P("dp", "space", None, None), P("dp", "space", None, None), P(), P()),
        check_vma=False,
    )
```
